32 devices in a mesh: parts: 2 (over y), row: 8 (over z, x), col: 2 (over core).
Axes of the slice: x: 2, y: 2, z: 4, core: 2. Of those that a mesh axis runs over, the one named last changes fastest.
Arguments:
- queries: bfloat16 [16384, 256], P(('parts', 'row', 'col')), parts along dimension 0, may hold values from -6 to 6
- counts: int32 [32], P(('parts', 'row', 'col')), parts along dimension 0, may hold values from 1 to 512, as said below
- memory: bfloat16 [512, 256], P(('parts', 'row', 'col')), parts along dimension 0, may hold values from -6 to 6
- mem_mask: int32 [512], P(('parts', 'row', 'col')), parts along dimension 0, may hold values from 0 to 1, as said below
- cross_wq: bfloat16 [256, 256], replicated, may hold values from -0.375 to 0.375
- cross_wkv: bfloat16 [256, 512], replicated, may hold values from -0.375 to 0.375
- cross_wo: bfloat16 [256, 256], replicated, may hold values from -0.375 to 0.375
- self_wqkv: bfloat16 [256, 768], replicated, may hold values from -0.375 to 0.375
- self_wo: bfloat16 [256, 256], replicated, may hold values from -0.375 to 0.375
- ffn_up: bfloat16 [256, 2048], replicated, may hold values from -0.375 to 0.375
- ffn_down: bfloat16 [2048, 256], replicated, may hold values from -0.125 to 0.125
- box_w1: bfloat16 [256, 256], replicated, may hold values from -0.375 to 0.375
- box_w2: bfloat16 [256, 256], replicated, may hold values from -0.375 to 0.375
- box_w3: bfloat16 [256, 4], replicated, may hold values from -0.375 to 0.375
- cross_temp: float32 [8], replicated, may hold values from 1 to 100
- self_temp: float32 [8], replicated, may hold values from 1 to 100
Outputs:
- features: float32 [16384, 256], P(('parts', 'row', 'col')), parts along dimension 0
- boxes: float32 [4, 16384], P(None, ('parts', 'row', 'col')), parts along dimension 1
The draws below stay inside these ranges and needn't reach their ends.
There are 2 independent parts, one for each index of `parts`. The reference program is written for one: setup_inputs(seed, part) draws one part's arguments, and reference() takes and returns one part's arrays. A program takes and returns all parts, laid end to end along the dimension named above; an argument that names none is the same for every part. Nothing has to cross between parts.
Inputs may be any that keep to these rules, and one draw needn't show every extreme that they name: The first counts[t] slots of tile t are live; some tile is full. `mem_mask`: the first memory token of every tile is live.
All inputs are finite; a program needn't handle non-finite values.
Results may differ from the reference program's by a relative error of at most 0.038.
The reference program's roundings to bfloat16 on the way (of `qc`, `kvm`, `ctx`, `qkv`, `sctx`, `upper` and `b2`) count: a program that leaves them out, or rounds other values in their place, can miss the bound.
Values may be sent and summed in bfloat16 or wider, within the bound.
No kernel may reach another device: no remote copies, remote signals or barrier semaphores. Data moves between devices by JAX's collectives and lax.ppermute only.
A program may use at most 64 MiB of HBM per device.

```python
import math
import jax
import jax.numpy as jnp
from jax import lax

D = 256
HEADS = 8
FF = 2048
Q_DEV = 512
M_DEV = 16
TILES = 16
NQ = 8192
MEM = 256
N_ROW = 8
N_COL = 2


def draw_counts(key, part):
    first = jax.random.fold_in(key, 11)
    second = jax.random.fold_in(key, 12)
    values = jax.random.randint(first, (TILES,), 1, Q_DEV + 1)
    full_tile = jax.random.randint(second, (), 0, TILES)
    return jnp.where(jnp.arange(TILES) == full_tile, Q_DEV, values).astype(jnp.int32)


def draw_mem_mask(key, part):
    bits = jax.random.randint(jax.random.fold_in(key, 21), (MEM,), 0, 4)
    first = jnp.arange(MEM) % M_DEV == 0
    return jnp.where((bits > 0) | first, 1, 0).astype(jnp.int32)


def temper(key, salt):
    spread = jax.random.uniform(jax.random.fold_in(key, salt), (HEADS,), jnp.float32)
    high = jnp.full((HEADS,), math.log(6.0), jnp.float32)
    return jnp.exp(spread * high).astype(jnp.float32)


def draw_cross_temp(key, part):
    return temper(key, 31)


def draw_self_temp(key, part):
    return temper(key, 41)


def level_of(own_key, shape, cuts, low, top_value):
    def one(position, parts):
        heights = jax.random.uniform(jax.random.fold_in(jax.random.fold_in(own_key, 6), position), (parts,), jnp.float32, low / len(cuts), top_value / len(cuts))
        return jnp.repeat(jnp.exp(heights), shape[position] // parts).reshape((-1,) + (1,) * (len(shape) - position - 1))

    gain = one(*cuts[0])
    for cut in cuts[1:]:
        gain = gain * one(*cut)
    return gain


def bell_draw(own_key, dims, scale, limit, pieces=(), held_as=jnp.bfloat16):
    array = jax.random.normal(own_key, dims, jnp.float32) * scale
    if len(pieces) > 0:
        array = level_of(own_key, dims, pieces, -0.22, 0.18) * array
    return jnp.clip(array, min=-limit, max=limit).astype(held_as)


def setup_inputs(seed: int = 0, part: int = 0) -> dict:
    splits = jax.random.split(jax.random.key(seed), 17)
    part_splits = jax.random.split(jax.random.fold_in(splits[16], part), 17)
    queries = bell_draw(part_splits[0], (NQ, D), 1.0, 6.0, ((0, 16),))
    counts = draw_counts(jax.random.fold_in(jax.random.fold_in(splits[16], part), 71), part)
    memory = bell_draw(part_splits[2], (MEM, D), 1.0, 6.0, ((0, 16),))
    mem_mask = draw_mem_mask(jax.random.fold_in(jax.random.fold_in(splits[16], part), 71), part)
    cross_wq = bell_draw(splits[4], (D, D), D ** -0.5, 0.375)
    cross_wkv = bell_draw(splits[5], (D, 2 * D), D ** -0.5, 0.375)
    cross_wo = bell_draw(splits[6], (D, D), D ** -0.5, 0.375)
    self_wqkv = bell_draw(splits[7], (D, 3 * D), D ** -0.5, 0.375)
    self_wo = bell_draw(splits[8], (D, D), D ** -0.5, 0.375)
    ffn_up = bell_draw(splits[9], (D, FF), D ** -0.5, 0.375)
    ffn_down = bell_draw(splits[10], (FF, D), FF ** -0.5, 0.125)
    box_w1 = bell_draw(splits[11], (D, D), D ** -0.5, 0.375)
    box_w2 = bell_draw(splits[12], (D, D), D ** -0.5, 0.375)
    box_w3 = bell_draw(splits[13], (D, 4), D ** -0.5, 0.375)
    cross_temp = draw_cross_temp(jax.random.fold_in(splits[16], 71), part)
    self_temp = draw_self_temp(jax.random.fold_in(splits[16], 71), part)
    return dict(queries=queries, counts=counts, memory=memory, mem_mask=mem_mask, cross_wq=cross_wq, cross_wkv=cross_wkv, cross_wo=cross_wo, self_wqkv=self_wqkv, self_wo=self_wo, ffn_up=ffn_up, ffn_down=ffn_down, box_w1=box_w1, box_w2=box_w2, box_w3=box_w3, cross_temp=cross_temp, self_temp=self_temp)


EPS = 1e-06

def rms_norm(x):
    return x * lax.rsqrt(lax.optimization_barrier(jnp.mean(x * x, axis=-1, keepdims=True)) + EPS)

def attend(query, keyval, live, scale):
    rows = query.shape[0]
    width = query.shape[1]
    heads = scale.shape[0]
    hsize = width // heads
    q3 = query.astype(jnp.float32).reshape(rows, heads, hsize)
    keys = keyval[:, :width].astype(jnp.float32).reshape(-1, heads, hsize)
    values = keyval[:, width:].astype(jnp.float32).reshape(-1, heads, hsize)
    scores = jnp.einsum('qhd,khd->hqk', q3, keys, precision=lax.Precision.HIGHEST) * scale[:, None, None]
    keep = (live > 0)[None, None, :]
    top = lax.optimization_barrier(jnp.max(jnp.where(keep, scores, -1e+30), axis=-1, keepdims=True))
    weights = jnp.where(keep, jnp.exp(scores - top), 0.0)
    total = lax.optimization_barrier(jnp.sum(weights, axis=-1))
    rounded = lax.optimization_barrier(weights.astype(jnp.bfloat16)).astype(jnp.float32)
    mixed = jnp.einsum('hqk,khd->qhd', rounded, values, precision=lax.Precision.HIGHEST)
    mixed = mixed / jnp.transpose(total)[:, :, None]
    return mixed.reshape(rows, width)

def reference(queries, counts, memory, mem_mask, cross_wq, cross_wkv, cross_wo, self_wqkv, self_wo, ffn_up, ffn_down, box_w1, box_w2, box_w3, cross_temp, self_temp):
    hsize = D // HEADS
    slots = jnp.arange(Q_DEV, dtype=jnp.int32)
    valid = (slots[None, :] < counts[:, None]).reshape(NQ)
    xres = queries.astype(jnp.float32)
    hn0 = rms_norm(xres).astype(jnp.bfloat16)
    qc = jnp.dot(hn0, cross_wq, preferred_element_type=jnp.float32).astype(jnp.bfloat16)
    kvm = jnp.dot(memory, cross_wkv, preferred_element_type=jnp.float32).astype(jnp.bfloat16)
    scale_c = cross_temp / jnp.sqrt(jnp.float32(hsize))
    q_tiles = qc.reshape(N_ROW, N_COL, Q_DEV, D)
    kv_tiles = kvm.reshape(N_ROW, N_COL, M_DEV, 2 * D)
    m_tiles = mem_mask.reshape(N_ROW, N_COL, M_DEV)
    columns = []
    for column in range(N_COL):
        strip = kv_tiles[:, column].reshape(N_ROW * M_DEV, 2 * D)
        strip_live = m_tiles[:, column].reshape(N_ROW * M_DEV)
        columns.append(lax.map(lambda q: attend(q, strip, strip_live, scale_c), q_tiles[:, column]))
    ctx = jnp.stack(columns, axis=1).reshape(NQ, D)
    ctx = jnp.where(valid[:, None], ctx, 0.0).astype(jnp.bfloat16)
    x1 = xres + jnp.dot(ctx, cross_wo, preferred_element_type=jnp.float32)
    hn1 = rms_norm(x1).astype(jnp.bfloat16)
    qkv = jnp.dot(hn1, self_wqkv, preferred_element_type=jnp.float32).astype(jnp.bfloat16)
    scale_s = self_temp / jnp.sqrt(jnp.float32(hsize))
    row_qkv = qkv.reshape(N_ROW, N_COL * Q_DEV, 3 * D)
    row_live = valid.astype(jnp.int32).reshape(N_ROW, N_COL * Q_DEV)

    def self_row(pair):
        block, live = pair
        return attend(block[:, :D], block[:, D:], live, scale_s)
    sctx = lax.map(self_row, (row_qkv, row_live)).reshape(NQ, D)
    sctx = jnp.where(valid[:, None], sctx, 0.0).astype(jnp.bfloat16)
    x2 = x1 + jnp.dot(sctx, self_wo, preferred_element_type=jnp.float32)
    hn2 = rms_norm(x2).astype(jnp.bfloat16)
    upper = jnp.maximum(jnp.dot(hn2, ffn_up, preferred_element_type=jnp.float32), 0.0).astype(jnp.bfloat16)
    x3 = x2 + jnp.dot(upper, ffn_down, preferred_element_type=jnp.float32)
    features = jnp.where(valid[:, None], x3, 0.0).astype(jnp.float32)
    hn3 = rms_norm(x3).astype(jnp.bfloat16)
    b1 = jnp.maximum(jnp.dot(hn3, box_w1, preferred_element_type=jnp.float32), 0.0).astype(jnp.bfloat16)
    b2 = jnp.maximum(jnp.dot(b1, box_w2, preferred_element_type=jnp.float32), 0.0).astype(jnp.bfloat16)
    raw_box = jax.nn.sigmoid(jnp.dot(b2, box_w3, preferred_element_type=jnp.float32))
    boxes = jnp.transpose(jnp.where(valid[:, None], raw_box, 0.0))
    return (features, boxes)
```

```python
import jax
import jax.numpy as jnp
from jax import lax
from jax.sharding import PartitionSpec as P

EPS = 1e-06
DEAD = jnp.bfloat16(64.0)


def rms_round(x):
    return (x * lax.rsqrt(jnp.mean(x * x, axis=-1, keepdims=True) + EPS)).astype(jnp.bfloat16)


def blend(state, q_block, keyval, live, scale):
    top_old, total_old, acc_old = state
    rows, heads, hsize = q_block.shape
    width = heads * hsize
    keys = keyval[:, :width].reshape(-1, heads, hsize)
    values = keyval[:, width:].reshape(-1, heads, hsize)
    scores = (
        jnp.einsum("qhd,khd->hqk", q_block, keys, preferred_element_type=jnp.float32)
        * scale[:, None, None]
    )
    keep = (live > 0)[None, None, :]
    top_new = jnp.maximum(top_old, jnp.max(jnp.where(keep, scores, -1e30), axis=-1))
    weights = jnp.where(keep, jnp.exp(scores - top_new[:, :, None]), 0.0)
    fade = jnp.exp(top_old - top_new)
    total_new = total_old * fade + jnp.sum(weights, axis=-1)
    mixed = jnp.einsum(
        "hqk,khd->qhd", weights.astype(jnp.bfloat16), values, preferred_element_type=jnp.float32
    )
    acc_new = acc_old * jnp.repeat(jnp.transpose(fade), hsize, axis=1) + mixed.reshape(rows, width)
    return (top_new, total_new, acc_new)


def sweep(state, q_all, keyval, live, scale, blocks, block):
    heads = scale.shape[0]
    hsize = q_all.shape[1] // heads

    def visit(index, carry):
        top, total, acc = carry
        begin = index * block
        q_block = lax.dynamic_slice_in_dim(q_all, begin, block, 0).reshape(block, heads, hsize)
        sub = (
            lax.dynamic_slice_in_dim(top, begin, block, 1),
            lax.dynamic_slice_in_dim(total, begin, block, 1),
            lax.dynamic_slice_in_dim(acc, begin, block, 0),
        )
        top_b, total_b, acc_b = blend(sub, q_block, keyval, live, scale)
        return (
            lax.dynamic_update_slice_in_dim(top, top_b, begin, 1),
            lax.dynamic_update_slice_in_dim(total, total_b, begin, 1),
            lax.dynamic_update_slice_in_dim(acc, acc_b, begin, 0),
        )

    return lax.fori_loop(0, blocks, visit, state)


def start_state(heads, rows, width):
    return (
        jnp.full((heads, rows), -1e30, jnp.float32),
        jnp.zeros((heads, rows), jnp.float32),
        jnp.zeros((rows, width), jnp.float32),
    )


def finish(state, valid, hsize):
    top, total, acc = state
    mixed = acc / jnp.repeat(jnp.transpose(total), hsize, axis=1)
    return jnp.where(valid[:, None], mixed, 0.0).astype(jnp.bfloat16)


def gather_xor(x, axis):
    size = lax.axis_size(axis)
    step = 1
    while step < size:
        group = min(8, size // step)
        parts = [x]
        for k in range(1, group):
            pairs = [(i, i ^ (k * step)) for i in range(size)]
            parts.append(lax.ppermute(x, axis, pairs))
        x = jnp.concatenate(parts, axis=0)
        step *= group
    return x


def swap(x, axis):
    size = lax.axis_size(axis)
    return lax.ppermute(x, axis, [(i, i ^ 1) for i in range(size)])


def local(
    queries,
    counts,
    memory,
    mem_mask,
    cross_wq,
    cross_wkv,
    cross_wo,
    self_wqkv,
    self_wo,
    ffn_up,
    ffn_down,
    box_w1,
    box_w2,
    box_w3,
    cross_temp,
    self_temp,
):
    rows = queries.shape[0]
    width = queries.shape[1]
    heads = cross_temp.shape[0]
    hsize = width // heads
    block = min(128, rows)
    blocks = rows // block
    valid = jnp.arange(rows, dtype=jnp.int32) < counts[0]
    xres = queries.astype(jnp.float32)
    hn0 = rms_round(xres)
    qc = jnp.dot(hn0, cross_wq, preferred_element_type=jnp.float32).astype(jnp.bfloat16)
    scale_c = cross_temp / jnp.sqrt(jnp.float32(hsize))
    tokens = gather_xor(jnp.where((mem_mask > 0)[:, None], memory, DEAD), "row")
    partner_count = swap(counts, "col")
    initial = start_state(heads, rows, width)
    kvm = jnp.dot(tokens, cross_wkv, preferred_element_type=jnp.float32).astype(jnp.bfloat16)
    piece = (kvm, (tokens[:, 0] < DEAD).astype(jnp.float32))
    state = sweep(initial, qc, piece[0], piece[1], scale_c, blocks, block)
    ctx = finish(state, valid, hsize)
    x1 = xres + jnp.dot(ctx, cross_wo, preferred_element_type=jnp.float32)
    hn1 = rms_round(x1)
    qkv = jnp.dot(hn1, self_wqkv, preferred_element_type=jnp.float32).astype(jnp.bfloat16)
    q_self = qkv[:, :width]
    kv_self = qkv[:, width:]
    scale_s = self_temp / jnp.sqrt(jnp.float32(hsize))
    slots = jnp.arange(rows, dtype=jnp.int32)
    piece = (
        jnp.concatenate([kv_self, swap(kv_self, "col")], axis=0),
        jnp.concatenate([slots < counts[0], slots < partner_count[0]]).astype(jnp.float32),
    )
    state_self = sweep(
        start_state(heads, rows, width), q_self, piece[0], piece[1], scale_s, blocks, block
    )
    sctx = finish(state_self, valid, hsize)
    x2 = x1 + jnp.dot(sctx, self_wo, preferred_element_type=jnp.float32)
    hn2 = rms_round(x2)
    upper = jnp.maximum(jnp.dot(hn2, ffn_up, preferred_element_type=jnp.float32), 0.0).astype(
        jnp.bfloat16
    )
    x3 = x2 + jnp.dot(upper, ffn_down, preferred_element_type=jnp.float32)
    features = jnp.where(valid[:, None], x3, 0.0)
    hn3 = rms_round(x3)
    b1 = jnp.maximum(jnp.dot(hn3, box_w1, preferred_element_type=jnp.float32), 0.0).astype(
        jnp.bfloat16
    )
    b2 = jnp.maximum(jnp.dot(b1, box_w2, preferred_element_type=jnp.float32), 0.0).astype(
        jnp.bfloat16
    )
    raw_box = jax.nn.sigmoid(jnp.dot(b2, box_w3, preferred_element_type=jnp.float32))
    boxes = jnp.transpose(jnp.where(valid[:, None], raw_box, 0.0))
    return (features, boxes)


def solution(mesh):
    return jax.shard_map(
        local,
        mesh=mesh,
        in_specs=(
            P(("parts", "row", "col"), None),
            P(("parts", "row", "col")),
            P(("parts", "row", "col"), None),
            P(("parts", "row", "col")),
            P(),
            P(),
            P(),
            P(),
            P(),
            P(),
            P(),
            P(),
            P(),
            P(),
            P(),
            P(),
        ),
        out_specs=(P(("parts", "row", "col"), None), P(None, ("parts", "row", "col"))),
        check_vma=False,
    )
```

```python
import functools
import math

import jax
import jax.numpy as jnp
from jax import lax
from jax.experimental import pallas as pl
from jax.experimental.pallas import tpu as pltpu
from jax.sharding import PartitionSpec as P

EPS = 1e-06
DEAD = 64.0
DEAD_V = 4096.0
LOG2E = math.log2(math.e)
VMEM = pl.BlockSpec(memory_space=pltpu.VMEM)
SMEM = pl.BlockSpec(memory_space=pltpu.SMEM)


def rms_round(x):
    return (x * lax.rsqrt(jnp.mean(x * x, axis=-1, keepdims=True) + EPS)).astype(jnp.bfloat16)


def dot(a, b):
    return jnp.dot(a, b, preferred_element_type=jnp.float32)


def dot_t(a, b):
    return lax.dot_general(a, b, (((1,), (1,)), ((), ())), preferred_element_type=jnp.float32)


def head_of_lane(rows, width, heads):
    return lax.broadcasted_iota(jnp.int32, (rows, width), 1) // (width // heads)


def only(x, head, lane_head):
    return jnp.where(lane_head == head, x, jnp.zeros_like(x))


def flagged(values, flags, head, heads, lane_head):
    other = (head + heads // 2) % heads
    rest = jnp.where(lane_head == other, flags, jnp.zeros_like(values))
    return jnp.where(lane_head == head, values, rest)


def weigh(scores, top, scale):
    return jnp.exp2(((scores - top) * scale).astype(jnp.bfloat16))


def normed(low, high):
    half = low.shape[1] // 2
    return jnp.concatenate(
        [low[:, :half] / low[:, half:], high[:, half:] / high[:, :half]], axis=1
    ).astype(jnp.bfloat16)


def cross_kernel(n, block, tile, temp, counts, queries, *refs):
    pieces = refs[:n]
    wq, wkv, wo, wqkv, x1_ref, q_ref, kv_ref, kbd, vbd = refs[n:]
    heads = temp.shape[0]
    rows, width = queries.shape
    hsize = width // heads
    tokens, flags = [], []
    for piece in pieces:
        held = piece[...].astype(jnp.float32)
        dead = held >= DEAD
        for begin in range(0, held.shape[0], tile):
            part = held[begin : begin + tile]
            gone = dead[begin : begin + tile]
            tokens.append(jnp.where(gone, part[:1], part).astype(jnp.bfloat16))
            flags.append(jnp.where(gone, 0.0, 1.0).astype(jnp.bfloat16))
    tokens = jnp.concatenate(tokens, axis=0)
    flags = jnp.concatenate(flags, axis=0)
    count = tokens.shape[0]
    kvm = dot(tokens, wkv[...]).astype(jnp.bfloat16)
    keys = kvm[:, :width]
    values = kvm[:, width:] * flags
    lane_head = head_of_lane(count, width, heads)
    for head in range(heads):
        at = pl.ds(head * count, count)
        kbd[at, :] = only(keys, head, lane_head)
        vbd[at, :] = flagged(values, flags, head, heads, lane_head)
    middle = heads // 2 * count
    for begin in range(0, rows, block):
        at = pl.ds(begin, block)
        x = queries[at, :].astype(jnp.float32)
        qc = dot(rms_round(x), wq[...]).astype(jnp.bfloat16)
        scores = dot_t(qc, kbd[...])
        weights = []
        for head in range(heads):
            s = scores[:, head * count : (head + 1) * count]
            top = jnp.max(s, axis=-1, keepdims=True)
            weights.append(weigh(s, top, temp[head] * (LOG2E / math.sqrt(hsize))))
        low = dot(jnp.concatenate(weights[: heads // 2], axis=1), vbd[:middle, :])
        high = dot(jnp.concatenate(weights[heads // 2 :], axis=1), vbd[middle:, :])
        x1 = x + dot(normed(low, high), wo[...])
        x1_ref[at, :] = x1
        qkv = dot(rms_round(x1), wqkv[...]).astype(jnp.bfloat16)
        q_ref[at, :] = qkv[:, :width]
        slot = lax.broadcasted_iota(jnp.int32, (block, width), 0) + begin
        live = slot < counts[0]
        key = qkv[:, width : 2 * width]
        if begin == 0:
            first = key[:1]
        kv_ref[at, :width] = jnp.where(live, key, first)
        kv_ref[at, width:] = jnp.where(live, qkv[:, 2 * width :], jnp.bfloat16(DEAD_V))


def self_kernel(
    block, temp, counts, x1_ref, q_ref, own, other, wo, up, down, w1, w2, w3, features, boxes, vbd
):
    heads = temp.shape[0]
    rows, width = q_ref.shape
    hsize = width // heads
    lane_head = head_of_lane(rows, width, heads)
    for side, kv in enumerate((own, other)):
        values = kv[:, width:]
        live = values < jnp.bfloat16(DEAD_V)
        flags = jnp.where(live, jnp.bfloat16(1), jnp.bfloat16(0))
        values = jnp.where(live, values, jnp.bfloat16(0))
        for head in range(heads):
            vbd[side, head] = flagged(values, flags, head, heads, lane_head)
    lane_head = head_of_lane(block, width, heads)

    def visit(index, carry):
        begin = pl.multiple_of(index * block, block)
        at = pl.ds(begin, block)
        q = q_ref[at, :]
        sums = []
        for head in range(heads):
            qm = only(q, head, lane_head)
            s0 = dot_t(qm, own[:, :width])
            s1 = dot_t(qm, other[:, :width])
            top = jnp.maximum(
                jnp.max(s0, axis=-1, keepdims=True), jnp.max(s1, axis=-1, keepdims=True)
            )
            scale = temp[head] * (LOG2E / math.sqrt(hsize))
            part = dot(weigh(s0, top, scale), vbd[0, head])
            part += dot(weigh(s1, top, scale), vbd[1, head])
            if head % (heads // 2) == 0:
                sums.append(part)
            else:
                sums[-1] += part
        x2 = x1_ref[at, :] + dot(normed(*sums), wo[...])
        upper = jnp.maximum(dot(rms_round(x2), up[...]), 0.0).astype(jnp.bfloat16)
        x3 = x2 + dot(upper, down[...])
        slot = lax.broadcasted_iota(jnp.int32, (block, width), 0) + begin
        features[at, :] = jnp.where(slot < counts[0], x3, 0.0)
        b1 = jnp.maximum(dot(rms_round(x3), w1[...]), 0.0).astype(jnp.bfloat16)
        b2 = jnp.maximum(dot(b1, w2[...]), 0.0).astype(jnp.bfloat16)
        raw = lax.dot_general(
            w3[...], b2, (((0,), (1,)), ((), ())), preferred_element_type=jnp.float32
        )
        slot = lax.broadcasted_iota(jnp.int32, raw.shape, 1) + begin
        boxes[:, at] = jnp.where(slot < counts[0], 1.0 / (1.0 + jnp.exp(-raw)), 0.0)
        return carry

    lax.fori_loop(0, rows // block, visit, 0)


def gather_xor(x, axis):
    size = lax.axis_size(axis)
    step = 1
    pieces = [x]
    while step < size:
        group = min(8, size // step)
        x = pieces[0] if len(pieces) == 1 else jnp.concatenate(pieces, axis=0)
        pieces = [x]
        for k in range(1, group):
            pairs = [(i, i ^ (k * step)) for i in range(size)]
            pieces.append(lax.ppermute(x, axis, pairs))
        step *= group
    return pieces


def swap(x, axis):
    size = lax.axis_size(axis)
    return lax.ppermute(x, axis, [(i, i ^ 1) for i in range(size)])


def local(
    queries,
    counts,
    memory,
    mem_mask,
    cross_wq,
    cross_wkv,
    cross_wo,
    self_wqkv,
    self_wo,
    ffn_up,
    ffn_down,
    box_w1,
    box_w2,
    box_w3,
    cross_temp,
    self_temp,
):
    rows, width = queries.shape
    heads = cross_temp.shape[0]
    pieces = gather_xor(jnp.where((mem_mask > 0)[:, None], memory, jnp.bfloat16(DEAD)), "row")
    tile = memory.shape[0]
    count = sum(piece.shape[0] for piece in pieces)
    block = rows if count <= 128 else min(rows, 128)
    x1, q, kv = pl.pallas_call(
        functools.partial(cross_kernel, len(pieces), block, tile),
        out_shape=(
            jax.ShapeDtypeStruct((rows, width), jnp.float32),
            jax.ShapeDtypeStruct((rows, width), jnp.bfloat16),
            jax.ShapeDtypeStruct((rows, 2 * width), jnp.bfloat16),
        ),
        in_specs=[SMEM, SMEM] + [VMEM] * (5 + len(pieces)),
        out_specs=(VMEM, VMEM, VMEM),
        scratch_shapes=[
            pltpu.VMEM((heads * count, width), jnp.bfloat16),
            pltpu.VMEM((heads * count, width), jnp.bfloat16),
        ],
        compiler_params=pltpu.CompilerParams(vmem_limit_bytes=40 * 2**20),
        name="cross",
    )(cross_temp, counts, queries, *pieces, cross_wq, cross_wkv, cross_wo, self_wqkv)
    other = swap(kv, "col")
    block = min(256, rows)
    features, boxes = pl.pallas_call(
        functools.partial(self_kernel, block),
        out_shape=(
            jax.ShapeDtypeStruct((rows, width), jnp.float32),
            jax.ShapeDtypeStruct((box_w3.shape[1], rows), jnp.float32),
        ),
        in_specs=[SMEM, SMEM] + [VMEM] * 10,
        out_specs=(VMEM, VMEM),
        scratch_shapes=[pltpu.VMEM((2, heads, rows, width), jnp.bfloat16)],
        compiler_params=pltpu.CompilerParams(vmem_limit_bytes=40 * 2**20),
        name="self",
    )(
        self_temp, counts, x1, q, kv, other, self_wo, ffn_up, ffn_down, box_w1, box_w2, box_w3
    )
    return features, boxes


def solution(mesh):
    return jax.shard_map(
        local,
        mesh=mesh,
        in_specs=(
            P(("parts", "row", "col"), None),
            P(("parts", "row", "col")),
            P(("parts", "row", "col"), None),
            P(("parts", "row", "col")),
            P(),
            P(),
            P(),
            P(),
            P(),
            P(),
            P(),
            P(),
            P(),
            P(),
            P(),
            P(),
        ),
        out_specs=(P(("parts", "row", "col"), None), P(None, ("parts", "row", "col"))),
        check_vma=False,
    )
```

```python
import functools
import math

import jax
import jax.numpy as jnp
from jax import lax
from jax.experimental import pallas as pl
from jax.experimental.pallas import tpu as pltpu
from jax.sharding import PartitionSpec as P

EPS = 1e-06
DEAD = 64.0
DEAD_V = 4096.0
LOG2E = math.log2(math.e)
VMEM = pl.BlockSpec(memory_space=pltpu.VMEM)
HBM = pl.BlockSpec(memory_space=pltpu.HBM)


def rms_round(x):
    return (x * lax.rsqrt(jnp.mean(x * x, axis=-1, keepdims=True) + EPS)).astype(jnp.bfloat16)


def dot(a, b):
    return jnp.dot(a, b, preferred_element_type=jnp.float32)


def dot_t(a, b):
    return lax.dot_general(a, b, (((1,), (1,)), ((), ())), preferred_element_type=jnp.float32)


def head_of_lane(rows, width, heads):
    return lax.broadcasted_iota(jnp.int32, (rows, width), 1) // (width // heads)


def only(x, head, lane_head):
    return jnp.where(lane_head == head, x, jnp.zeros_like(x))


def flagged(values, flags, head, heads, lane_head):
    other = (head + heads // 2) % heads
    rest = jnp.where(lane_head == other, flags, jnp.zeros_like(values))
    return jnp.where(lane_head == head, values, rest)


def weigh(scores, top, scale):
    return jnp.exp2(((scores - top) * scale).astype(jnp.bfloat16))


def normed(low, high):
    half = low.shape[1] // 2
    return jnp.concatenate(
        [low[:, :half] / low[:, half:], high[:, half:] / high[:, :half]], axis=1
    ).astype(jnp.bfloat16)


def mark_kernel(memory, mask, out, held, flags, sems):
    copies = [
        pltpu.make_async_copy(memory, held, sems.at[0]),
        pltpu.make_async_copy(mask, flags, sems.at[1]),
    ]
    for copy in copies:
        copy.start()
    for copy in copies:
        copy.wait()
    row = lax.broadcasted_iota(jnp.int32, held.shape, 0)
    tokens = held[...].astype(jnp.float32)
    for j in range(held.shape[0]):
        tokens = jnp.where((row == j) & (flags[j] <= 0), DEAD, tokens)
    out[...] = tokens.astype(jnp.bfloat16)


def load_kernel(n, *refs):
    queries, wq, counts, cross_temp, self_temp = refs[:5]
    sources = refs[5 : 5 + n]
    x_ref, qc_ref, scale_ref, count_ref = refs[5 + n : 9 + n]
    targets = refs[9 + n : 9 + 2 * n]
    wq_held, count_held, cross_held, self_held, sems = refs[9 + 2 * n :]
    pairs = [
        (counts, count_held),
        (cross_temp, cross_held),
        (self_temp, self_held),
        (queries, x_ref),
        (wq, wq_held),
    ]
    pairs += list(zip(sources, targets))
    copies = [pltpu.make_async_copy(a, b, sems.at[i]) for i, (a, b) in enumerate(pairs)]
    for copy in copies:
        copy.start()
    for copy in copies[:5]:
        copy.wait()
    heads = cross_temp.shape[0]
    factor = LOG2E / math.sqrt(x_ref.shape[1] // heads)
    lanes = scale_ref.shape[1]
    for side, temp in enumerate((cross_held, self_held)):
        for head in range(heads):
            at = pl.ds(side * heads + head, 1)
            scale_ref[at, :] = jnp.full((1, lanes), temp[head] * factor, jnp.float32)
    count_ref[...] = jnp.full(count_ref.shape, count_held[0], jnp.int32)
    x = x_ref[...].astype(jnp.float32)
    qc_ref[...] = dot(rms_round(x), wq_held[...]).astype(jnp.bfloat16)
    for copy in copies[5:]:
        copy.wait()


def cross_kernel(n, block, tile, heads, scales, counts, queries, qc, *refs):
    pieces = refs[:n]
    wkv, wo, wqkv, x1_ref, q_ref, kv_ref, kbd, vbd = refs[n:]
    rows, width = queries.shape
    tokens, flags = [], []
    for piece in pieces:
        held = piece[...].astype(jnp.float32)
        dead = held >= DEAD
        for begin in range(0, held.shape[0], tile):
            part = held[begin : begin + tile]
            gone = dead[begin : begin + tile]
            tokens.append(jnp.where(gone, part[:1], part).astype(jnp.bfloat16))
            flags.append(jnp.where(gone, 0.0, 1.0).astype(jnp.bfloat16))
    tokens = jnp.concatenate(tokens, axis=0)
    flags = jnp.concatenate(flags, axis=0)
    count = tokens.shape[0]
    kvm = dot(tokens, wkv[...]).astype(jnp.bfloat16)
    keys = kvm[:, :width]
    values = kvm[:, width:] * flags
    lane_head = head_of_lane(count, width, heads)
    for head in range(heads):
        at = pl.ds(head * count, count)
        kbd[at, :] = only(keys, head, lane_head)
        vbd[at, :] = flagged(values, flags, head, heads, lane_head)
    middle = heads // 2 * count
    for begin in range(0, rows, block):
        at = pl.ds(begin, block)
        x = queries[at, :].astype(jnp.float32)
        scores = dot_t(qc[at, :], kbd[...])
        weights = []
        for head in range(heads):
            s = scores[:, head * count : (head + 1) * count]
            top = jnp.max(s, axis=-1, keepdims=True)
            weights.append(weigh(s, top, scales[head : head + 1, :1]))
        low = dot(jnp.concatenate(weights[: heads // 2], axis=1), vbd[:middle, :])
        high = dot(jnp.concatenate(weights[heads // 2 :], axis=1), vbd[middle:, :])
        x1 = x + dot(normed(low, high), wo[...])
        x1_ref[at, :] = x1
        qkv = dot(rms_round(x1), wqkv[...]).astype(jnp.bfloat16)
        q_ref[at, :] = qkv[:, :width]
        slot = lax.broadcasted_iota(jnp.int32, (block, width), 0) + begin
        live = slot < counts[:1, :1]
        key = qkv[:, width : 2 * width]
        if begin == 0:
            first = key[:1]
        kv_ref[at, :width] = jnp.where(live, key, first)
        kv_ref[at, width:] = jnp.where(live, qkv[:, 2 * width :], jnp.bfloat16(DEAD_V))


def self_kernel(
    block,
    heads,
    scales,
    counts,
    x1_ref,
    q_ref,
    own,
    other,
    wo,
    up,
    down,
    w1,
    w2,
    w3,
    features,
    boxes,
    vbd,
    out,
    sems,
):
    rows, width = q_ref.shape
    lane_head = head_of_lane(rows, width, heads)
    for side, kv in enumerate((own, other)):
        values = kv[:, width:]
        live = values < jnp.bfloat16(DEAD_V)
        flags = jnp.where(live, jnp.bfloat16(1), jnp.bfloat16(0))
        values = jnp.where(live, values, jnp.bfloat16(0))
        for head in range(heads):
            vbd[side, head] = flagged(values, flags, head, heads, lane_head)
    lane_head = head_of_lane(block, width, heads)
    blocks = rows // block

    def leave(index):
        at = pl.ds(pl.multiple_of(index * block, block), block)
        return pltpu.make_async_copy(out.at[at, :], features.at[at, :], sems.at[index])

    def visit(index, carry):
        begin = pl.multiple_of(index * block, block)
        at = pl.ds(begin, block)
        q = q_ref[at, :]
        sums = []
        for head in range(heads):
            qm = only(q, head, lane_head)
            s0 = dot_t(qm, own[:, :width])
            s1 = dot_t(qm, other[:, :width])
            top = jnp.maximum(
                jnp.max(s0, axis=-1, keepdims=True), jnp.max(s1, axis=-1, keepdims=True)
            )
            scale = scales[heads + head : heads + head + 1, :1]
            part = dot(weigh(s0, top, scale), vbd[0, head])
            part += dot(weigh(s1, top, scale), vbd[1, head])
            if head % (heads // 2) == 0:
                sums.append(part)
            else:
                sums[-1] += part
        x2 = x1_ref[at, :] + dot(normed(*sums), wo[...])
        upper = jnp.maximum(dot(rms_round(x2), up[...]), 0.0).astype(jnp.bfloat16)
        x3 = x2 + dot(upper, down[...])
        slot = lax.broadcasted_iota(jnp.int32, (block, width), 0) + begin
        out[at, :] = jnp.where(slot < counts[:1, :1], x3, 0.0)
        leave(index).start()
        b1 = jnp.maximum(dot(rms_round(x3), w1[...]), 0.0).astype(jnp.bfloat16)
        b2 = jnp.maximum(dot(b1, w2[...]), 0.0).astype(jnp.bfloat16)
        raw = dot_t(w3[...], b2)
        slot = lax.broadcasted_iota(jnp.int32, raw.shape, 1) + begin
        boxes[:, at] = jnp.where(slot < counts[:1, :1], 1.0 / (1.0 + jnp.exp(-raw)), 0.0)
        return carry

    lax.fori_loop(0, blocks, visit, 0)
    for index in range(blocks):
        leave(index).wait()


def gather_doubling(x, axis):
    size = lax.axis_size(axis)
    step = 1
    while step < size:
        other = lax.ppermute(x, axis, [(i, i ^ step) for i in range(size)])
        step *= 2
        if step == size:
            return [x, other]
        x = jnp.concatenate([x, other], axis=0)
    return [x]


def swap(x, axis):
    size = lax.axis_size(axis)
    return lax.ppermute(x, axis, [(i, i ^ 1) for i in range(size)])


def local(
    queries,
    counts,
    memory,
    mem_mask,
    cross_wq,
    cross_wkv,
    cross_wo,
    self_wqkv,
    self_wo,
    ffn_up,
    ffn_down,
    box_w1,
    box_w2,
    box_w3,
    cross_temp,
    self_temp,
):
    rows, width = queries.shape
    heads = cross_temp.shape[0]
    tile = memory.shape[0]
    params = pltpu.CompilerParams(vmem_limit_bytes=40 * 2**20)
    marked = pl.pallas_call(
        mark_kernel,
        out_shape=jax.ShapeDtypeStruct(memory.shape, memory.dtype),
        in_specs=[HBM, HBM],
        out_specs=VMEM,
        scratch_shapes=[
            pltpu.VMEM(memory.shape, memory.dtype),
            pltpu.SMEM(mem_mask.shape, mem_mask.dtype),
            pltpu.SemaphoreType.DMA((2,)),
        ],
        name="mark",
    )(memory, mem_mask)
    pieces = gather_doubling(marked, "row")
    weights = [cross_wkv, cross_wo, self_wqkv, self_wo, ffn_up, ffn_down]
    weights += [box_w1, box_w2, jnp.transpose(box_w3)]
    shapes = [jax.ShapeDtypeStruct(w.shape, w.dtype) for w in weights]
    tokens = jax.ShapeDtypeStruct((rows, width), jnp.bfloat16)
    x, qc, scales, live, *weights = pl.pallas_call(
        functools.partial(load_kernel, len(weights)),
        out_shape=[
            tokens,
            tokens,
            jax.ShapeDtypeStruct((2 * heads, 128), jnp.float32),
            jax.ShapeDtypeStruct((8, 128), jnp.int32),
        ]
        + shapes,
        in_specs=[HBM] * (5 + len(weights)),
        out_specs=[VMEM] * (4 + len(weights)),
        scratch_shapes=[
            pltpu.VMEM(cross_wq.shape, cross_wq.dtype),
            pltpu.SMEM(counts.shape, counts.dtype),
            pltpu.SMEM(cross_temp.shape, cross_temp.dtype),
            pltpu.SMEM(self_temp.shape, self_temp.dtype),
            pltpu.SemaphoreType.DMA((5 + len(weights),)),
        ],
        compiler_params=params,
        cost_estimate=pl.CostEstimate(
            flops=2 * rows * width * width, bytes_accessed=4 * 2**20, transcendentals=0
        ),
        name="load",
    )(queries, cross_wq, counts, cross_temp, self_temp, *weights)
    wkv, wo, wqkv, *weights = weights
    count = sum(piece.shape[0] for piece in pieces)
    block = rows if count <= 128 else min(rows, 128)
    x1, q, kv = pl.pallas_call(
        functools.partial(cross_kernel, len(pieces), block, tile, heads),
        out_shape=(
            jax.ShapeDtypeStruct((rows, width), jnp.float32),
            tokens,
            jax.ShapeDtypeStruct((rows, 2 * width), jnp.bfloat16),
        ),
        in_specs=[VMEM] * (7 + len(pieces)),
        out_specs=(VMEM, VMEM, VMEM),
        scratch_shapes=[
            pltpu.VMEM((heads * count, width), jnp.bfloat16),
            pltpu.VMEM((heads * count, width), jnp.bfloat16),
        ],
        compiler_params=params,
        name="cross",
    )(scales, live, x, qc, *pieces, wkv, wo, wqkv)
    other = swap(kv, "col")
    block = min(256, rows)
    return pl.pallas_call(
        functools.partial(self_kernel, block, heads),
        out_shape=(
            jax.ShapeDtypeStruct((rows, width), jnp.float32),
            jax.ShapeDtypeStruct((box_w3.shape[1], rows), jnp.float32),
        ),
        in_specs=[VMEM] * (6 + len(weights)),
        out_specs=(HBM, VMEM),
        scratch_shapes=[
            pltpu.VMEM((2, heads, rows, width), jnp.bfloat16),
            pltpu.VMEM((rows, width), jnp.float32),
            pltpu.SemaphoreType.DMA((rows // block,)),
        ],
        compiler_params=params,
        name="self",
    )(scales, live, x1, q, kv, other, *weights)


def solution(mesh):
    return jax.shard_map(
        local,
        mesh=mesh,
        in_specs=(
            P(("parts", "row", "col"), None),
            P(("parts", "row", "col")),
            P(("parts", "row", "col"), None),
            P(("parts", "row", "col")),
            P(),
            P(),
            P(),
            P(),
            P(),
            P(),
            P(),
            P(),
            P(),
            P(),
            P(),
            P(),
        ),
        out_specs=(P(("parts", "row", "col"), None), P(None, ("parts", "row", "col"))),
        check_vma=False,
    )
```

```python
import functools
import math

import jax
import jax.numpy as jnp
from jax import lax
from jax.experimental import pallas as pl
from jax.experimental.pallas import tpu as pltpu
from jax.sharding import PartitionSpec as P

EPS = 1e-06
DEAD = 64.0
DEAD_V = 4096.0
LOG2E = math.log2(math.e)
VMEM = pl.BlockSpec(memory_space=pltpu.VMEM)
SMEM = pl.BlockSpec(memory_space=pltpu.SMEM)
HBM = pl.BlockSpec(memory_space=pltpu.HBM)


def rms_round(x):
    return (x * lax.rsqrt(jnp.mean(x * x, axis=-1, keepdims=True) + EPS)).astype(jnp.bfloat16)


def dot(a, b):
    return jnp.dot(a, b, preferred_element_type=jnp.float32)


def dot_t(a, b):
    return lax.dot_general(a, b, (((1,), (1,)), ((), ())), preferred_element_type=jnp.float32)


def head_of_lane(rows, width, heads):
    return lax.broadcasted_iota(jnp.int32, (rows, width), 1) // (width // heads)


def only(x, head, lane_head):
    return jnp.where(lane_head == head, x, jnp.zeros_like(x))


def flagged(values, flags, head, heads, lane_head):
    other = (head + heads // 2) % heads
    rest = jnp.where(lane_head == other, flags, jnp.zeros_like(values))
    return jnp.where(lane_head == head, values, rest)


def weigh(scores, top, scale):
    return jnp.exp2(((scores - top) * scale).astype(jnp.bfloat16))


def normed(low, high):
    half = low.shape[1] // 2
    return jnp.concatenate(
        [low[:, :half] / low[:, half:], high[:, half:] / high[:, :half]], axis=1
    ).astype(jnp.bfloat16)


def mark_kernel(memory, mask, out, held, flags, sems):
    copies = [
        pltpu.make_async_copy(memory, held, sems.at[0]),
        pltpu.make_async_copy(mask, flags, sems.at[1]),
    ]
    for copy in copies:
        copy.start()
    for copy in copies:
        copy.wait()
    row = lax.broadcasted_iota(jnp.int32, held.shape, 0)
    tokens = held[...].astype(jnp.float32)
    for j in range(held.shape[0]):
        tokens = jnp.where((row == j) & (flags[j] <= 0), DEAD, tokens)
    tokens = tokens.astype(jnp.bfloat16)
    for copy in range(out.shape[0]):
        out[copy] = tokens


def load_kernel(n, *refs):
    counts, queries, wq, cross_temp, self_temp = refs[:5]
    sources = refs[5 : 5 + n]
    x_ref, qc_ref, scale_ref, count_ref = refs[5 + n : 9 + n]
    targets = refs[9 + n : 9 + 2 * n]
    wq_held, cross_held, self_held, sems = refs[9 + 2 * n :]
    pairs = [
        (cross_temp, cross_held),
        (self_temp, self_held),
        (queries, x_ref),
        (wq, wq_held),
    ]
    pairs += list(zip(sources, targets))
    copies = [pltpu.make_async_copy(a, b, sems.at[i]) for i, (a, b) in enumerate(pairs)]
    for copy in copies:
        copy.start()
    for copy in copies[:4]:
        copy.wait()
    heads = cross_temp.shape[0]
    factor = LOG2E / math.sqrt(x_ref.shape[1] // heads)
    lanes = scale_ref.shape[1]
    for side, temp in enumerate((cross_held, self_held)):
        for head in range(heads):
            at = pl.ds(side * heads + head, 1)
            scale_ref[at, :] = jnp.full((1, lanes), temp[head] * factor, jnp.float32)
    count_ref[...] = jnp.full(count_ref.shape, counts[0], jnp.int32)
    x = x_ref[...].astype(jnp.float32)
    qc_ref[...] = dot(rms_round(x), wq_held[...]).astype(jnp.bfloat16)
    for copy in copies[4:]:
        copy.wait()


def cross_kernel(n, block, tile, heads, scales, counts, queries, qc, *refs):
    pieces = refs[:n]
    wkv, wo, wqkv, x1_ref, q_ref, kv_ref, kbd, vbd = refs[n:]
    rows, width = queries.shape
    tokens, flags = [], []
    for piece in pieces:
        held = piece[...].astype(jnp.float32)
        dead = held >= DEAD
        for begin in range(0, held.shape[0], tile):
            part = held[begin : begin + tile]
            gone = dead[begin : begin + tile]
            tokens.append(jnp.where(gone, part[:1], part).astype(jnp.bfloat16))
            flags.append(jnp.where(gone, 0.0, 1.0).astype(jnp.bfloat16))
    tokens = jnp.concatenate(tokens, axis=0)
    flags = jnp.concatenate(flags, axis=0)
    count = tokens.shape[0]
    kvm = dot(tokens, wkv[...]).astype(jnp.bfloat16)
    keys = kvm[:, :width]
    values = kvm[:, width:] * flags
    lane_head = head_of_lane(count, width, heads)
    for head in range(heads):
        at = pl.ds(head * count, count)
        kbd[at, :] = only(keys, head, lane_head)
        vbd[at, :] = flagged(values, flags, head, heads, lane_head)
    middle = heads // 2 * count
    for begin in range(0, rows, block):
        at = pl.ds(begin, block)
        x = queries[at, :].astype(jnp.float32)
        scores = dot_t(qc[at, :], kbd[...])
        weights = []
        for head in range(heads):
            s = scores[:, head * count : (head + 1) * count]
            top = jnp.max(s, axis=-1, keepdims=True)
            weights.append(weigh(s, top, scales[head : head + 1, :1]))
        low = dot(jnp.concatenate(weights[: heads // 2], axis=1), vbd[:middle, :])
        high = dot(jnp.concatenate(weights[heads // 2 :], axis=1), vbd[middle:, :])
        x1 = x + dot(normed(low, high), wo[...])
        x1_ref[at, :] = x1
        qkv = dot(rms_round(x1), wqkv[...]).astype(jnp.bfloat16)
        q_ref[at, :] = qkv[:, :width]
        slot = lax.broadcasted_iota(jnp.int32, (block, width), 0) + begin
        live = slot < counts[:1, :1]
        key = qkv[:, width : 2 * width]
        if begin == 0:
            first = key[:1]
        kv_ref[at, :width] = jnp.where(live, key, first)
        kv_ref[at, width:] = jnp.where(live, qkv[:, 2 * width :], jnp.bfloat16(DEAD_V))


def self_kernel(
    block,
    heads,
    scales,
    counts,
    x1_ref,
    q_ref,
    own,
    other,
    wo,
    up,
    down,
    w1,
    w2,
    w3,
    features,
    boxes,
    vbd,
    out,
    sems,
):
    rows, width = q_ref.shape
    lane_head = head_of_lane(rows, width, heads)
    for side, kv in enumerate((own, other)):
        values = kv[:, width:]
        live = values < jnp.bfloat16(DEAD_V)
        flags = jnp.where(live, jnp.bfloat16(1), jnp.bfloat16(0))
        values = jnp.where(live, values, jnp.bfloat16(0))
        for head in range(heads):
            vbd[side, head] = flagged(values, flags, head, heads, lane_head)
    lane_head = head_of_lane(block, width, heads)
    blocks = rows // block

    def leave(index):
        at = pl.ds(pl.multiple_of(index * block, block), block)
        return pltpu.make_async_copy(out.at[at, :], features.at[at, :], sems.at[index])

    def visit(index, carry):
        begin = pl.multiple_of(index * block, block)
        at = pl.ds(begin, block)
        q = q_ref[at, :]
        sums = []
        for head in range(heads):
            qm = only(q, head, lane_head)
            s0 = dot_t(qm, own[:, :width])
            s1 = dot_t(qm, other[:, :width])
            top = jnp.maximum(
                jnp.max(s0, axis=-1, keepdims=True), jnp.max(s1, axis=-1, keepdims=True)
            )
            scale = scales[heads + head : heads + head + 1, :1]
            part = dot(weigh(s0, top, scale), vbd[0, head])
            part += dot(weigh(s1, top, scale), vbd[1, head])
            if head % (heads // 2) == 0:
                sums.append(part)
            else:
                sums[-1] += part
        x2 = x1_ref[at, :] + dot(normed(*sums), wo[...])
        upper = jnp.maximum(dot(rms_round(x2), up[...]), 0.0).astype(jnp.bfloat16)
        x3 = x2 + dot(upper, down[...])
        slot = lax.broadcasted_iota(jnp.int32, (block, width), 0) + begin
        out[at, :] = jnp.where(slot < counts[:1, :1], x3, 0.0)
        leave(index).start()
        b1 = jnp.maximum(dot(rms_round(x3), w1[...]), 0.0).astype(jnp.bfloat16)
        b2 = jnp.maximum(dot(b1, w2[...]), 0.0).astype(jnp.bfloat16)
        raw = dot_t(w3[...], b2)
        slot = lax.broadcasted_iota(jnp.int32, raw.shape, 1) + begin
        boxes[:, at] = jnp.where(slot < counts[:1, :1], 1.0 / (1.0 + jnp.exp(-raw)), 0.0)
        return carry

    lax.fori_loop(0, blocks, visit, 0)
    for index in range(blocks):
        leave(index).wait()


def in_hbm(x):
    return pltpu.with_memory_space_constraint(x, pltpu.HBM)


def swap(x, axis):
    size = lax.axis_size(axis)
    return lax.ppermute(x, axis, [(i, i ^ 1) for i in range(size)])


def local(
    queries,
    counts,
    memory,
    mem_mask,
    cross_wq,
    cross_wkv,
    cross_wo,
    self_wqkv,
    self_wo,
    ffn_up,
    ffn_down,
    box_w1,
    box_w2,
    box_w3,
    cross_temp,
    self_temp,
):
    rows, width = queries.shape
    heads = cross_temp.shape[0]
    tile = memory.shape[0]
    params = pltpu.CompilerParams(vmem_limit_bytes=32 * 2**20)
    marked = pl.pallas_call(
        mark_kernel,
        out_shape=pltpu.VMEM((lax.axis_size("row"), tile, width), memory.dtype),
        in_specs=[HBM, HBM],
        out_specs=VMEM,
        scratch_shapes=[
            pltpu.VMEM(memory.shape, memory.dtype),
            pltpu.SMEM(mem_mask.shape, mem_mask.dtype),
            pltpu.SemaphoreType.DMA((2,)),
        ],
        name="mark",
    )(in_hbm(memory), in_hbm(mem_mask))
    gathered = lax.all_to_all(marked, "row", 0, 0, tiled=True)
    pieces = [gathered.reshape(-1, width)]
    weights = [cross_wkv, cross_wo, self_wqkv, self_wo, ffn_up, ffn_down]
    weights += [box_w1, box_w2, jnp.transpose(box_w3)]
    shapes = [pltpu.VMEM(w.shape, w.dtype) for w in weights]
    tokens = pltpu.VMEM((rows, width), jnp.bfloat16)
    x, qc, scales, live, *weights = pl.pallas_call(
        functools.partial(load_kernel, len(weights)),
        out_shape=[
            tokens,
            tokens,
            pltpu.VMEM((2 * heads, 128), jnp.float32),
            pltpu.VMEM((8, 128), jnp.int32),
        ]
        + shapes,
        in_specs=[SMEM] + [HBM] * (4 + len(weights)),
        out_specs=[VMEM] * (4 + len(weights)),
        scratch_shapes=[
            pltpu.VMEM(cross_wq.shape, cross_wq.dtype),
            pltpu.SMEM(cross_temp.shape, cross_temp.dtype),
            pltpu.SMEM(self_temp.shape, self_temp.dtype),
            pltpu.SemaphoreType.DMA((4 + len(weights),)),
        ],
        compiler_params=params,
        cost_estimate=pl.CostEstimate(
            flops=2 * rows * width * width, bytes_accessed=4 * 2**20, transcendentals=0
        ),
        name="load",
    )(counts, *map(in_hbm, (queries, cross_wq, cross_temp, self_temp, *weights)))
    wkv, wo, wqkv, *weights = weights
    count = sum(piece.shape[0] for piece in pieces)
    block = rows if count <= 128 else min(rows, 128)
    x1, q, kv = pl.pallas_call(
        functools.partial(cross_kernel, len(pieces), block, tile, heads),
        out_shape=(
            pltpu.VMEM((rows, width), jnp.float32),
            tokens,
            pltpu.VMEM((rows, 2 * width), jnp.bfloat16),
        ),
        in_specs=[VMEM] * (7 + len(pieces)),
        out_specs=(VMEM, VMEM, VMEM),
        scratch_shapes=[
            pltpu.VMEM((heads * count, width), jnp.bfloat16),
            pltpu.VMEM((heads * count, width), jnp.bfloat16),
        ],
        compiler_params=params,
        name="cross",
    )(scales, live, x, qc, *pieces, wkv, wo, wqkv)
    other = swap(kv, "col")
    block = min(256, rows)
    return pl.pallas_call(
        functools.partial(self_kernel, block, heads),
        out_shape=(
            jax.ShapeDtypeStruct((rows, width), jnp.float32),
            jax.ShapeDtypeStruct((box_w3.shape[1], rows), jnp.float32),
        ),
        in_specs=[VMEM] * (6 + len(weights)),
        out_specs=(HBM, VMEM),
        scratch_shapes=[
            pltpu.VMEM((2, heads, rows, width), jnp.bfloat16),
            pltpu.VMEM((rows, width), jnp.float32),
            pltpu.SemaphoreType.DMA((rows // block,)),
        ],
        compiler_params=params,
        name="self",
    )(scales, live, x1, q, kv, other, *weights)


def solution(mesh):
    return jax.shard_map(
        local,
        mesh=mesh,
        in_specs=(
            P(("parts", "row", "col"), None),
            P(("parts", "row", "col")),
            P(("parts", "row", "col"), None),
            P(("parts", "row", "col")),
            P(),
            P(),
            P(),
            P(),
            P(),
            P(),
            P(),
            P(),
            P(),
            P(),
            P(),
            P(),
        ),
        out_specs=(P(("parts", "row", "col"), None), P(None, ("parts", "row", "col"))),
        check_vma=False,
    )
```

```python
import functools
import math

import jax
import jax.numpy as jnp
from jax import lax
from jax.experimental import pallas as pl
from jax.experimental.pallas import tpu as pltpu
from jax.sharding import PartitionSpec as P

EPS = 1e-06
DEAD = 64.0
DEAD_V = 4096.0
LOG2E = math.log2(math.e)
VMEM = pl.BlockSpec(memory_space=pltpu.VMEM)
SMEM = pl.BlockSpec(memory_space=pltpu.SMEM)
HBM = pl.BlockSpec(memory_space=pltpu.HBM)


def rms_round(x):
    return (x * lax.rsqrt(jnp.mean(x * x, axis=-1, keepdims=True) + EPS)).astype(jnp.bfloat16)


def dot(a, b):
    return jnp.dot(a, b, preferred_element_type=jnp.float32)


def dot_t(a, b):
    return lax.dot_general(a, b, (((1,), (1,)), ((), ())), preferred_element_type=jnp.float32)


def head_of_lane(rows, width, heads):
    return lax.broadcasted_iota(jnp.int32, (rows, width), 1) // (width // heads)


def only(x, head, lane_head):
    return jnp.where(lane_head == head, x, jnp.zeros_like(x))


def flagged(values, flags, head, heads, lane_head):
    other = (head + heads // 2) % heads
    rest = jnp.where(lane_head == other, flags, jnp.zeros_like(values))
    return jnp.where(lane_head == head, values, rest)


def weigh(scores, top, scale):
    return jnp.exp2(((scores - top) * scale).astype(jnp.bfloat16))


def normed(low, high):
    half = low.shape[1] // 2
    return jnp.concatenate(
        [low[:, :half] / low[:, half:], high[:, half:] / high[:, :half]], axis=1
    ).astype(jnp.bfloat16)


def mark_kernel(memory, mask, out, held, flags, sems):
    copies = [
        pltpu.make_async_copy(memory, held, sems.at[0]),
        pltpu.make_async_copy(mask, flags, sems.at[1]),
    ]
    for copy in copies:
        copy.start()
    for copy in copies:
        copy.wait()
    row = lax.broadcasted_iota(jnp.int32, held.shape, 0)
    tokens = held[...].astype(jnp.float32)
    for j in range(held.shape[0]):
        tokens = jnp.where((row == j) & (flags[j] <= 0), DEAD, tokens)
    tokens = tokens.astype(jnp.bfloat16)
    for copy in range(out.shape[0]):
        out[copy] = tokens


def load_kernel(
    counts,
    queries,
    wq,
    cross_temp,
    self_temp,
    wkv,
    wo,
    wqkv,
    x_ref,
    qc_ref,
    scale_ref,
    count_ref,
    packed,
    wvt_ref,
    wq_held,
    cross_held,
    self_held,
    sems,
):
    width = x_ref.shape[1]
    pairs = [(queries, x_ref), (wq, wq_held), (cross_temp, cross_held), (self_temp, self_held)]
    begin = 0
    for source in (wkv, wo, wqkv):
        end = begin + source.shape[1]
        pairs.append((source, packed.at[:, begin:end]))
        begin = end
    copies = [pltpu.make_async_copy(a, b, sems.at[i]) for i, (a, b) in enumerate(pairs)]
    for copy in copies:
        copy.start()
    for copy in copies[:4]:
        copy.wait()
    heads = cross_temp.shape[0]
    factor = LOG2E / math.sqrt(width // heads)
    lanes = scale_ref.shape[1]
    for side, temp in enumerate((cross_held, self_held)):
        for head in range(heads):
            at = pl.ds(side * heads + head, 1)
            scale_ref[at, :] = jnp.full((1, lanes), temp[head] * factor, jnp.float32)
    count_ref[...] = jnp.full(count_ref.shape, counts[0], jnp.int32)
    x = x_ref[...].astype(jnp.float32)
    qc_ref[...] = dot(rms_round(x), wq_held[...]).astype(jnp.bfloat16)
    for copy in copies[4:]:
        copy.wait()
    wvt_ref[...] = jnp.transpose(packed[:, -width:])


def cross_kernel(n, block, tile, heads, scales, counts, queries, qc, *refs):
    pieces = refs[:n]
    packed, wvt, x1_ref, q_ref, kv_ref, kbd, vbd = refs[n:]
    rows, width = queries.shape
    wkv = packed[:, : 2 * width]
    wo = packed[:, 2 * width : 3 * width]
    wqk = packed[:, 3 * width : 5 * width]
    tokens, flags = [], []
    for piece in pieces:
        held = piece[...].astype(jnp.float32)
        dead = held >= DEAD
        for begin in range(0, held.shape[0], tile):
            part = held[begin : begin + tile]
            gone = dead[begin : begin + tile]
            tokens.append(jnp.where(gone, part[:1], part).astype(jnp.bfloat16))
            flags.append(jnp.where(gone, 0.0, 1.0).astype(jnp.bfloat16))
    tokens = jnp.concatenate(tokens, axis=0)
    flags = jnp.concatenate(flags, axis=0)
    count = tokens.shape[0]
    kvm = dot(tokens, wkv).astype(jnp.bfloat16)
    keys = kvm[:, :width]
    values = kvm[:, width:] * flags
    lane_head = head_of_lane(count, width, heads)
    for head in range(heads):
        at = pl.ds(head * count, count)
        kbd[at, :] = only(keys, head, lane_head)
        vbd[at, :] = flagged(values, flags, head, heads, lane_head)
    middle = heads // 2 * count
    for begin in range(0, rows, block):
        at = pl.ds(begin, block)
        x = queries[at, :].astype(jnp.float32)
        scores = dot_t(qc[at, :], kbd[...])
        weights = []
        for head in range(heads):
            s = scores[:, head * count : (head + 1) * count]
            top = jnp.max(s, axis=-1, keepdims=True)
            weights.append(weigh(s, top, scales[head : head + 1, :1]))
        low = dot(jnp.concatenate(weights[: heads // 2], axis=1), vbd[:middle, :])
        high = dot(jnp.concatenate(weights[heads // 2 :], axis=1), vbd[middle:, :])
        x1 = x + dot(normed(low, high), wo)
        x1_ref[at, :] = x1
        hn1 = rms_round(x1)
        qk = dot(hn1, wqk).astype(jnp.bfloat16)
        q_ref[at, :] = qk[:, :width]
        slot = lax.broadcasted_iota(jnp.int32, (block, width), 0) + begin
        key = qk[:, width:]
        if begin == 0:
            first = key[:1]
        kv_ref[at, :] = jnp.where(slot < counts[:1, :1], key, first)
        value = dot_t(wvt[...], hn1).astype(jnp.bfloat16)
        slot = lax.broadcasted_iota(jnp.int32, (width, block), 1) + begin
        value = jnp.where(slot < counts[:1, :1], value, jnp.bfloat16(DEAD_V))
        for part in range(0, block, width):
            place = begin + part
            size = min(block, width)
            target = pl.ds(rows + place // width * width, width)
            lanes = pl.ds(place % width, size)
            kv_ref[target, lanes] = value[:, part : part + size]


def self_kernel(
    block,
    heads,
    scales,
    counts,
    x1_ref,
    q_ref,
    own,
    other,
    wo,
    up,
    down,
    w1,
    w2,
    w3,
    features,
    boxes,
    vt,
    ctx,
    out,
    wo_held,
    up_held,
    down_held,
    w1_held,
    w2_held,
    w3_held,
    sems,
):
    rows, width = q_ref.shape
    hsize = width // heads
    part = vt.shape[1] // heads
    held = (wo_held, up_held, down_held, w1_held, w2_held, w3_held)
    pairs = zip((wo, up, down, w1, w2, w3), held)
    copies = [pltpu.make_async_copy(a, b, sems.at[i]) for i, (a, b) in enumerate(pairs)]
    for copy in copies:
        copy.start()
    for side, kv in enumerate((own, other)):
        for begin in range(0, rows, width):
            lanes = pl.ds(begin, width)
            values = kv[rows + begin : rows + begin + width, :]
            live = values < jnp.bfloat16(DEAD_V)
            flags = jnp.where(live[: part - hsize], jnp.bfloat16(1), jnp.bfloat16(0))
            values = jnp.where(live, values, jnp.bfloat16(0))
            for head in range(heads):
                at = head * part
                vt[side, at : at + hsize, lanes] = values[head * hsize : (head + 1) * hsize]
                vt[side, at + hsize : at + part, lanes] = flags
    lane_head = head_of_lane(rows, width, heads)

    def visit(index, carry):
        at = pl.ds(pl.multiple_of(index * block, block), block)
        q = q_ref[at, :]
        for head in range(heads):
            s0 = dot_t(only(own[:rows, :], head, lane_head), q)
            s1 = dot_t(only(other[:rows, :], head, lane_head), q)
            top = jnp.maximum(
                jnp.max(s0, axis=0, keepdims=True), jnp.max(s1, axis=0, keepdims=True)
            )
            scale = scales[heads + head : heads + head + 1, :1]
            mine = pl.ds(head * part, part)
            total = dot(vt[0, mine, :], weigh(s0, top, scale))
            total += dot(vt[1, mine, :], weigh(s1, top, scale))
            mixed = total[:hsize] / total[hsize : hsize + 1]
            ctx[head * hsize : (head + 1) * hsize, at] = mixed.astype(jnp.bfloat16)
        return carry

    lax.fori_loop(0, rows // block, visit, 0)
    for copy in copies:
        copy.wait()
    mixed = lax.dot_general(
        ctx[...], wo_held[...], (((0,), (0,)), ((), ())), preferred_element_type=jnp.float32
    )
    x2 = x1_ref[...] + mixed
    upper = jnp.maximum(dot(rms_round(x2), up_held[...]), 0.0).astype(jnp.bfloat16)
    x3 = x2 + dot(upper, down_held[...])
    slot = lax.broadcasted_iota(jnp.int32, (rows, width), 0)
    out[...] = jnp.where(slot < counts[:1, :1], x3, 0.0)
    leave = pltpu.make_async_copy(out, features, sems.at[len(copies)])
    leave.start()
    b1 = jnp.maximum(dot(rms_round(x3), w1_held[...]), 0.0).astype(jnp.bfloat16)
    b2 = jnp.maximum(dot(b1, w2_held[...]), 0.0).astype(jnp.bfloat16)
    raw = dot_t(w3_held[...], b2)
    slot = lax.broadcasted_iota(jnp.int32, raw.shape, 1)
    boxes[...] = jnp.where(slot < counts[:1, :1], 1.0 / (1.0 + jnp.exp(-raw)), 0.0)
    leave.wait()


def in_hbm(x):
    return pltpu.with_memory_space_constraint(x, pltpu.HBM)


def swap(x, axis):
    size = lax.axis_size(axis)
    return lax.ppermute(x, axis, [(i, i ^ 1) for i in range(size)])


def local(
    queries,
    counts,
    memory,
    mem_mask,
    cross_wq,
    cross_wkv,
    cross_wo,
    self_wqkv,
    self_wo,
    ffn_up,
    ffn_down,
    box_w1,
    box_w2,
    box_w3,
    cross_temp,
    self_temp,
):
    rows, width = queries.shape
    heads = cross_temp.shape[0]
    tile = memory.shape[0]
    params = pltpu.CompilerParams(vmem_limit_bytes=32 * 2**20)
    marked = pl.pallas_call(
        mark_kernel,
        out_shape=pltpu.VMEM((lax.axis_size("row"), tile, width), memory.dtype),
        in_specs=[HBM, HBM],
        out_specs=VMEM,
        scratch_shapes=[
            pltpu.VMEM(memory.shape, memory.dtype),
            pltpu.SMEM(mem_mask.shape, mem_mask.dtype),
            pltpu.SemaphoreType.DMA((2,)),
        ],
        name="mark",
    )(in_hbm(memory), in_hbm(mem_mask))
    gathered = lax.all_to_all(marked, "row", 0, 0, tiled=True)
    pieces = [gathered.reshape(-1, width)]
    tokens = pltpu.VMEM((rows, width), jnp.bfloat16)
    packed_width = cross_wkv.shape[1] + cross_wo.shape[1] + self_wqkv.shape[1]
    sources = (queries, cross_wq, cross_temp, self_temp, cross_wkv, cross_wo, self_wqkv)
    x, qc, scales, live, packed, wvt = pl.pallas_call(
        load_kernel,
        out_shape=[
            tokens,
            tokens,
            pltpu.VMEM((2 * heads, 128), jnp.float32),
            pltpu.VMEM((8, 128), jnp.int32),
            pltpu.VMEM((width, packed_width), jnp.bfloat16),
            pltpu.VMEM((width, width), jnp.bfloat16),
        ],
        in_specs=[SMEM] + [HBM] * len(sources),
        out_specs=[VMEM] * 6,
        scratch_shapes=[
            pltpu.VMEM(cross_wq.shape, cross_wq.dtype),
            pltpu.SMEM(cross_temp.shape, cross_temp.dtype),
            pltpu.SMEM(self_temp.shape, self_temp.dtype),
            pltpu.SemaphoreType.DMA((len(sources),)),
        ],
        compiler_params=params,
        cost_estimate=pl.CostEstimate(
            flops=2 * rows * width * width, bytes_accessed=4 * 2**20, transcendentals=0
        ),
        name="load",
    )(counts, *map(in_hbm, sources))
    count = sum(piece.shape[0] for piece in pieces)
    block = rows if count <= 128 else min(rows, 128)
    kv_shape = pltpu.VMEM((2 * rows, width), jnp.bfloat16)
    x1, q, kv = pl.pallas_call(
        functools.partial(cross_kernel, len(pieces), block, tile, heads),
        out_shape=(pltpu.VMEM((rows, width), jnp.float32), tokens, kv_shape),
        in_specs=[VMEM] * (6 + len(pieces)),
        out_specs=(VMEM, VMEM, VMEM),
        scratch_shapes=[
            pltpu.VMEM((heads * count, width), jnp.bfloat16),
            pltpu.VMEM((heads * count, width), jnp.bfloat16),
        ],
        compiler_params=params,
        name="cross",
    )(scales, live, x, qc, *pieces, packed, wvt)
    other = swap(kv, "col")
    block = min(256, rows)
    late = (self_wo, ffn_up, ffn_down, box_w1, box_w2, jnp.transpose(box_w3))
    part = width // heads + 16
    return pl.pallas_call(
        functools.partial(self_kernel, block, heads),
        out_shape=(
            jax.ShapeDtypeStruct((rows, width), jnp.float32),
            jax.ShapeDtypeStruct((box_w3.shape[1], rows), jnp.float32),
        ),
        in_specs=[VMEM] * 6 + [HBM] * len(late),
        out_specs=(HBM, VMEM),
        scratch_shapes=[
            pltpu.VMEM((2, heads * part, rows), jnp.bfloat16),
            pltpu.VMEM((width, rows), jnp.bfloat16),
            pltpu.VMEM((rows, width), jnp.float32),
        ]
        + [pltpu.VMEM(w.shape, w.dtype) for w in late]
        + [pltpu.SemaphoreType.DMA((len(late) + 1,))],
        compiler_params=params,
        name="self",
    )(scales, live, x1, q, kv, other, *map(in_hbm, late))


def solution(mesh):
    return jax.shard_map(
        local,
        mesh=mesh,
        in_specs=(
            P(("parts", "row", "col"), None),
            P(("parts", "row", "col")),
            P(("parts", "row", "col"), None),
            P(("parts", "row", "col")),
            P(),
            P(),
            P(),
            P(),
            P(),
            P(),
            P(),
            P(),
            P(),
            P(),
            P(),
            P(),
        ),
        out_specs=(P(("parts", "row", "col"), None), P(None, ("parts", "row", "col"))),
        check_vma=False,
    )
```

```python
import functools
import math

import jax
import jax.numpy as jnp
from jax import lax
from jax.experimental import pallas as pl
from jax.experimental.pallas import tpu as pltpu
from jax.sharding import PartitionSpec as P

EPS = 1e-06
DEAD = 64.0
DEAD_V = 4096.0
LOG2E = math.log2(math.e)
VMEM = pl.BlockSpec(memory_space=pltpu.VMEM)
SMEM = pl.BlockSpec(memory_space=pltpu.SMEM)
HBM = pl.BlockSpec(memory_space=pltpu.HBM)


def rms_round(x):
    return (x * lax.rsqrt(jnp.mean(x * x, axis=-1, keepdims=True) + EPS)).astype(jnp.bfloat16)


def dot(a, b):
    return jnp.dot(a, b, preferred_element_type=jnp.float32)


def dot_t(a, b):
    return lax.dot_general(a, b, (((1,), (1,)), ((), ())), preferred_element_type=jnp.float32)


def head_of_lane(rows, width, heads):
    return lax.broadcasted_iota(jnp.int32, (rows, width), 1) // (width // heads)


def only(x, head, lane_head):
    return jnp.where(lane_head == head, x, jnp.zeros_like(x))


def flagged(values, flags, head, heads, lane_head):
    other = (head + heads // 2) % heads
    rest = jnp.where(lane_head == other, flags, jnp.zeros_like(values))
    return jnp.where(lane_head == head, values, rest)


def weigh(scores, top, scale):
    return jnp.exp2(((scores - top) * scale).astype(jnp.bfloat16))


def normed(low, high):
    half = low.shape[1] // 2
    return jnp.concatenate(
        [low[:, :half] / low[:, half:], high[:, half:] / high[:, :half]], axis=1
    ).astype(jnp.bfloat16)


def mark_kernel(memory, mask, out, held, flags, sems):
    copies = [
        pltpu.make_async_copy(memory, held, sems.at[0]),
        pltpu.make_async_copy(mask, flags, sems.at[1]),
    ]
    for copy in copies:
        copy.start()
    for copy in copies:
        copy.wait()
    row = lax.broadcasted_iota(jnp.int32, held.shape, 0)
    tokens = held[...].astype(jnp.float32)
    for j in range(held.shape[0]):
        tokens = jnp.where((row == j) & (flags[j] <= 0), DEAD, tokens)
    tokens = tokens.astype(jnp.bfloat16)
    for copy in range(out.shape[0]):
        out[copy] = tokens


def load_kernel(
    counts,
    queries,
    wq,
    cross_temp,
    self_temp,
    wkv,
    wo,
    wqkv,
    x_ref,
    qc_ref,
    scale_ref,
    count_ref,
    packed,
    wvt_ref,
    wqt_ref,
    wq_held,
    cross_held,
    self_held,
    sems,
):
    width = x_ref.shape[1]
    pairs = [(queries, x_ref), (wq, wq_held), (cross_temp, cross_held), (self_temp, self_held)]
    begin = 0
    for source in (wkv, wo, wqkv):
        end = begin + source.shape[1]
        pairs.append((source, packed.at[:, begin:end]))
        begin = end
    copies = [pltpu.make_async_copy(a, b, sems.at[i]) for i, (a, b) in enumerate(pairs)]
    for copy in copies:
        copy.start()
    for copy in copies[:4]:
        copy.wait()
    heads = cross_temp.shape[0]
    factor = LOG2E / math.sqrt(width // heads)
    lanes = scale_ref.shape[1]
    for side, temp in enumerate((cross_held, self_held)):
        for head in range(heads):
            at = pl.ds(side * heads + head, 1)
            scale_ref[at, :] = jnp.full((1, lanes), temp[head] * factor, jnp.float32)
    count_ref[...] = jnp.full(count_ref.shape, counts[0], jnp.int32)
    x = x_ref[...].astype(jnp.float32)
    qc_ref[...] = dot(rms_round(x), wq_held[...]).astype(jnp.bfloat16)
    for copy in copies[4:]:
        copy.wait()
    wvt_ref[...] = jnp.transpose(packed[:, -width:])
    wqt_ref[...] = jnp.transpose(packed[:, -3 * width : -2 * width])


def cross_kernel(n, block, tile, heads, scales, counts, queries, qc, *refs):
    pieces = refs[:n]
    packed, wvt, x1_ref, hn_ref, kv_ref, kbd, vbd = refs[n:]
    rows, width = queries.shape
    wkv = packed[:, : 2 * width]
    wo = packed[:, 2 * width : 3 * width]
    wk = packed[:, 4 * width : 5 * width]
    tokens, flags = [], []
    for piece in pieces:
        held = piece[...].astype(jnp.float32)
        dead = held >= DEAD
        for begin in range(0, held.shape[0], tile):
            part = held[begin : begin + tile]
            gone = dead[begin : begin + tile]
            tokens.append(jnp.where(gone, part[:1], part).astype(jnp.bfloat16))
            flags.append(jnp.where(gone, 0.0, 1.0).astype(jnp.bfloat16))
    tokens = jnp.concatenate(tokens, axis=0)
    flags = jnp.concatenate(flags, axis=0)
    count = tokens.shape[0]
    kvm = dot(tokens, wkv).astype(jnp.bfloat16)
    keys = kvm[:, :width]
    values = kvm[:, width:] * flags
    lane_head = head_of_lane(count, width, heads)
    for head in range(heads):
        at = pl.ds(head * count, count)
        kbd[at, :] = only(keys, head, lane_head)
        vbd[at, :] = flagged(values, flags, head, heads, lane_head)
    middle = heads // 2 * count
    for begin in range(0, rows, block):
        at = pl.ds(begin, block)
        x = queries[at, :].astype(jnp.float32)
        scores = dot_t(qc[at, :], kbd[...])
        weights = []
        for head in range(heads):
            s = scores[:, head * count : (head + 1) * count]
            top = jnp.max(s, axis=-1, keepdims=True)
            weights.append(weigh(s, top, scales[head : head + 1, :1]))
        low = dot(jnp.concatenate(weights[: heads // 2], axis=1), vbd[:middle, :])
        high = dot(jnp.concatenate(weights[heads // 2 :], axis=1), vbd[middle:, :])
        x1 = x + dot(normed(low, high), wo)
        x1_ref[at, :] = x1
        hn1 = rms_round(x1)
        hn_ref[at, :] = hn1
        key = dot(hn1, wk).astype(jnp.bfloat16)
        slot = lax.broadcasted_iota(jnp.int32, (block, width), 0) + begin
        if begin == 0:
            first = key[:1]
        kv_ref[at, :] = jnp.where(slot < counts[:1, :1], key, first)
        value = dot_t(wvt[...], hn1).astype(jnp.bfloat16)
        slot = lax.broadcasted_iota(jnp.int32, (width, block), 1) + begin
        value = jnp.where(slot < counts[:1, :1], value, jnp.bfloat16(DEAD_V))
        for part in range(0, block, width):
            place = begin + part
            size = min(block, width)
            target = pl.ds(rows + place // width * width, width)
            lanes = pl.ds(place % width, size)
            kv_ref[target, lanes] = value[:, part : part + size]


def transposed_values(kv, vt, heads):
    rows, width = vt.shape[1], kv.shape[1]
    hsize, part = width // heads, vt.shape[0] // heads
    for begin in range(0, rows, width):
        lanes = pl.ds(begin, width)
        values = kv[rows + begin : rows + begin + width, :]
        live = values < jnp.bfloat16(DEAD_V)
        flags = jnp.where(live[: part - hsize], jnp.bfloat16(1), jnp.bfloat16(0))
        values = jnp.where(live, values, jnp.bfloat16(0))
        for head in range(heads):
            at = head * part
            vt[at : at + hsize, lanes] = values[head * hsize : (head + 1) * hsize]
            vt[at + hsize : at + part, lanes] = flags


def half_attention(scales, qt, kv, vt, heads, use):
    rows, width = vt.shape[1], kv.shape[1]
    part = vt.shape[0] // heads
    depth = qt.shape[0] // heads
    per = heads * depth // width

    def scores(head):
        lanes = head // per * depth
        return dot(kv[:rows, lanes : lanes + depth], qt[head * depth : (head + 1) * depth, :])

    ahead = scores(0)
    for head in range(heads):
        s = ahead
        if head + 1 < heads:
            ahead = scores(head + 1)
        top = jnp.max(s, axis=0, keepdims=True)
        scale = scales[heads + head : heads + head + 1, :1]
        use(head, top, dot(vt[head * part : (head + 1) * part, :], weigh(s, top, scale)))


def own_kernel(heads, scales, hn, kv, wqt, qt, top_ref, sum_ref, vt):
    width = hn.shape[1]
    hsize = width // heads
    depth = qt.shape[0] // heads
    part = vt.shape[0] // heads
    q = dot_t(wqt[...], hn[...]).astype(jnp.bfloat16)
    qt[...] = jnp.zeros_like(qt)
    for head in range(heads):
        begin = head * hsize
        at = head * depth + begin % depth
        qt[at : at + hsize, :] = q[begin : begin + hsize]
    transposed_values(kv, vt, heads)

    def use(head, top, total):
        top_ref[head : head + 1, :] = top
        sum_ref[head * part : (head + 1) * part, :] = total

    half_attention(scales, qt, kv, vt, heads, use)


def rest_kernel(
    heads,
    scales,
    counts,
    x1_ref,
    kv,
    qt,
    top_ref,
    sum_ref,
    wo,
    up,
    down,
    w1,
    w2,
    w3,
    features,
    boxes,
    vt,
    ctx,
    out,
    wo_held,
    up_held,
    down_held,
    w1_held,
    w2_held,
    w3_held,
    sems,
):
    rows, width = x1_ref.shape
    hsize = width // heads
    part = vt.shape[0] // heads
    held = (wo_held, up_held, down_held, w1_held, w2_held, w3_held)
    pairs = zip((wo, up, down, w1, w2, w3), held)
    copies = [pltpu.make_async_copy(a, b, sems.at[i]) for i, (a, b) in enumerate(pairs)]
    for copy in copies:
        copy.start()
    transposed_values(kv, vt, heads)

    def use(head, top, total):
        scale = scales[heads + head : heads + head + 1, :1]
        first = top_ref[head : head + 1, :]
        most = jnp.maximum(first, top)
        total = total * jnp.exp2((top - most) * scale)
        total += sum_ref[head * part : (head + 1) * part, :] * jnp.exp2((first - most) * scale)
        mixed = total[:hsize] / total[hsize : hsize + 1]
        ctx[head * hsize : (head + 1) * hsize, :] = mixed.astype(jnp.bfloat16)

    half_attention(scales, qt, kv, vt, heads, use)
    for copy in copies:
        copy.wait()
    mixed = lax.dot_general(
        ctx[...], wo_held[...], (((0,), (0,)), ((), ())), preferred_element_type=jnp.float32
    )
    x2 = x1_ref[...] + mixed
    upper = jnp.maximum(dot(rms_round(x2), up_held[...]), 0.0).astype(jnp.bfloat16)
    x3 = x2 + dot(upper, down_held[...])
    slot = lax.broadcasted_iota(jnp.int32, (rows, width), 0)
    out[...] = jnp.where(slot < counts[:1, :1], x3, 0.0)
    leave = pltpu.make_async_copy(out, features, sems.at[len(copies)])
    leave.start()
    b1 = jnp.maximum(dot(rms_round(x3), w1_held[...]), 0.0).astype(jnp.bfloat16)
    b2 = jnp.maximum(dot(b1, w2_held[...]), 0.0).astype(jnp.bfloat16)
    raw = dot_t(w3_held[...], b2)
    slot = lax.broadcasted_iota(jnp.int32, raw.shape, 1)
    boxes[...] = jnp.where(slot < counts[:1, :1], 1.0 / (1.0 + jnp.exp(-raw)), 0.0)
    leave.wait()


def in_hbm(x):
    return pltpu.with_memory_space_constraint(x, pltpu.HBM)


def swap(x, axis):
    size = lax.axis_size(axis)
    return lax.ppermute(x, axis, [(i, i ^ 1) for i in range(size)])


def local(
    queries,
    counts,
    memory,
    mem_mask,
    cross_wq,
    cross_wkv,
    cross_wo,
    self_wqkv,
    self_wo,
    ffn_up,
    ffn_down,
    box_w1,
    box_w2,
    box_w3,
    cross_temp,
    self_temp,
):
    rows, width = queries.shape
    heads = cross_temp.shape[0]
    tile = memory.shape[0]
    params = pltpu.CompilerParams(vmem_limit_bytes=32 * 2**20)
    marked = pl.pallas_call(
        mark_kernel,
        out_shape=pltpu.VMEM((lax.axis_size("row"), tile, width), memory.dtype),
        in_specs=[HBM, HBM],
        out_specs=VMEM,
        scratch_shapes=[
            pltpu.VMEM(memory.shape, memory.dtype),
            pltpu.SMEM(mem_mask.shape, mem_mask.dtype),
            pltpu.SemaphoreType.DMA((2,)),
        ],
        name="mark",
    )(in_hbm(memory), in_hbm(mem_mask))
    gathered = lax.all_to_all(marked, "row", 0, 0, tiled=True)
    pieces = [gathered.reshape(-1, width)]
    tokens = pltpu.VMEM((rows, width), jnp.bfloat16)
    packed_width = cross_wkv.shape[1] + cross_wo.shape[1] + self_wqkv.shape[1]
    sources = (queries, cross_wq, cross_temp, self_temp, cross_wkv, cross_wo, self_wqkv)
    x, qc, scales, live, packed, wvt, wqt = pl.pallas_call(
        load_kernel,
        out_shape=[
            tokens,
            tokens,
            pltpu.VMEM((2 * heads, 128), jnp.float32),
            pltpu.VMEM((8, 128), jnp.int32),
            pltpu.VMEM((width, packed_width), jnp.bfloat16),
            pltpu.VMEM((width, width), jnp.bfloat16),
            pltpu.VMEM((width, width), jnp.bfloat16),
        ],
        in_specs=[SMEM] + [HBM] * len(sources),
        out_specs=[VMEM] * 7,
        scratch_shapes=[
            pltpu.VMEM(cross_wq.shape, cross_wq.dtype),
            pltpu.SMEM(cross_temp.shape, cross_temp.dtype),
            pltpu.SMEM(self_temp.shape, self_temp.dtype),
            pltpu.SemaphoreType.DMA((len(sources),)),
        ],
        compiler_params=params,
        cost_estimate=pl.CostEstimate(
            flops=2 * rows * width * width, bytes_accessed=4 * 2**20, transcendentals=0
        ),
        name="load",
    )(counts, *map(in_hbm, sources))
    count = sum(piece.shape[0] for piece in pieces)
    block = rows if count <= 128 else min(rows, 128)
    kv_shape = pltpu.VMEM((2 * rows, width), jnp.bfloat16)
    x1, hn, kv = pl.pallas_call(
        functools.partial(cross_kernel, len(pieces), block, tile, heads),
        out_shape=(pltpu.VMEM((rows, width), jnp.float32), tokens, kv_shape),
        in_specs=[VMEM] * (6 + len(pieces)),
        out_specs=(VMEM, VMEM, VMEM),
        scratch_shapes=[
            pltpu.VMEM((heads * count, width), jnp.bfloat16),
            pltpu.VMEM((heads * count, width), jnp.bfloat16),
        ],
        compiler_params=params,
        name="cross",
    )(scales, live, x, qc, *pieces, packed, wvt)
    other = swap(kv, "col")
    part = width // heads + 16
    depth = min(128, width)
    qt, tops, sums = pl.pallas_call(
        functools.partial(own_kernel, heads),
        out_shape=(
            pltpu.VMEM((heads * depth, rows), jnp.bfloat16),
            pltpu.VMEM((heads, rows), jnp.float32),
            pltpu.VMEM((heads * part, rows), jnp.float32),
        ),
        in_specs=[VMEM] * 4,
        out_specs=(VMEM, VMEM, VMEM),
        scratch_shapes=[pltpu.VMEM((heads * part, rows), jnp.bfloat16)],
        compiler_params=params,
        cost_estimate=pl.CostEstimate(
            flops=8 * heads * rows * rows * width, bytes_accessed=2**20, transcendentals=0
        ),
        name="own",
    )(scales, hn, kv, wqt)
    late = (self_wo, ffn_up, ffn_down, box_w1, box_w2, jnp.transpose(box_w3))
    return pl.pallas_call(
        functools.partial(rest_kernel, heads),
        out_shape=(
            jax.ShapeDtypeStruct((rows, width), jnp.float32),
            jax.ShapeDtypeStruct((box_w3.shape[1], rows), jnp.float32),
        ),
        in_specs=[VMEM] * 7 + [HBM] * len(late),
        out_specs=(HBM, VMEM),
        scratch_shapes=[
            pltpu.VMEM((heads * part, rows), jnp.bfloat16),
            pltpu.VMEM((width, rows), jnp.bfloat16),
            pltpu.VMEM((rows, width), jnp.float32),
        ]
        + [pltpu.VMEM(w.shape, w.dtype) for w in late]
        + [pltpu.SemaphoreType.DMA((len(late) + 1,))],
        compiler_params=params,
        name="rest",
    )(scales, live, x1, other, qt, tops, sums, *map(in_hbm, late))


def solution(mesh):
    return jax.shard_map(
        local,
        mesh=mesh,
        in_specs=(
            P(("parts", "row", "col"), None),
            P(("parts", "row", "col")),
            P(("parts", "row", "col"), None),
            P(("parts", "row", "col")),
            P(),
            P(),
            P(),
            P(),
            P(),
            P(),
            P(),
            P(),
            P(),
            P(),
            P(),
            P(),
        ),
        out_specs=(P(("parts", "row", "col"), None), P(None, ("parts", "row", "col"))),
        check_vma=False,
    )
```

```python
import functools
import math

import jax
import jax.numpy as jnp
from jax import lax
from jax.experimental import pallas as pl
from jax.experimental.pallas import tpu as pltpu
from jax.sharding import PartitionSpec as P

EPS = 1e-06
DEAD = 64.0
DEAD_V = 4096.0
LOG2E = math.log2(math.e)
VMEM = pl.BlockSpec(memory_space=pltpu.VMEM)
SMEM = pl.BlockSpec(memory_space=pltpu.SMEM)
HBM = pl.BlockSpec(memory_space=pltpu.HBM)


def rms_round(x):
    return (x * lax.rsqrt(jnp.mean(x * x, axis=-1, keepdims=True) + EPS)).astype(jnp.bfloat16)


def dot(a, b):
    return jnp.dot(a, b, preferred_element_type=jnp.float32)


def dot_t(a, b):
    return lax.dot_general(a, b, (((1,), (1,)), ((), ())), preferred_element_type=jnp.float32)


def head_of_lane(rows, width, heads):
    return lax.broadcasted_iota(jnp.int32, (rows, width), 1) // (width // heads)


def only(x, head, lane_head):
    return jnp.where(lane_head == head, x, jnp.zeros_like(x))


def flagged(values, flags, head, heads, lane_head):
    other = (head + heads // 2) % heads
    rest = jnp.where(lane_head == other, flags, jnp.zeros_like(values))
    return jnp.where(lane_head == head, values, rest)


def weigh(scores, top, scale):
    return jnp.exp2(((scores - top) * scale).astype(jnp.bfloat16))


def normed(low, high):
    half = low.shape[1] // 2
    return jnp.concatenate(
        [low[:, :half] / low[:, half:], high[:, half:] / high[:, :half]], axis=1
    ).astype(jnp.bfloat16)


def mark_kernel(memory, mask, out, held, flags, sems):
    copies = [
        pltpu.make_async_copy(memory, held, sems.at[0]),
        pltpu.make_async_copy(mask, flags, sems.at[1]),
    ]
    for copy in copies:
        copy.start()
    for copy in copies:
        copy.wait()
    row = lax.broadcasted_iota(jnp.int32, held.shape, 0)
    tokens = held[...].astype(jnp.float32)
    for j in range(held.shape[0]):
        tokens = jnp.where((row == j) & (flags[j] <= 0), DEAD, tokens)
    tokens = tokens.astype(jnp.bfloat16)
    for copy in range(out.shape[0]):
        out[copy] = tokens


def load_kernel(
    counts,
    queries,
    wq,
    cross_temp,
    self_temp,
    wkv,
    wo,
    wqkv,
    x_ref,
    qc_ref,
    scale_ref,
    count_ref,
    packed,
    wvt_ref,
    wqt_ref,
    wq_held,
    cross_held,
    self_held,
    sems,
):
    width = x_ref.shape[1]
    pairs = [(queries, x_ref), (wq, wq_held), (cross_temp, cross_held), (self_temp, self_held)]
    begin = 0
    for source in (wkv, wo, wqkv):
        end = begin + source.shape[1]
        pairs.append((source, packed.at[:, begin:end]))
        begin = end
    copies = [pltpu.make_async_copy(a, b, sems.at[i]) for i, (a, b) in enumerate(pairs)]
    for copy in copies:
        copy.start()
    for copy in copies[:4]:
        copy.wait()
    heads = cross_temp.shape[0]
    factor = LOG2E / math.sqrt(width // heads)
    lanes = scale_ref.shape[1]
    for side, temp in enumerate((cross_held, self_held)):
        for head in range(heads):
            at = pl.ds(side * heads + head, 1)
            scale_ref[at, :] = jnp.full((1, lanes), temp[head] * factor, jnp.float32)
    count_ref[...] = jnp.full(count_ref.shape, counts[0], jnp.int32)
    x = x_ref[...].astype(jnp.float32)
    qc_ref[...] = dot(rms_round(x), wq_held[...]).astype(jnp.bfloat16)
    for copy in copies[4:]:
        copy.wait()
    wvt_ref[...] = jnp.transpose(packed[:, -width:])
    wqt_ref[...] = jnp.transpose(packed[:, -3 * width : -2 * width])


def cross_kernel(n, block, tile, heads, scales, counts, queries, qc, *refs):
    pieces = refs[:n]
    packed, wvt, x1_ref, hn_ref, kv_ref, kbd, vbd = refs[n:]
    rows, width = queries.shape
    wkv = packed[:, : 2 * width]
    wo = packed[:, 2 * width : 3 * width]
    wk = packed[:, 4 * width : 5 * width]
    tokens, flags = [], []
    for piece in pieces:
        held = piece[...].astype(jnp.float32)
        dead = held >= DEAD
        for begin in range(0, held.shape[0], tile):
            part = held[begin : begin + tile]
            gone = dead[begin : begin + tile]
            tokens.append(jnp.where(gone, part[:1], part).astype(jnp.bfloat16))
            flags.append(jnp.where(gone, 0.0, 1.0).astype(jnp.bfloat16))
    tokens = jnp.concatenate(tokens, axis=0)
    flags = jnp.concatenate(flags, axis=0)
    count = tokens.shape[0]
    kvm = dot(tokens, wkv).astype(jnp.bfloat16)
    keys = kvm[:, :width]
    values = kvm[:, width:] * flags
    lane_head = head_of_lane(count, width, heads)
    for head in range(heads):
        at = pl.ds(head * count, count)
        kbd[at, :] = only(keys, head, lane_head)
        vbd[at, :] = flagged(values, flags, head, heads, lane_head)
    middle = heads // 2 * count
    for begin in range(0, rows, block):
        at = pl.ds(begin, block)
        x = queries[at, :].astype(jnp.float32)
        scores = dot_t(qc[at, :], kbd[...])
        weights = []
        for head in range(heads):
            s = scores[:, head * count : (head + 1) * count]
            top = jnp.max(s, axis=-1, keepdims=True)
            weights.append(weigh(s, top, scales[head : head + 1, :1]))
        low = dot(jnp.concatenate(weights[: heads // 2], axis=1), vbd[:middle, :])
        high = dot(jnp.concatenate(weights[heads // 2 :], axis=1), vbd[middle:, :])
        x1 = x + dot(normed(low, high), wo)
        x1_ref[at, :] = x1
        hn1 = rms_round(x1)
        hn_ref[at, :] = hn1
        key = dot(hn1, wk).astype(jnp.bfloat16)
        slot = lax.broadcasted_iota(jnp.int32, (block, width), 0) + begin
        if begin == 0:
            first = key[:1]
        kv_ref[at, :] = jnp.where(slot < counts[:1, :1], key, first)
        value = dot_t(wvt[...], hn1).astype(jnp.bfloat16)
        slot = lax.broadcasted_iota(jnp.int32, (width, block), 1) + begin
        value = jnp.where(slot < counts[:1, :1], value, jnp.bfloat16(DEAD_V))
        for part in range(0, block, width):
            place = begin + part
            size = min(block, width)
            target = pl.ds(rows + place // width * width, width)
            lanes = pl.ds(place % width, size)
            kv_ref[target, lanes] = value[:, part : part + size]


def transposed_values(kv, vt, heads):
    rows, width = vt.shape[1], kv.shape[1]
    hsize, part = width // heads, vt.shape[0] // heads
    for begin in range(0, rows, width):
        lanes = pl.ds(begin, width)
        values = kv[rows + begin : rows + begin + width, :]
        live = values < jnp.bfloat16(DEAD_V)
        flags = jnp.where(live[: part - hsize], jnp.bfloat16(1), jnp.bfloat16(0))
        values = jnp.where(live, values, jnp.bfloat16(0))
        for head in range(heads):
            at = head * part
            vt[at : at + hsize, lanes] = values[head * hsize : (head + 1) * hsize]
            vt[at + hsize : at + part, lanes] = flags


def half_attention(scales, qt, kv, vt, heads, s_held, p_held, use):
    rows, width = vt.shape[1], kv.shape[1]
    part = vt.shape[0] // heads
    depth = qt.shape[0] // heads
    per = heads * depth // width
    block = s_held.shape[2]
    units = [(head, begin) for head in range(heads) for begin in range(0, rows, block)]
    tops = {}

    def score(unit):
        head, begin = units[unit]
        lanes = head // per * depth
        q = qt[head * depth : (head + 1) * depth, begin : begin + block]
        s = dot(kv[:rows, lanes : lanes + depth], q)
        s_held[unit % 2] = s
        tops[unit] = jnp.max(s, axis=0, keepdims=True)

    def soften(unit):
        head, begin = units[unit]
        scale = scales[heads + head : heads + head + 1, :1]
        p_held[unit % 2] = weigh(s_held[unit % 2], tops[unit], scale)

    def mix(unit):
        head, begin = units[unit]
        total = dot(vt[head * part : (head + 1) * part, :], p_held[unit % 2])
        use(head, pl.ds(begin, block), tops[unit], total)

    for step in range(len(units) + 2):
        if step < len(units):
            score(step)
        if 0 <= step - 1 < len(units):
            soften(step - 1)
        if 0 <= step - 2:
            mix(step - 2)


def own_kernel(heads, scales, hn, kv, wqt, qt, top_ref, sum_ref, vt, s_held, p_held):
    width = hn.shape[1]
    hsize = width // heads
    depth = qt.shape[0] // heads
    part = vt.shape[0] // heads
    q = dot_t(wqt[...], hn[...]).astype(jnp.bfloat16)
    qt[...] = jnp.zeros_like(qt)
    for head in range(heads):
        begin = head * hsize
        at = head * depth + begin % depth
        qt[at : at + hsize, :] = q[begin : begin + hsize]
    transposed_values(kv, vt, heads)

    def use(head, at, top, total):
        top_ref[head : head + 1, at] = top
        sum_ref[head * part : (head + 1) * part, at] = total

    half_attention(scales, qt, kv, vt, heads, s_held, p_held, use)


def rest_kernel(
    heads,
    scales,
    counts,
    x1_ref,
    kv,
    qt,
    top_ref,
    sum_ref,
    wo,
    up,
    down,
    w1,
    w2,
    w3,
    features,
    boxes,
    vt,
    s_held,
    p_held,
    ctx,
    out,
    upper,
    wo_held,
    up_held,
    down_held,
    w1_held,
    w2_held,
    w3_held,
    sems,
):
    rows, width = x1_ref.shape
    hsize = width // heads
    part = vt.shape[0] // heads
    held = (wo_held, up_held, down_held, w1_held, w2_held, w3_held)
    pairs = zip((wo, up, down, w1, w2, w3), held)
    copies = [pltpu.make_async_copy(a, b, sems.at[i]) for i, (a, b) in enumerate(pairs)]
    for copy in copies:
        copy.start()
    transposed_values(kv, vt, heads)

    def use(head, at, top, total):
        scale = scales[heads + head : heads + head + 1, :1]
        first = top_ref[head : head + 1, at]
        most = jnp.maximum(first, top)
        total = total * jnp.exp2((top - most) * scale)
        total += sum_ref[head * part : (head + 1) * part, at] * jnp.exp2((first - most) * scale)
        mixed = total[:hsize] / total[hsize : hsize + 1]
        ctx[head * hsize : (head + 1) * hsize, at] = mixed.astype(jnp.bfloat16)

    half_attention(scales, qt, kv, vt, heads, s_held, p_held, use)
    for copy in copies:
        copy.wait()
    block = upper.shape[1]
    starts = list(range(0, rows, block))
    ff = up_held.shape[1]
    chunk = ff // 4
    x2, x3, leaves = {}, {}, []

    def project(i):
        at = pl.ds(starts[i], block)
        mixed = lax.dot_general(
            ctx[:, at], wo_held[...], (((0,), (0,)), ((), ())), preferred_element_type=jnp.float32
        )
        x2[i] = x1_ref[at, :] + mixed

    def widen(i):
        hn2 = rms_round(x2[i])
        for begin in range(0, ff, chunk):
            cut = pl.ds(begin, chunk)
            upper[i % 2, :, cut] = jnp.maximum(dot(hn2, up_held[:, cut]), 0.0).astype(jnp.bfloat16)

    def narrow(i):
        at = pl.ds(starts[i], block)
        x3[i] = x2[i] + dot(upper[i % 2], down_held[...])
        slot = lax.broadcasted_iota(jnp.int32, (block, width), 0) + starts[i]
        out[at, :] = jnp.where(slot < counts[:1, :1], x3[i], 0.0)
        leaves.append(
            pltpu.make_async_copy(out.at[at, :], features.at[at, :], sems.at[len(copies) + i])
        )
        leaves[-1].start()

    def box(i):
        b1 = jnp.maximum(dot(rms_round(x3[i]), w1_held[...]), 0.0).astype(jnp.bfloat16)
        b2 = jnp.maximum(dot(b1, w2_held[...]), 0.0).astype(jnp.bfloat16)
        raw = dot_t(w3_held[...], b2)
        slot = lax.broadcasted_iota(jnp.int32, raw.shape, 1) + starts[i]
        boxes[:, pl.ds(starts[i], block)] = jnp.where(
            slot < counts[:1, :1], 1.0 / (1.0 + jnp.exp(-raw)), 0.0
        )

    for step in range(len(starts) + 3):
        for stage, work in enumerate((project, widen, narrow, box)):
            if 0 <= step - stage < len(starts):
                work(step - stage)
    for leave in leaves:
        leave.wait()


def in_hbm(x):
    return pltpu.with_memory_space_constraint(x, pltpu.HBM)


def swap(x, axis):
    size = lax.axis_size(axis)
    return lax.ppermute(x, axis, [(i, i ^ 1) for i in range(size)])


def local(
    queries,
    counts,
    memory,
    mem_mask,
    cross_wq,
    cross_wkv,
    cross_wo,
    self_wqkv,
    self_wo,
    ffn_up,
    ffn_down,
    box_w1,
    box_w2,
    box_w3,
    cross_temp,
    self_temp,
):
    rows, width = queries.shape
    heads = cross_temp.shape[0]
    tile = memory.shape[0]
    params = pltpu.CompilerParams(vmem_limit_bytes=32 * 2**20)
    marked = pl.pallas_call(
        mark_kernel,
        out_shape=pltpu.VMEM((lax.axis_size("row"), tile, width), memory.dtype),
        in_specs=[HBM, HBM],
        out_specs=VMEM,
        scratch_shapes=[
            pltpu.VMEM(memory.shape, memory.dtype),
            pltpu.SMEM(mem_mask.shape, mem_mask.dtype),
            pltpu.SemaphoreType.DMA((2,)),
        ],
        name="mark",
    )(in_hbm(memory), in_hbm(mem_mask))
    gathered = lax.all_to_all(marked, "row", 0, 0, tiled=True)
    pieces = [gathered.reshape(-1, width)]
    tokens = pltpu.VMEM((rows, width), jnp.bfloat16)
    packed_width = cross_wkv.shape[1] + cross_wo.shape[1] + self_wqkv.shape[1]
    sources = (queries, cross_wq, cross_temp, self_temp, cross_wkv, cross_wo, self_wqkv)
    x, qc, scales, live, packed, wvt, wqt = pl.pallas_call(
        load_kernel,
        out_shape=[
            tokens,
            tokens,
            pltpu.VMEM((2 * heads, 128), jnp.float32),
            pltpu.VMEM((8, 128), jnp.int32),
            pltpu.VMEM((width, packed_width), jnp.bfloat16),
            pltpu.VMEM((width, width), jnp.bfloat16),
            pltpu.VMEM((width, width), jnp.bfloat16),
        ],
        in_specs=[SMEM] + [HBM] * len(sources),
        out_specs=[VMEM] * 7,
        scratch_shapes=[
            pltpu.VMEM(cross_wq.shape, cross_wq.dtype),
            pltpu.SMEM(cross_temp.shape, cross_temp.dtype),
            pltpu.SMEM(self_temp.shape, self_temp.dtype),
            pltpu.SemaphoreType.DMA((len(sources),)),
        ],
        compiler_params=params,
        cost_estimate=pl.CostEstimate(
            flops=2 * rows * width * width, bytes_accessed=4 * 2**20, transcendentals=0
        ),
        name="load",
    )(counts, *map(in_hbm, sources))
    count = sum(piece.shape[0] for piece in pieces)
    block = rows if count <= 128 else min(rows, 128)
    kv_shape = pltpu.VMEM((2 * rows, width), jnp.bfloat16)
    x1, hn, kv = pl.pallas_call(
        functools.partial(cross_kernel, len(pieces), block, tile, heads),
        out_shape=(pltpu.VMEM((rows, width), jnp.float32), tokens, kv_shape),
        in_specs=[VMEM] * (6 + len(pieces)),
        out_specs=(VMEM, VMEM, VMEM),
        scratch_shapes=[
            pltpu.VMEM((heads * count, width), jnp.bfloat16),
            pltpu.VMEM((heads * count, width), jnp.bfloat16),
        ],
        compiler_params=params,
        name="cross",
    )(scales, live, x, qc, *pieces, packed, wvt)
    other = swap(kv, "col")
    part = width // heads + 16
    depth = min(128, width)
    block = min(256, rows)
    held = [
        pltpu.VMEM((heads * part, rows), jnp.bfloat16),
        pltpu.VMEM((2, rows, block), jnp.float32),
        pltpu.VMEM((2, rows, block), jnp.bfloat16),
    ]
    qt, tops, sums = pl.pallas_call(
        functools.partial(own_kernel, heads),
        out_shape=(
            pltpu.VMEM((heads * depth, rows), jnp.bfloat16),
            pltpu.VMEM((heads, rows), jnp.float32),
            pltpu.VMEM((heads * part, rows), jnp.float32),
        ),
        in_specs=[VMEM] * 4,
        out_specs=(VMEM, VMEM, VMEM),
        scratch_shapes=held,
        compiler_params=params,
        cost_estimate=pl.CostEstimate(
            flops=8 * heads * rows * rows * width, bytes_accessed=2**20, transcendentals=0
        ),
        name="own",
    )(scales, hn, kv, wqt)
    late = (self_wo, ffn_up, ffn_down, box_w1, box_w2, jnp.transpose(box_w3))
    return pl.pallas_call(
        functools.partial(rest_kernel, heads),
        out_shape=(
            jax.ShapeDtypeStruct((rows, width), jnp.float32),
            jax.ShapeDtypeStruct((box_w3.shape[1], rows), jnp.float32),
        ),
        in_specs=[VMEM] * 7 + [HBM] * len(late),
        out_specs=(HBM, VMEM),
        scratch_shapes=held
        + [
            pltpu.VMEM((width, rows), jnp.bfloat16),
            pltpu.VMEM((rows, width), jnp.float32),
            pltpu.VMEM((2, block, ffn_up.shape[1]), jnp.bfloat16),
        ]
        + [pltpu.VMEM(w.shape, w.dtype) for w in late]
        + [pltpu.SemaphoreType.DMA((len(late) + rows // block,))],
        compiler_params=params,
        name="rest",
    )(scales, live, x1, other, qt, tops, sums, *map(in_hbm, late))


def solution(mesh):
    return jax.shard_map(
        local,
        mesh=mesh,
        in_specs=(
            P(("parts", "row", "col"), None),
            P(("parts", "row", "col")),
            P(("parts", "row", "col"), None),
            P(("parts", "row", "col")),
            P(),
            P(),
            P(),
            P(),
            P(),
            P(),
            P(),
            P(),
            P(),
            P(),
            P(),
            P(),
        ),
        out_specs=(P(("parts", "row", "col"), None), P(None, ("parts", "row", "col"))),
        check_vma=False,
    )
```

```python
import functools
import math

import jax
import jax.numpy as jnp
from jax import lax
from jax.experimental import pallas as pl
from jax.experimental.pallas import tpu as pltpu
from jax.sharding import PartitionSpec as P

EPS = 1e-06
DEAD = 64.0
DEAD_V = 4096.0
LOG2E = math.log2(math.e)
VMEM = pl.BlockSpec(memory_space=pltpu.VMEM)
SMEM = pl.BlockSpec(memory_space=pltpu.SMEM)
HBM = pl.BlockSpec(memory_space=pltpu.HBM)


def rms_round(x):
    return (x * lax.rsqrt(jnp.mean(x * x, axis=-1, keepdims=True) + EPS)).astype(jnp.bfloat16)


def dot(a, b):
    return jnp.dot(a, b, preferred_element_type=jnp.float32)


def dot_t(a, b):
    return lax.dot_general(a, b, (((1,), (1,)), ((), ())), preferred_element_type=jnp.float32)


def head_of_lane(rows, width, heads):
    return lax.broadcasted_iota(jnp.int32, (rows, width), 1) // (width // heads)


def only(x, head, lane_head):
    return jnp.where(lane_head == head, x, jnp.zeros_like(x))


def flagged(values, flags, head, heads, lane_head):
    other = (head + heads // 2) % heads
    rest = jnp.where(lane_head == other, flags, jnp.zeros_like(values))
    return jnp.where(lane_head == head, values, rest)


def weigh(scores, top, scale):
    return jnp.exp2(((scores - top) * scale).astype(jnp.bfloat16))


def normed(low, high):
    half = low.shape[1] // 2
    return jnp.concatenate(
        [low[:, :half] / low[:, half:], high[:, half:] / high[:, :half]], axis=1
    ).astype(jnp.bfloat16)


def mark_kernel(memory, mask, out, held, flags, sems):
    copies = [
        pltpu.make_async_copy(memory, held, sems.at[0]),
        pltpu.make_async_copy(mask, flags, sems.at[1]),
    ]
    for copy in copies:
        copy.start()
    for copy in copies:
        copy.wait()
    row = lax.broadcasted_iota(jnp.int32, held.shape, 0)
    tokens = held[...].astype(jnp.float32)
    for j in range(held.shape[0]):
        tokens = jnp.where((row == j) & (flags[j] <= 0), DEAD, tokens)
    tokens = tokens.astype(jnp.bfloat16)
    for copy in range(out.shape[0]):
        out[copy] = tokens


def load_kernel(
    counts,
    queries,
    wq,
    cross_temp,
    self_temp,
    wkv,
    wo,
    wqkv,
    x_ref,
    qc_ref,
    scale_ref,
    count_ref,
    packed,
    wvt_ref,
    wqt_ref,
    wq_held,
    cross_held,
    self_held,
    sems,
):
    width = x_ref.shape[1]
    pairs = [(queries, x_ref), (wq, wq_held), (cross_temp, cross_held), (self_temp, self_held)]
    begin = 0
    for source in (wkv, wo, wqkv):
        end = begin + source.shape[1]
        pairs.append((source, packed.at[:, begin:end]))
        begin = end
    copies = [pltpu.make_async_copy(a, b, sems.at[i]) for i, (a, b) in enumerate(pairs)]
    for copy in copies:
        copy.start()
    for copy in copies[:4]:
        copy.wait()
    heads = cross_temp.shape[0]
    factor = LOG2E / math.sqrt(width // heads)
    lanes = scale_ref.shape[1]
    for side, temp in enumerate((cross_held, self_held)):
        for head in range(heads):
            at = pl.ds(side * heads + head, 1)
            scale_ref[at, :] = jnp.full((1, lanes), temp[head] * factor, jnp.float32)
    count_ref[...] = jnp.full(count_ref.shape, counts[0], jnp.int32)
    x = x_ref[...].astype(jnp.float32)
    qc_ref[...] = dot(rms_round(x), wq_held[...]).astype(jnp.bfloat16)
    for copy in copies[4:]:
        copy.wait()
    wvt_ref[...] = jnp.transpose(packed[:, -width:])
    wqt_ref[...] = jnp.transpose(packed[:, -3 * width : -2 * width])


def cross_kernel(n, block, tile, heads, scales, counts, queries, qc, *refs):
    pieces = refs[:n]
    packed, wvt, x1_ref, hn_ref, kv_ref, kbd, vbd = refs[n:]
    rows, width = queries.shape
    wkv = packed[:, : 2 * width]
    wo = packed[:, 2 * width : 3 * width]
    wk = packed[:, 4 * width : 5 * width]
    tokens, flags = [], []
    for piece in pieces:
        held = piece[...].astype(jnp.float32)
        dead = held >= DEAD
        for begin in range(0, held.shape[0], tile):
            part = held[begin : begin + tile]
            gone = dead[begin : begin + tile]
            tokens.append(jnp.where(gone, part[:1], part).astype(jnp.bfloat16))
            flags.append(jnp.where(gone, 0.0, 1.0).astype(jnp.bfloat16))
    tokens = jnp.concatenate(tokens, axis=0)
    flags = jnp.concatenate(flags, axis=0)
    count = tokens.shape[0]
    kvm = dot(tokens, wkv).astype(jnp.bfloat16)
    keys = kvm[:, :width]
    values = kvm[:, width:] * flags
    lane_head = head_of_lane(count, width, heads)
    for head in range(heads):
        at = pl.ds(head * count, count)
        kbd[at, :] = only(keys, head, lane_head)
        vbd[at, :] = flagged(values, flags, head, heads, lane_head)
    middle = heads // 2 * count
    for begin in range(0, rows, block):
        at = pl.ds(begin, block)
        x = queries[at, :].astype(jnp.float32)
        scores = dot_t(qc[at, :], kbd[...])
        weights = []
        for head in range(heads):
            s = scores[:, head * count : (head + 1) * count]
            top = jnp.max(s, axis=-1, keepdims=True)
            weights.append(weigh(s, top, scales[head : head + 1, :1]))
        low = dot(jnp.concatenate(weights[: heads // 2], axis=1), vbd[:middle, :])
        high = dot(jnp.concatenate(weights[heads // 2 :], axis=1), vbd[middle:, :])
        x1 = x + dot(normed(low, high), wo)
        x1_ref[at, :] = x1
        hn1 = rms_round(x1)
        hn_ref[at, :] = hn1
        key = dot(hn1, wk).astype(jnp.bfloat16)
        slot = lax.broadcasted_iota(jnp.int32, (block, width), 0) + begin
        if begin == 0:
            first = key[:1]
        kv_ref[at, :] = jnp.where(slot < counts[:1, :1], key, first)
        value = dot_t(wvt[...], hn1).astype(jnp.bfloat16)
        slot = lax.broadcasted_iota(jnp.int32, (width, block), 1) + begin
        value = jnp.where(slot < counts[:1, :1], value, jnp.bfloat16(DEAD_V))
        for part in range(0, block, width):
            place = begin + part
            size = min(block, width)
            target = pl.ds(rows + place // width * width, width)
            lanes = pl.ds(place % width, size)
            kv_ref[target, lanes] = value[:, part : part + size]


def transposed_values(kv, vt, heads):
    rows, width = vt.shape[1], kv.shape[1]
    hsize, part = width // heads, vt.shape[0] // heads
    for begin in range(0, rows, width):
        lanes = pl.ds(begin, width)
        values = kv[rows + begin : rows + begin + width, :]
        live = values < jnp.bfloat16(DEAD_V)
        flags = jnp.where(live[: part - hsize], jnp.bfloat16(1), jnp.bfloat16(0))
        values = jnp.where(live, values, jnp.bfloat16(0))
        for head in range(heads):
            at = head * part
            vt[at : at + hsize, lanes] = values[head * hsize : (head + 1) * hsize]
            vt[at + hsize : at + part, lanes] = flags


def half_attention(scales, qt, kv, vt, heads, s_held, p_held, top_held, use):
    rows, width = vt.shape[1], kv.shape[1]
    part = vt.shape[0] // heads
    depth = qt.shape[0] // heads
    per = heads * depth // width
    block = s_held.shape[2]
    blocks = rows // block
    units = heads * blocks

    def place(unit):
        head = unit // blocks
        begin = unit % blocks * block
        if not isinstance(unit, int):
            begin = pl.multiple_of(begin, block)
        return head, pl.ds(begin, block)

    def score(unit):
        head, at = place(unit)
        lanes = head // per * depth
        if not isinstance(unit, int):
            lanes = pl.multiple_of(lanes, depth)
        q = qt[pl.ds(head * depth, depth), at]
        s = dot(kv[:rows, pl.ds(lanes, depth)], q)
        s_held[unit % 2] = s
        top_held[unit % 4, :1] = jnp.max(s, axis=0, keepdims=True)

    def soften(unit):
        head, at = place(unit)
        scale = scales[pl.ds(heads + head, 1), :1]
        p_held[unit % 2] = weigh(s_held[unit % 2], top_held[unit % 4, :1], scale)

    def mix(unit):
        head, at = place(unit)
        total = dot(vt[pl.ds(head * part, part), :], p_held[unit % 2])
        use(head, at, top_held[unit % 4, :1], total)

    def step(unit, carry):
        score(unit)
        soften(unit - 1)
        mix(unit - 2)
        return carry

    score(0)
    score(1)
    soften(0)
    lax.fori_loop(2, units, step, 0)
    soften(units - 1)
    mix(units - 2)
    mix(units - 1)


def own_kernel(heads, scales, hn, kv, wqt, qt, top_ref, sum_ref, vt, s_held, p_held, top_held):
    width = hn.shape[1]
    hsize = width // heads
    depth = qt.shape[0] // heads
    part = vt.shape[0] // heads
    q = dot_t(wqt[...], hn[...]).astype(jnp.bfloat16)
    qt[...] = jnp.zeros_like(qt)
    for head in range(heads):
        begin = head * hsize
        at = head * depth + begin % depth
        qt[at : at + hsize, :] = q[begin : begin + hsize]
    transposed_values(kv, vt, heads)

    def use(head, at, top, total):
        top_ref[pl.ds(head, 1), at] = top
        sum_ref[pl.ds(head * part, part), at] = total

    half_attention(scales, qt, kv, vt, heads, s_held, p_held, top_held, use)


def rest_kernel(
    heads,
    scales,
    counts,
    x1_ref,
    kv,
    qt,
    top_ref,
    sum_ref,
    wo,
    up,
    down,
    w1,
    w2,
    w3,
    features,
    boxes,
    vt,
    s_held,
    p_held,
    top_held,
    ctx,
    out,
    upper,
    wo_held,
    up_held,
    down_held,
    w1_held,
    w2_held,
    w3_held,
    sems,
):
    rows, width = x1_ref.shape
    hsize = width // heads
    part = vt.shape[0] // heads
    held = (wo_held, up_held, down_held, w1_held, w2_held, w3_held)
    pairs = zip((wo, up, down, w1, w2, w3), held)
    copies = [pltpu.make_async_copy(a, b, sems.at[i]) for i, (a, b) in enumerate(pairs)]
    for copy in copies:
        copy.start()
    transposed_values(kv, vt, heads)

    def use(head, at, top, total):
        scale = scales[pl.ds(heads + head, 1), :1]
        first = top_ref[pl.ds(head, 1), at]
        most = jnp.maximum(first, top)
        total = total * jnp.exp2((top - most) * scale)
        total += sum_ref[pl.ds(head * part, part), at] * jnp.exp2((first - most) * scale)
        mixed = total[:hsize] / total[hsize : hsize + 1]
        ctx[pl.ds(head * hsize, hsize), at] = mixed.astype(jnp.bfloat16)

    half_attention(scales, qt, kv, vt, heads, s_held, p_held, top_held, use)
    for copy in copies:
        copy.wait()
    block = upper.shape[1]
    starts = list(range(0, rows, block))
    ff = up_held.shape[1]
    chunk = ff // 4
    x2, x3, leaves = {}, {}, []

    def project(i):
        at = pl.ds(starts[i], block)
        mixed = lax.dot_general(
            ctx[:, at], wo_held[...], (((0,), (0,)), ((), ())), preferred_element_type=jnp.float32
        )
        x2[i] = x1_ref[at, :] + mixed

    def widen(i):
        hn2 = rms_round(x2[i])
        for begin in range(0, ff, chunk):
            cut = pl.ds(begin, chunk)
            upper[i % 2, :, cut] = jnp.maximum(dot(hn2, up_held[:, cut]), 0.0).astype(jnp.bfloat16)

    def narrow(i):
        at = pl.ds(starts[i], block)
        x3[i] = x2[i] + dot(upper[i % 2], down_held[...])
        slot = lax.broadcasted_iota(jnp.int32, (block, width), 0) + starts[i]
        out[at, :] = jnp.where(slot < counts[:1, :1], x3[i], 0.0)
        leaves.append(
            pltpu.make_async_copy(out.at[at, :], features.at[at, :], sems.at[len(copies) + i])
        )
        leaves[-1].start()

    def box(i):
        b1 = jnp.maximum(dot(rms_round(x3[i]), w1_held[...]), 0.0).astype(jnp.bfloat16)
        b2 = jnp.maximum(dot(b1, w2_held[...]), 0.0).astype(jnp.bfloat16)
        raw = dot_t(w3_held[...], b2)
        slot = lax.broadcasted_iota(jnp.int32, raw.shape, 1) + starts[i]
        boxes[:, pl.ds(starts[i], block)] = jnp.where(
            slot < counts[:1, :1], 1.0 / (1.0 + jnp.exp(-raw)), 0.0
        )

    for step in range(len(starts) + 3):
        for stage, work in enumerate((project, widen, narrow, box)):
            if 0 <= step - stage < len(starts):
                work(step - stage)
    for leave in leaves:
        leave.wait()


def in_hbm(x):
    return pltpu.with_memory_space_constraint(x, pltpu.HBM)


def swap(x, axis):
    size = lax.axis_size(axis)
    return lax.ppermute(x, axis, [(i, i ^ 1) for i in range(size)])


def local(
    queries,
    counts,
    memory,
    mem_mask,
    cross_wq,
    cross_wkv,
    cross_wo,
    self_wqkv,
    self_wo,
    ffn_up,
    ffn_down,
    box_w1,
    box_w2,
    box_w3,
    cross_temp,
    self_temp,
):
    rows, width = queries.shape
    heads = cross_temp.shape[0]
    tile = memory.shape[0]
    params = pltpu.CompilerParams(vmem_limit_bytes=32 * 2**20)
    marked = pl.pallas_call(
        mark_kernel,
        out_shape=pltpu.VMEM((lax.axis_size("row"), tile, width), memory.dtype),
        in_specs=[HBM, HBM],
        out_specs=VMEM,
        scratch_shapes=[
            pltpu.VMEM(memory.shape, memory.dtype),
            pltpu.SMEM(mem_mask.shape, mem_mask.dtype),
            pltpu.SemaphoreType.DMA((2,)),
        ],
        name="mark",
    )(in_hbm(memory), in_hbm(mem_mask))
    gathered = lax.all_to_all(marked, "row", 0, 0, tiled=True)
    pieces = [gathered.reshape(-1, width)]
    tokens = pltpu.VMEM((rows, width), jnp.bfloat16)
    packed_width = cross_wkv.shape[1] + cross_wo.shape[1] + self_wqkv.shape[1]
    sources = (queries, cross_wq, cross_temp, self_temp, cross_wkv, cross_wo, self_wqkv)
    x, qc, scales, live, packed, wvt, wqt = pl.pallas_call(
        load_kernel,
        out_shape=[
            tokens,
            tokens,
            pltpu.VMEM((2 * heads, 128), jnp.float32),
            pltpu.VMEM((8, 128), jnp.int32),
            pltpu.VMEM((width, packed_width), jnp.bfloat16),
            pltpu.VMEM((width, width), jnp.bfloat16),
            pltpu.VMEM((width, width), jnp.bfloat16),
        ],
        in_specs=[SMEM] + [HBM] * len(sources),
        out_specs=[VMEM] * 7,
        scratch_shapes=[
            pltpu.VMEM(cross_wq.shape, cross_wq.dtype),
            pltpu.SMEM(cross_temp.shape, cross_temp.dtype),
            pltpu.SMEM(self_temp.shape, self_temp.dtype),
            pltpu.SemaphoreType.DMA((len(sources),)),
        ],
        compiler_params=params,
        cost_estimate=pl.CostEstimate(
            flops=2 * rows * width * width, bytes_accessed=4 * 2**20, transcendentals=0
        ),
        name="load",
    )(counts, *map(in_hbm, sources))
    count = sum(piece.shape[0] for piece in pieces)
    block = rows if count <= 128 else min(rows, 128)
    kv_shape = pltpu.VMEM((2 * rows, width), jnp.bfloat16)
    x1, hn, kv = pl.pallas_call(
        functools.partial(cross_kernel, len(pieces), block, tile, heads),
        out_shape=(pltpu.VMEM((rows, width), jnp.float32), tokens, kv_shape),
        in_specs=[VMEM] * (6 + len(pieces)),
        out_specs=(VMEM, VMEM, VMEM),
        scratch_shapes=[
            pltpu.VMEM((heads * count, width), jnp.bfloat16),
            pltpu.VMEM((heads * count, width), jnp.bfloat16),
        ],
        compiler_params=params,
        name="cross",
    )(scales, live, x, qc, *pieces, packed, wvt)
    other = swap(kv, "col")
    part = width // heads + 16
    depth = min(128, width)
    block = min(256, rows)
    held = [
        pltpu.VMEM((heads * part, rows), jnp.bfloat16),
        pltpu.VMEM((2, rows, block), jnp.float32),
        pltpu.VMEM((2, rows, block), jnp.bfloat16),
        pltpu.VMEM((4, 8, block), jnp.float32),
    ]
    qt, tops, sums = pl.pallas_call(
        functools.partial(own_kernel, heads),
        out_shape=(
            pltpu.VMEM((heads * depth, rows), jnp.bfloat16),
            pltpu.VMEM((heads, rows), jnp.float32),
            pltpu.VMEM((heads * part, rows), jnp.float32),
        ),
        in_specs=[VMEM] * 4,
        out_specs=(VMEM, VMEM, VMEM),
        scratch_shapes=held,
        compiler_params=params,
        cost_estimate=pl.CostEstimate(
            flops=8 * heads * rows * rows * width, bytes_accessed=2**20, transcendentals=0
        ),
        name="own",
    )(scales, hn, kv, wqt)
    late = (self_wo, ffn_up, ffn_down, box_w1, box_w2, jnp.transpose(box_w3))
    return pl.pallas_call(
        functools.partial(rest_kernel, heads),
        out_shape=(
            jax.ShapeDtypeStruct((rows, width), jnp.float32),
            jax.ShapeDtypeStruct((box_w3.shape[1], rows), jnp.float32),
        ),
        in_specs=[VMEM] * 7 + [HBM] * len(late),
        out_specs=(HBM, VMEM),
        scratch_shapes=held
        + [
            pltpu.VMEM((width, rows), jnp.bfloat16),
            pltpu.VMEM((rows, width), jnp.float32),
            pltpu.VMEM((2, block, ffn_up.shape[1]), jnp.bfloat16),
        ]
        + [pltpu.VMEM(w.shape, w.dtype) for w in late]
        + [pltpu.SemaphoreType.DMA((len(late) + rows // block,))],
        compiler_params=params,
        name="rest",
    )(scales, live, x1, other, qt, tops, sums, *map(in_hbm, late))


def solution(mesh):
    return jax.shard_map(
        local,
        mesh=mesh,
        in_specs=(
            P(("parts", "row", "col"), None),
            P(("parts", "row", "col")),
            P(("parts", "row", "col"), None),
            P(("parts", "row", "col")),
            P(),
            P(),
            P(),
            P(),
            P(),
            P(),
            P(),
            P(),
            P(),
            P(),
            P(),
            P(),
        ),
        out_specs=(P(("parts", "row", "col"), None), P(None, ("parts", "row", "col"))),
        check_vma=False,
    )
```

```python
import functools
import math

import jax
import jax.numpy as jnp
from jax import lax
from jax.experimental import pallas as pl
from jax.experimental.pallas import tpu as pltpu
from jax.sharding import PartitionSpec as P

EPS = 1e-06
DEAD = 64.0
DEAD_V = 4096.0
LOG2E = math.log2(math.e)
VMEM = pl.BlockSpec(memory_space=pltpu.VMEM)
SMEM = pl.BlockSpec(memory_space=pltpu.SMEM)
HBM = pl.BlockSpec(memory_space=pltpu.HBM)


def rms_round(x):
    return (x * lax.rsqrt(jnp.mean(x * x, axis=-1, keepdims=True) + EPS)).astype(jnp.bfloat16)


def dot(a, b):
    return jnp.dot(a, b, preferred_element_type=jnp.float32)


def dot_t(a, b):
    return lax.dot_general(a, b, (((1,), (1,)), ((), ())), preferred_element_type=jnp.float32)


def head_of_lane(rows, width, heads):
    return lax.broadcasted_iota(jnp.int32, (rows, width), 1) // (width // heads)


def only(x, head, lane_head):
    return jnp.where(lane_head == head, x, jnp.zeros_like(x))


def flagged(values, flags, head, heads, lane_head):
    other = (head + heads // 2) % heads
    rest = jnp.where(lane_head == other, flags, jnp.zeros_like(values))
    return jnp.where(lane_head == head, values, rest)


def weigh(scores, top, scale):
    return jnp.exp2((scores - top) * scale).astype(jnp.bfloat16)


def normed(low, high):
    half = low.shape[1] // 2
    return jnp.concatenate(
        [low[:, :half] / low[:, half:], high[:, half:] / high[:, :half]], axis=1
    ).astype(jnp.bfloat16)


def mark_kernel(memory, mask, out, held, flags, sems):
    copies = [
        pltpu.make_async_copy(memory, held, sems.at[0]),
        pltpu.make_async_copy(mask, flags, sems.at[1]),
    ]
    for copy in copies:
        copy.start()
    for copy in copies:
        copy.wait()
    row = lax.broadcasted_iota(jnp.int32, held.shape, 0)
    tokens = held[...].astype(jnp.float32)
    for j in range(held.shape[0]):
        tokens = jnp.where((row == j) & (flags[j] <= 0), DEAD, tokens)
    tokens = tokens.astype(jnp.bfloat16)
    for copy in range(out.shape[0]):
        out[copy] = tokens


def load_kernel(
    counts,
    queries,
    wq,
    cross_temp,
    self_temp,
    wkv,
    wo,
    wqkv,
    x_ref,
    qc_ref,
    scale_ref,
    count_ref,
    packed,
    wvt_ref,
    wqt_ref,
    wq_held,
    cross_held,
    self_held,
    sems,
):
    width = x_ref.shape[1]
    pairs = [(queries, x_ref), (wq, wq_held), (cross_temp, cross_held), (self_temp, self_held)]
    begin = 0
    for source in (wkv, wo, wqkv):
        end = begin + source.shape[1]
        pairs.append((source, packed.at[:, begin:end]))
        begin = end
    copies = [pltpu.make_async_copy(a, b, sems.at[i]) for i, (a, b) in enumerate(pairs)]
    for copy in copies:
        copy.start()
    for copy in copies[:4]:
        copy.wait()
    heads = cross_temp.shape[0]
    factor = LOG2E / math.sqrt(width // heads)
    lanes = scale_ref.shape[1]
    for side, temp in enumerate((cross_held, self_held)):
        for head in range(heads):
            at = pl.ds(side * heads + head, 1)
            scale_ref[at, :] = jnp.full((1, lanes), temp[head] * factor, jnp.float32)
    count_ref[...] = jnp.full(count_ref.shape, counts[0], jnp.int32)
    x = x_ref[...].astype(jnp.float32)
    qc_ref[...] = dot(rms_round(x), wq_held[...]).astype(jnp.bfloat16)
    for copy in copies[4:]:
        copy.wait()
    wvt_ref[...] = jnp.transpose(packed[:, -width:])
    wqt_ref[...] = jnp.transpose(packed[:, -3 * width : -2 * width])


def cross_kernel(n, block, tile, heads, scales, counts, queries, qc, *refs):
    pieces = refs[:n]
    packed, wvt, x1_ref, hn_ref, kv_ref, kbd, vbd = refs[n:]
    rows, width = queries.shape
    wkv = packed[:, : 2 * width]
    wo = packed[:, 2 * width : 3 * width]
    wk = packed[:, 4 * width : 5 * width]
    tokens, flags = [], []
    for piece in pieces:
        held = piece[...].astype(jnp.float32)
        dead = held >= DEAD
        for begin in range(0, held.shape[0], tile):
            part = held[begin : begin + tile]
            gone = dead[begin : begin + tile]
            tokens.append(jnp.where(gone, part[:1], part).astype(jnp.bfloat16))
            flags.append(jnp.where(gone, 0.0, 1.0).astype(jnp.bfloat16))
    tokens = jnp.concatenate(tokens, axis=0)
    flags = jnp.concatenate(flags, axis=0)
    count = tokens.shape[0]
    kvm = dot(tokens, wkv).astype(jnp.bfloat16)
    keys = kvm[:, :width]
    values = kvm[:, width:] * flags
    lane_head = head_of_lane(count, width, heads)
    for head in range(heads):
        at = pl.ds(head * count, count)
        kbd[at, :] = only(keys, head, lane_head)
        vbd[at, :] = flagged(values, flags, head, heads, lane_head)
    middle = heads // 2 * count
    for begin in range(0, rows, block):
        at = pl.ds(begin, block)
        x = queries[at, :].astype(jnp.float32)
        scores = dot_t(qc[at, :], kbd[...])
        weights = []
        for head in range(heads):
            s = scores[:, head * count : (head + 1) * count]
            top = jnp.max(s, axis=-1, keepdims=True)
            weights.append(weigh(s, top, scales[head : head + 1, :1]))
        low = dot(jnp.concatenate(weights[: heads // 2], axis=1), vbd[:middle, :])
        high = dot(jnp.concatenate(weights[heads // 2 :], axis=1), vbd[middle:, :])
        x1 = x + dot(normed(low, high), wo)
        x1_ref[at, :] = x1
        hn1 = rms_round(x1)
        hn_ref[at, :] = hn1
        key = dot(hn1, wk).astype(jnp.bfloat16)
        slot = lax.broadcasted_iota(jnp.int32, (block, width), 0) + begin
        if begin == 0:
            first = key[:1]
        kv_ref[at, :] = jnp.where(slot < counts[:1, :1], key, first)
        value = dot_t(wvt[...], hn1).astype(jnp.bfloat16)
        slot = lax.broadcasted_iota(jnp.int32, (width, block), 1) + begin
        value = jnp.where(slot < counts[:1, :1], value, jnp.bfloat16(DEAD_V))
        for part in range(0, block, width):
            place = begin + part
            size = min(block, width)
            target = pl.ds(rows + place // width * width, width)
            lanes = pl.ds(place % width, size)
            kv_ref[target, lanes] = value[:, part : part + size]


def transposed_values(kv, vt, heads):
    rows, width = vt.shape[1], kv.shape[1]
    hsize, part = width // heads, vt.shape[0] // heads
    for begin in range(0, rows, width):
        lanes = pl.ds(begin, width)
        values = kv[rows + begin : rows + begin + width, :]
        live = values < jnp.bfloat16(DEAD_V)
        flags = jnp.where(live[: part - hsize], jnp.bfloat16(1), jnp.bfloat16(0))
        values = jnp.where(live, values, jnp.bfloat16(0))
        for head in range(heads):
            at = head * part
            vt[at : at + hsize, lanes] = values[head * hsize : (head + 1) * hsize]
            vt[at + hsize : at + part, lanes] = flags


def half_attention(scales, qt, kv, vt, heads, s_held, p_held, use):
    rows, width = vt.shape[1], kv.shape[1]
    part = vt.shape[0] // heads
    depth = qt.shape[0] // heads
    per = heads * depth // width
    block = s_held.shape[2]
    units = [(head, begin) for head in range(heads) for begin in range(0, rows, block)]
    tops = {}

    def score(unit):
        head, begin = units[unit]
        lanes = head // per * depth
        q = qt[head * depth : (head + 1) * depth, begin : begin + block]
        s = dot(kv[:rows, lanes : lanes + depth], q)
        s_held[unit % 2] = s
        tops[unit] = jnp.max(s, axis=0, keepdims=True)

    def soften(unit):
        head, begin = units[unit]
        scale = scales[heads + head : heads + head + 1, :1]
        p_held[unit % 2] = weigh(s_held[unit % 2], tops[unit], scale)

    def mix(unit):
        head, begin = units[unit]
        total = dot(vt[head * part : (head + 1) * part, :], p_held[unit % 2])
        use(head, pl.ds(begin, block), tops[unit], total)

    for step in range(len(units) + 2):
        if step < len(units):
            score(step)
        if 0 <= step - 1 < len(units):
            soften(step - 1)
        if 0 <= step - 2:
            mix(step - 2)


def own_kernel(heads, scales, hn, kv, wqt, qt, top_ref, sum_ref, vt, s_held, p_held):
    width = hn.shape[1]
    hsize = width // heads
    depth = qt.shape[0] // heads
    part = vt.shape[0] // heads
    q = dot_t(wqt[...], hn[...]).astype(jnp.bfloat16)
    qt[...] = jnp.zeros_like(qt)
    for head in range(heads):
        begin = head * hsize
        at = head * depth + begin % depth
        qt[at : at + hsize, :] = q[begin : begin + hsize]
    transposed_values(kv, vt, heads)

    def use(head, at, top, total):
        top_ref[head : head + 1, at] = top
        sum_ref[head * part : (head + 1) * part, at] = total

    half_attention(scales, qt, kv, vt, heads, s_held, p_held, use)


def rest_kernel(
    heads,
    scales,
    counts,
    x1_ref,
    kv,
    qt,
    top_ref,
    sum_ref,
    wo,
    up,
    down,
    w1,
    w2,
    w3,
    features,
    boxes,
    vt,
    s_held,
    p_held,
    ctx,
    out,
    upper,
    wo_held,
    up_held,
    down_held,
    w1_held,
    w2_held,
    w3_held,
    sems,
):
    rows, width = x1_ref.shape
    hsize = width // heads
    part = vt.shape[0] // heads
    held = (wo_held, up_held, down_held, w1_held, w2_held, w3_held)
    pairs = zip((wo, up, down, w1, w2, w3), held)
    copies = [pltpu.make_async_copy(a, b, sems.at[i]) for i, (a, b) in enumerate(pairs)]
    for copy in copies:
        copy.start()
    transposed_values(kv, vt, heads)

    def use(head, at, top, total):
        scale = scales[heads + head : heads + head + 1, :1]
        first = top_ref[head : head + 1, at]
        most = jnp.maximum(first, top)
        total = total * jnp.exp2((top - most) * scale)
        total += sum_ref[head * part : (head + 1) * part, at] * jnp.exp2((first - most) * scale)
        mixed = total[:hsize] / total[hsize : hsize + 1]
        ctx[head * hsize : (head + 1) * hsize, at] = mixed.astype(jnp.bfloat16)

    half_attention(scales, qt, kv, vt, heads, s_held, p_held, use)
    for copy in copies:
        copy.wait()
    block = upper.shape[1]
    starts = list(range(0, rows, block))
    ff = up_held.shape[1]
    chunk = ff // 4
    x2, x3, leaves = {}, {}, []

    def project(i):
        at = pl.ds(starts[i], block)
        mixed = lax.dot_general(
            ctx[:, at], wo_held[...], (((0,), (0,)), ((), ())), preferred_element_type=jnp.float32
        )
        x2[i] = x1_ref[at, :] + mixed

    def widen(i):
        hn2 = rms_round(x2[i])
        for begin in range(0, ff, chunk):
            cut = pl.ds(begin, chunk)
            upper[i % 2, :, cut] = jnp.maximum(dot(hn2, up_held[:, cut]), 0.0).astype(jnp.bfloat16)

    def narrow(i):
        at = pl.ds(starts[i], block)
        x3[i] = x2[i] + dot(upper[i % 2], down_held[...])
        slot = lax.broadcasted_iota(jnp.int32, (block, width), 0) + starts[i]
        out[at, :] = jnp.where(slot < counts[:1, :1], x3[i], 0.0)
        leaves.append(
            pltpu.make_async_copy(out.at[at, :], features.at[at, :], sems.at[len(copies) + i])
        )
        leaves[-1].start()

    def box(i):
        b1 = jnp.maximum(dot(rms_round(x3[i]), w1_held[...]), 0.0).astype(jnp.bfloat16)
        b2 = jnp.maximum(dot(b1, w2_held[...]), 0.0).astype(jnp.bfloat16)
        raw = dot_t(w3_held[...], b2)
        slot = lax.broadcasted_iota(jnp.int32, raw.shape, 1) + starts[i]
        boxes[:, pl.ds(starts[i], block)] = jnp.where(
            slot < counts[:1, :1], 1.0 / (1.0 + jnp.exp(-raw)), 0.0
        )

    for step in range(len(starts) + 3):
        for stage, work in enumerate((project, widen, narrow, box)):
            if 0 <= step - stage < len(starts):
                work(step - stage)
    for leave in leaves:
        leave.wait()


def in_hbm(x):
    return pltpu.with_memory_space_constraint(x, pltpu.HBM)


def swap(x, axis):
    size = lax.axis_size(axis)
    return lax.ppermute(x, axis, [(i, i ^ 1) for i in range(size)])


def local(
    queries,
    counts,
    memory,
    mem_mask,
    cross_wq,
    cross_wkv,
    cross_wo,
    self_wqkv,
    self_wo,
    ffn_up,
    ffn_down,
    box_w1,
    box_w2,
    box_w3,
    cross_temp,
    self_temp,
):
    rows, width = queries.shape
    heads = cross_temp.shape[0]
    tile = memory.shape[0]
    params = pltpu.CompilerParams(vmem_limit_bytes=32 * 2**20)
    marked = pl.pallas_call(
        mark_kernel,
        out_shape=pltpu.VMEM((lax.axis_size("row"), tile, width), memory.dtype),
        in_specs=[HBM, HBM],
        out_specs=VMEM,
        scratch_shapes=[
            pltpu.VMEM(memory.shape, memory.dtype),
            pltpu.SMEM(mem_mask.shape, mem_mask.dtype),
            pltpu.SemaphoreType.DMA((2,)),
        ],
        name="mark",
    )(in_hbm(memory), in_hbm(mem_mask))
    gathered = lax.all_to_all(marked, "row", 0, 0, tiled=True)
    pieces = [gathered.reshape(-1, width)]
    tokens = pltpu.VMEM((rows, width), jnp.bfloat16)
    packed_width = cross_wkv.shape[1] + cross_wo.shape[1] + self_wqkv.shape[1]
    sources = (queries, cross_wq, cross_temp, self_temp, cross_wkv, cross_wo, self_wqkv)
    x, qc, scales, live, packed, wvt, wqt = pl.pallas_call(
        load_kernel,
        out_shape=[
            tokens,
            tokens,
            pltpu.VMEM((2 * heads, 128), jnp.float32),
            pltpu.VMEM((8, 128), jnp.int32),
            pltpu.VMEM((width, packed_width), jnp.bfloat16),
            pltpu.VMEM((width, width), jnp.bfloat16),
            pltpu.VMEM((width, width), jnp.bfloat16),
        ],
        in_specs=[SMEM] + [HBM] * len(sources),
        out_specs=[VMEM] * 7,
        scratch_shapes=[
            pltpu.VMEM(cross_wq.shape, cross_wq.dtype),
            pltpu.SMEM(cross_temp.shape, cross_temp.dtype),
            pltpu.SMEM(self_temp.shape, self_temp.dtype),
            pltpu.SemaphoreType.DMA((len(sources),)),
        ],
        compiler_params=params,
        cost_estimate=pl.CostEstimate(
            flops=2 * rows * width * width, bytes_accessed=4 * 2**20, transcendentals=0
        ),
        name="load",
    )(counts, *map(in_hbm, sources))
    count = sum(piece.shape[0] for piece in pieces)
    block = rows if count <= 128 else min(rows, 128)
    kv_shape = pltpu.VMEM((2 * rows, width), jnp.bfloat16)
    x1, hn, kv = pl.pallas_call(
        functools.partial(cross_kernel, len(pieces), block, tile, heads),
        out_shape=(pltpu.VMEM((rows, width), jnp.float32), tokens, kv_shape),
        in_specs=[VMEM] * (6 + len(pieces)),
        out_specs=(VMEM, VMEM, VMEM),
        scratch_shapes=[
            pltpu.VMEM((heads * count, width), jnp.bfloat16),
            pltpu.VMEM((heads * count, width), jnp.bfloat16),
        ],
        compiler_params=params,
        name="cross",
    )(scales, live, x, qc, *pieces, packed, wvt)
    other = swap(kv, "col")
    part = width // heads + 16
    depth = min(128, width)
    block = min(256, rows)
    held = [
        pltpu.VMEM((heads * part, rows), jnp.bfloat16),
        pltpu.VMEM((2, rows, block), jnp.float32),
        pltpu.VMEM((2, rows, block), jnp.bfloat16),
    ]
    qt, tops, sums = pl.pallas_call(
        functools.partial(own_kernel, heads),
        out_shape=(
            pltpu.VMEM((heads * depth, rows), jnp.bfloat16),
            pltpu.VMEM((heads, rows), jnp.float32),
            pltpu.VMEM((heads * part, rows), jnp.float32),
        ),
        in_specs=[VMEM] * 4,
        out_specs=(VMEM, VMEM, VMEM),
        scratch_shapes=held,
        compiler_params=params,
        cost_estimate=pl.CostEstimate(
            flops=8 * heads * rows * rows * width, bytes_accessed=2**20, transcendentals=0
        ),
        name="own",
    )(scales, hn, kv, wqt)
    late = (self_wo, ffn_up, ffn_down, box_w1, box_w2, jnp.transpose(box_w3))
    return pl.pallas_call(
        functools.partial(rest_kernel, heads),
        out_shape=(
            jax.ShapeDtypeStruct((rows, width), jnp.float32),
            jax.ShapeDtypeStruct((box_w3.shape[1], rows), jnp.float32),
        ),
        in_specs=[VMEM] * 7 + [HBM] * len(late),
        out_specs=(HBM, VMEM),
        scratch_shapes=held
        + [
            pltpu.VMEM((width, rows), jnp.bfloat16),
            pltpu.VMEM((rows, width), jnp.float32),
            pltpu.VMEM((2, block, ffn_up.shape[1]), jnp.bfloat16),
        ]
        + [pltpu.VMEM(w.shape, w.dtype) for w in late]
        + [pltpu.SemaphoreType.DMA((len(late) + rows // block,))],
        compiler_params=params,
        name="rest",
    )(scales, live, x1, other, qt, tops, sums, *map(in_hbm, late))


def solution(mesh):
    return jax.shard_map(
        local,
        mesh=mesh,
        in_specs=(
            P(("parts", "row", "col"), None),
            P(("parts", "row", "col")),
            P(("parts", "row", "col"), None),
            P(("parts", "row", "col")),
            P(),
            P(),
            P(),
            P(),
            P(),
            P(),
            P(),
            P(),
            P(),
            P(),
            P(),
            P(),
        ),
        out_specs=(P(("parts", "row", "col"), None), P(None, ("parts", "row", "col"))),
        check_vma=False,
    )
```

```python
import functools
import math

import jax
import jax.numpy as jnp
from jax import lax
from jax.experimental import pallas as pl
from jax.experimental.pallas import tpu as pltpu
from jax.sharding import PartitionSpec as P

EPS = 1e-06
DEAD = 64.0
DEAD_V = 4096.0
LOG2E = math.log2(math.e)
VMEM = pl.BlockSpec(memory_space=pltpu.VMEM)
SMEM = pl.BlockSpec(memory_space=pltpu.SMEM)
HBM = pl.BlockSpec(memory_space=pltpu.HBM)


def rms_round(x):
    return (x * lax.rsqrt(jnp.mean(x * x, axis=-1, keepdims=True) + EPS)).astype(jnp.bfloat16)


def dot(a, b):
    return jnp.dot(a, b, preferred_element_type=jnp.float32)


def dot_t(a, b):
    return lax.dot_general(a, b, (((1,), (1,)), ((), ())), preferred_element_type=jnp.float32)


def head_of_lane(rows, width, heads):
    return lax.broadcasted_iota(jnp.int32, (rows, width), 1) // (width // heads)


def only(x, head, lane_head):
    return jnp.where(lane_head == head, x, jnp.zeros_like(x))


def flagged(values, flags, head, heads, lane_head):
    other = (head + heads // 2) % heads
    rest = jnp.where(lane_head == other, flags, jnp.zeros_like(values))
    return jnp.where(lane_head == head, values, rest)


def weigh(scores, top, scale):
    return jnp.exp2((scores - top) * scale).astype(jnp.bfloat16)


def normed(low, high):
    half = low.shape[1] // 2
    return jnp.concatenate(
        [low[:, :half] / low[:, half:], high[:, half:] / high[:, :half]], axis=1
    ).astype(jnp.bfloat16)


def mark_kernel(memory, mask, out, held, flags, sems):
    copies = [
        pltpu.make_async_copy(memory, held, sems.at[0]),
        pltpu.make_async_copy(mask, flags, sems.at[1]),
    ]
    for copy in copies:
        copy.start()
    for copy in copies:
        copy.wait()
    row = lax.broadcasted_iota(jnp.int32, held.shape, 0)
    tokens = held[...].astype(jnp.float32)
    for j in range(held.shape[0]):
        tokens = jnp.where((row == j) & (flags[j] <= 0), DEAD, tokens)
    tokens = tokens.astype(jnp.bfloat16)
    for copy in range(out.shape[0]):
        out[copy] = tokens


def load_kernel(
    counts,
    queries,
    wq,
    cross_temp,
    self_temp,
    wkv,
    wo,
    wqkv,
    x_ref,
    qc_ref,
    scale_ref,
    count_ref,
    packed,
    wvt_ref,
    wqt_ref,
    wq_held,
    cross_held,
    self_held,
    sems,
):
    width = x_ref.shape[1]
    pairs = [(queries, x_ref), (wq, wq_held), (cross_temp, cross_held), (self_temp, self_held)]
    begin = 0
    for source in (wkv, wo, wqkv):
        end = begin + source.shape[1]
        pairs.append((source, packed.at[:, begin:end]))
        begin = end
    copies = [pltpu.make_async_copy(a, b, sems.at[i]) for i, (a, b) in enumerate(pairs)]
    for copy in copies:
        copy.start()
    for copy in copies[:4]:
        copy.wait()
    heads = cross_temp.shape[0]
    factor = LOG2E / math.sqrt(width // heads)
    lanes = scale_ref.shape[1]
    for side, temp in enumerate((cross_held, self_held)):
        for head in range(heads):
            at = pl.ds(side * heads + head, 1)
            scale_ref[at, :] = jnp.full((1, lanes), temp[head] * factor, jnp.float32)
    count_ref[...] = jnp.full(count_ref.shape, counts[0], jnp.int32)
    x = x_ref[...].astype(jnp.float32)
    qc_ref[...] = dot(rms_round(x), wq_held[...]).astype(jnp.bfloat16)
    for copy in copies[4:]:
        copy.wait()
    wvt_ref[...] = jnp.transpose(packed[:, -width:])
    wqt_ref[...] = jnp.transpose(packed[:, -3 * width : -2 * width])


def cross_kernel(n, block, tile, heads, scales, counts, queries, qc, *refs):
    pieces = refs[:n]
    packed, wvt, x1_ref, hn_ref, kv_ref, kbd, vbd = refs[n:]
    rows, width = queries.shape
    wkv = packed[:, : 2 * width]
    wo = packed[:, 2 * width : 3 * width]
    wk = packed[:, 4 * width : 5 * width]
    tokens, flags = [], []
    for piece in pieces:
        held = piece[...].astype(jnp.float32)
        dead = held >= DEAD
        for begin in range(0, held.shape[0], tile):
            part = held[begin : begin + tile]
            gone = dead[begin : begin + tile]
            tokens.append(jnp.where(gone, part[:1], part).astype(jnp.bfloat16))
            flags.append(jnp.where(gone, 0.0, 1.0).astype(jnp.bfloat16))
    tokens = jnp.concatenate(tokens, axis=0)
    flags = jnp.concatenate(flags, axis=0)
    count = tokens.shape[0]
    kvm = dot(tokens, wkv).astype(jnp.bfloat16)
    keys = kvm[:, :width]
    values = kvm[:, width:] * flags
    lane_head = head_of_lane(count, width, heads)
    for head in range(heads):
        at = pl.ds(head * count, count)
        kbd[at, :] = only(keys, head, lane_head)
        vbd[at, :] = flagged(values, flags, head, heads, lane_head)
    middle = heads // 2 * count
    for begin in range(0, rows, block):
        at = pl.ds(begin, block)
        x = queries[at, :].astype(jnp.float32)
        scores = dot_t(qc[at, :], kbd[...])
        weights = []
        for head in range(heads):
            s = scores[:, head * count : (head + 1) * count]
            top = jnp.max(s, axis=-1, keepdims=True)
            weights.append(weigh(s, top, scales[head : head + 1, :1]))
        low = dot(jnp.concatenate(weights[: heads // 2], axis=1), vbd[:middle, :])
        high = dot(jnp.concatenate(weights[heads // 2 :], axis=1), vbd[middle:, :])
        x1 = x + dot(normed(low, high), wo)
        x1_ref[at, :] = x1
        hn1 = rms_round(x1)
        hn_ref[at, :] = hn1
        key = dot(hn1, wk).astype(jnp.bfloat16)
        slot = lax.broadcasted_iota(jnp.int32, (block, width), 0) + begin
        if begin == 0:
            first = key[:1]
        kv_ref[at, :] = jnp.where(slot < counts[:1, :1], key, first)
        value = dot_t(wvt[...], hn1).astype(jnp.bfloat16)
        slot = lax.broadcasted_iota(jnp.int32, (width, block), 1) + begin
        value = jnp.where(slot < counts[:1, :1], value, jnp.bfloat16(DEAD_V))
        for part in range(0, block, width):
            place = begin + part
            size = min(block, width)
            target = pl.ds(rows + place // width * width, width)
            lanes = pl.ds(place % width, size)
            kv_ref[target, lanes] = value[:, part : part + size]


def transposed_values(kv, vt, heads):
    rows, width = vt.shape[1], kv.shape[1]
    hsize, part = width // heads, vt.shape[0] // heads
    for begin in range(0, rows, width):
        lanes = pl.ds(begin, width)
        values = kv[rows + begin : rows + begin + width, :]
        live = values < jnp.bfloat16(DEAD_V)
        flags = jnp.where(live[: part - hsize], jnp.bfloat16(1), jnp.bfloat16(0))
        values = jnp.where(live, values, jnp.bfloat16(0))
        for head in range(heads):
            at = head * part
            vt[at : at + hsize, lanes] = values[head * hsize : (head + 1) * hsize]
            vt[at + hsize : at + part, lanes] = flags


def half_attention(scales, qt, kv, vt, heads, s_held, p_held, use, after=None):
    rows, width = vt.shape[1], kv.shape[1]
    part = vt.shape[0] // heads
    depth = qt.shape[0] // heads
    per = heads * depth // width
    block = s_held.shape[2]
    units = [(head, begin) for begin in range(0, rows, block) for head in range(heads)]
    tops = {}

    def score(unit):
        head, begin = units[unit]
        lanes = head // per * depth
        q = qt[head * depth : (head + 1) * depth, begin : begin + block]
        s = dot(kv[:rows, lanes : lanes + depth], q)
        s_held[unit % 2] = s
        tops[unit] = jnp.max(s, axis=0, keepdims=True)

    def soften(unit):
        head, begin = units[unit]
        scale = scales[heads + head : heads + head + 1, :1]
        p_held[unit % 2] = weigh(s_held[unit % 2], tops[unit], scale)

    def mix(unit):
        head, begin = units[unit]
        total = dot(vt[head * part : (head + 1) * part, :], p_held[unit % 2])
        use(head, pl.ds(begin, block), tops[unit], total)

    for step in range(len(units) + 2):
        if step < len(units):
            score(step)
        if 0 <= step - 1 < len(units):
            soften(step - 1)
        if 0 <= step - 2:
            mix(step - 2)
            if after is not None:
                after(step - 2)


def own_kernel(heads, scales, hn, kv, wqt, qt, top_ref, sum_ref, vt, s_held, p_held):
    width = hn.shape[1]
    hsize = width // heads
    depth = qt.shape[0] // heads
    part = vt.shape[0] // heads
    q = dot_t(wqt[...], hn[...]).astype(jnp.bfloat16)
    qt[...] = jnp.zeros_like(qt)
    for head in range(heads):
        begin = head * hsize
        at = head * depth + begin % depth
        qt[at : at + hsize, :] = q[begin : begin + hsize]
    transposed_values(kv, vt, heads)

    def use(head, at, top, total):
        top_ref[head : head + 1, at] = top
        sum_ref[head * part : (head + 1) * part, at] = total

    half_attention(scales, qt, kv, vt, heads, s_held, p_held, use)


def rest_kernel(
    heads,
    scales,
    counts,
    x1_ref,
    kv,
    qt,
    top_ref,
    sum_ref,
    wo,
    up,
    down,
    w1,
    w2,
    w3,
    features,
    boxes,
    vt,
    s_held,
    p_held,
    ctx,
    out,
    upper,
    wo_held,
    up_held,
    down_held,
    w1_held,
    w2_held,
    w3_held,
    sems,
):
    rows, width = x1_ref.shape
    hsize = width // heads
    part = vt.shape[0] // heads
    held = (wo_held, up_held, down_held, w1_held, w2_held, w3_held)
    pairs = zip((wo, up, down, w1, w2, w3), held)
    copies = [pltpu.make_async_copy(a, b, sems.at[i]) for i, (a, b) in enumerate(pairs)]
    for copy in copies:
        copy.start()
    transposed_values(kv, vt, heads)

    def use(head, at, top, total):
        scale = scales[heads + head : heads + head + 1, :1]
        first = top_ref[head : head + 1, at]
        most = jnp.maximum(first, top)
        total = total * jnp.exp2((top - most) * scale)
        total += sum_ref[head * part : (head + 1) * part, at] * jnp.exp2((first - most) * scale)
        mixed = total[:hsize] / total[hsize : hsize + 1]
        ctx[head * hsize : (head + 1) * hsize, at] = mixed.astype(jnp.bfloat16)

    block = upper.shape[1]
    starts = list(range(0, rows, block))
    ff = up_held.shape[1]
    chunk = ff // 4
    x2, x3, hn2, leaves = {}, {}, {}, []

    def project(i):
        at = pl.ds(starts[i], block)
        if i == 0:
            copies[0].wait()
        mixed = lax.dot_general(
            ctx[:, at], wo_held[...], (((0,), (0,)), ((), ())), preferred_element_type=jnp.float32
        )
        x2[i] = x1_ref[at, :] + mixed

    def widen(i, begin):
        if begin == 0:
            hn2[i] = rms_round(x2[i])
            if i == 0:
                copies[1].wait()
        cut = pl.ds(begin, chunk)
        up_cut = jnp.maximum(dot(hn2[i], up_held[:, cut]), 0.0)
        upper[i % 2, :, cut] = up_cut.astype(jnp.bfloat16)

    def narrow(i):
        at = pl.ds(starts[i], block)
        if i == 0:
            copies[2].wait()
        x3[i] = x2[i] + dot(upper[i % 2], down_held[...])
        slot = lax.broadcasted_iota(jnp.int32, (block, width), 0) + starts[i]
        out[at, :] = jnp.where(slot < counts[:1, :1], x3[i], 0.0)
        leaves.append(
            pltpu.make_async_copy(out.at[at, :], features.at[at, :], sems.at[len(copies) + i])
        )
        leaves[-1].start()

    def box(i):
        if i == 0:
            for copy in copies[3:]:
                copy.wait()
        b1 = jnp.maximum(dot(rms_round(x3[i]), w1_held[...]), 0.0).astype(jnp.bfloat16)
        b2 = jnp.maximum(dot(b1, w2_held[...]), 0.0).astype(jnp.bfloat16)
        raw = dot_t(w3_held[...], b2)
        slot = lax.broadcasted_iota(jnp.int32, raw.shape, 1) + starts[i]
        boxes[:, pl.ds(starts[i], block)] = jnp.where(
            slot < counts[:1, :1], 1.0 / (1.0 + jnp.exp(-raw)), 0.0
        )

    def tail(i):
        yield project(i)
        for begin in range(0, ff, chunk):
            yield widen(i, begin)
        yield narrow(i)
        yield box(i)

    tails = [tail(i) for i in range(len(starts))]

    def after(unit):
        done = (unit + 1) // heads
        for i in range(done):
            if next(tails[i], tails) is not tails:
                break

    half_attention(scales, qt, kv, vt, heads, s_held, p_held, use, after)
    for rest in tails:
        for _ in rest:
            pass
    for leave in leaves:
        leave.wait()


def in_hbm(x):
    return pltpu.with_memory_space_constraint(x, pltpu.HBM)


def swap(x, axis):
    size = lax.axis_size(axis)
    return lax.ppermute(x, axis, [(i, i ^ 1) for i in range(size)])


def local(
    queries,
    counts,
    memory,
    mem_mask,
    cross_wq,
    cross_wkv,
    cross_wo,
    self_wqkv,
    self_wo,
    ffn_up,
    ffn_down,
    box_w1,
    box_w2,
    box_w3,
    cross_temp,
    self_temp,
):
    rows, width = queries.shape
    heads = cross_temp.shape[0]
    tile = memory.shape[0]
    params = pltpu.CompilerParams(vmem_limit_bytes=32 * 2**20)
    marked = pl.pallas_call(
        mark_kernel,
        out_shape=pltpu.VMEM((lax.axis_size("row"), tile, width), memory.dtype),
        in_specs=[HBM, HBM],
        out_specs=VMEM,
        scratch_shapes=[
            pltpu.VMEM(memory.shape, memory.dtype),
            pltpu.SMEM(mem_mask.shape, mem_mask.dtype),
            pltpu.SemaphoreType.DMA((2,)),
        ],
        name="mark",
    )(in_hbm(memory), in_hbm(mem_mask))
    gathered = lax.all_to_all(marked, "row", 0, 0, tiled=True)
    pieces = [gathered.reshape(-1, width)]
    tokens = pltpu.VMEM((rows, width), jnp.bfloat16)
    packed_width = cross_wkv.shape[1] + cross_wo.shape[1] + self_wqkv.shape[1]
    sources = (queries, cross_wq, cross_temp, self_temp, cross_wkv, cross_wo, self_wqkv)
    x, qc, scales, live, packed, wvt, wqt = pl.pallas_call(
        load_kernel,
        out_shape=[
            tokens,
            tokens,
            pltpu.VMEM((2 * heads, 128), jnp.float32),
            pltpu.VMEM((8, 128), jnp.int32),
            pltpu.VMEM((width, packed_width), jnp.bfloat16),
            pltpu.VMEM((width, width), jnp.bfloat16),
            pltpu.VMEM((width, width), jnp.bfloat16),
        ],
        in_specs=[SMEM] + [HBM] * len(sources),
        out_specs=[VMEM] * 7,
        scratch_shapes=[
            pltpu.VMEM(cross_wq.shape, cross_wq.dtype),
            pltpu.SMEM(cross_temp.shape, cross_temp.dtype),
            pltpu.SMEM(self_temp.shape, self_temp.dtype),
            pltpu.SemaphoreType.DMA((len(sources),)),
        ],
        compiler_params=params,
        cost_estimate=pl.CostEstimate(
            flops=2 * rows * width * width, bytes_accessed=4 * 2**20, transcendentals=0
        ),
        name="load",
    )(counts, *map(in_hbm, sources))
    count = sum(piece.shape[0] for piece in pieces)
    block = rows if count <= 128 else min(rows, 128)
    kv_shape = pltpu.VMEM((2 * rows, width), jnp.bfloat16)
    x1, hn, kv = pl.pallas_call(
        functools.partial(cross_kernel, len(pieces), block, tile, heads),
        out_shape=(pltpu.VMEM((rows, width), jnp.float32), tokens, kv_shape),
        in_specs=[VMEM] * (6 + len(pieces)),
        out_specs=(VMEM, VMEM, VMEM),
        scratch_shapes=[
            pltpu.VMEM((heads * count, width), jnp.bfloat16),
            pltpu.VMEM((heads * count, width), jnp.bfloat16),
        ],
        compiler_params=params,
        name="cross",
    )(scales, live, x, qc, *pieces, packed, wvt)
    other = swap(kv, "col")
    part = width // heads + 16
    depth = min(128, width)
    block = min(256, rows)
    held = [
        pltpu.VMEM((heads * part, rows), jnp.bfloat16),
        pltpu.VMEM((2, rows, block), jnp.float32),
        pltpu.VMEM((2, rows, block), jnp.bfloat16),
    ]
    qt, tops, sums = pl.pallas_call(
        functools.partial(own_kernel, heads),
        out_shape=(
            pltpu.VMEM((heads * depth, rows), jnp.bfloat16),
            pltpu.VMEM((heads, rows), jnp.float32),
            pltpu.VMEM((heads * part, rows), jnp.float32),
        ),
        in_specs=[VMEM] * 4,
        out_specs=(VMEM, VMEM, VMEM),
        scratch_shapes=held,
        compiler_params=params,
        cost_estimate=pl.CostEstimate(
            flops=8 * heads * rows * rows * width, bytes_accessed=2**20, transcendentals=0
        ),
        name="own",
    )(scales, hn, kv, wqt)
    late = (self_wo, ffn_up, ffn_down, box_w1, box_w2, jnp.transpose(box_w3))
    return pl.pallas_call(
        functools.partial(rest_kernel, heads),
        out_shape=(
            jax.ShapeDtypeStruct((rows, width), jnp.float32),
            jax.ShapeDtypeStruct((box_w3.shape[1], rows), jnp.float32),
        ),
        in_specs=[VMEM] * 7 + [HBM] * len(late),
        out_specs=(HBM, VMEM),
        scratch_shapes=held
        + [
            pltpu.VMEM((width, rows), jnp.bfloat16),
            pltpu.VMEM((rows, width), jnp.float32),
            pltpu.VMEM((2, block, ffn_up.shape[1]), jnp.bfloat16),
        ]
        + [pltpu.VMEM(w.shape, w.dtype) for w in late]
        + [pltpu.SemaphoreType.DMA((len(late) + rows // block,))],
        compiler_params=params,
        name="rest",
    )(scales, live, x1, other, qt, tops, sums, *map(in_hbm, late))


def solution(mesh):
    return jax.shard_map(
        local,
        mesh=mesh,
        in_specs=(
            P(("parts", "row", "col"), None),
            P(("parts", "row", "col")),
            P(("parts", "row", "col"), None),
            P(("parts", "row", "col")),
            P(),
            P(),
            P(),
            P(),
            P(),
            P(),
            P(),
            P(),
            P(),
            P(),
            P(),
            P(),
        ),
        out_specs=(P(("parts", "row", "col"), None), P(None, ("parts", "row", "col"))),
        check_vma=False,
    )
```

```python
import functools
import math

import jax
import jax.numpy as jnp
from jax import lax
from jax.experimental import pallas as pl
from jax.experimental.pallas import tpu as pltpu
from jax.sharding import PartitionSpec as P

EPS = 1e-06
DEAD = 64.0
DEAD_V = 4096.0
LOG2E = math.log2(math.e)
LIMIT = 100.0
VMEM = pl.BlockSpec(memory_space=pltpu.VMEM)
SMEM = pl.BlockSpec(memory_space=pltpu.SMEM)
HBM = pl.BlockSpec(memory_space=pltpu.HBM)


def rms_round(x):
    return (x * lax.rsqrt(jnp.mean(x * x, axis=-1, keepdims=True) + EPS)).astype(jnp.bfloat16)


def dot(a, b):
    return jnp.dot(a, b, preferred_element_type=jnp.float32)


def dot_t(a, b):
    return lax.dot_general(a, b, (((1,), (1,)), ((), ())), preferred_element_type=jnp.float32)


def head_of_lane(rows, width, heads):
    return lax.broadcasted_iota(jnp.int32, (rows, width), 1) // (width // heads)


def only(x, head, lane_head):
    return jnp.where(lane_head == head, x, jnp.zeros_like(x))


def flagged(values, flags, head, heads, lane_head):
    other = (head + heads // 2) % heads
    rest = jnp.where(lane_head == other, flags, jnp.zeros_like(values))
    return jnp.where(lane_head == head, values, rest)


def weigh(scores, top, scale):
    return jnp.exp2((scores - top) * scale).astype(jnp.bfloat16)


def normed(low, high):
    half = low.shape[1] // 2
    return jnp.concatenate(
        [low[:, :half] / low[:, half:], high[:, half:] / high[:, :half]], axis=1
    ).astype(jnp.bfloat16)


def mark_kernel(memory, mask, out, held, flags, sems):
    copies = [
        pltpu.make_async_copy(memory, held, sems.at[0]),
        pltpu.make_async_copy(mask, flags, sems.at[1]),
    ]
    for copy in copies:
        copy.start()
    for copy in copies:
        copy.wait()
    row = lax.broadcasted_iota(jnp.int32, held.shape, 0)
    tokens = held[...].astype(jnp.float32)
    for j in range(held.shape[0]):
        tokens = jnp.where((row == j) & (flags[j] <= 0), DEAD, tokens)
    tokens = tokens.astype(jnp.bfloat16)
    for copy in range(out.shape[0]):
        out[copy] = tokens


def load_kernel(
    counts,
    queries,
    wq,
    cross_temp,
    self_temp,
    wkv,
    wo,
    wqkv,
    x_ref,
    qc_ref,
    scale_ref,
    count_ref,
    packed,
    wvt_ref,
    wqt_ref,
    wq_held,
    cross_held,
    self_held,
    sems,
):
    width = x_ref.shape[1]
    pairs = [(queries, x_ref), (wq, wq_held), (cross_temp, cross_held), (self_temp, self_held)]
    begin = 0
    for source in (wkv, wo, wqkv):
        end = begin + source.shape[1]
        pairs.append((source, packed.at[:, begin:end]))
        begin = end
    copies = [pltpu.make_async_copy(a, b, sems.at[i]) for i, (a, b) in enumerate(pairs)]
    for copy in copies:
        copy.start()
    for copy in copies[:4]:
        copy.wait()
    heads = cross_temp.shape[0]
    factor = LOG2E / math.sqrt(width // heads)
    lanes = scale_ref.shape[1]
    for side, temp in enumerate((cross_held, self_held)):
        for head in range(heads):
            at = pl.ds(side * heads + head, 1)
            scale_ref[at, :] = jnp.full((1, lanes), temp[head] * factor, jnp.float32)
    count_ref[...] = jnp.full(count_ref.shape, counts[0], jnp.int32)
    x = x_ref[...].astype(jnp.float32)
    qc_ref[...] = dot(rms_round(x), wq_held[...]).astype(jnp.bfloat16)
    for copy in copies[4:]:
        copy.wait()
    wvt_ref[...] = jnp.transpose(packed[:, -width:])
    wqt_ref[...] = jnp.transpose(packed[:, -3 * width : -2 * width])


def cross_kernel(n, block, tile, heads, scales, counts, queries, qc, *refs):
    pieces = refs[:n]
    packed, wvt, x1_ref, hn_ref, kv_ref, kbd, vbd = refs[n:]
    rows, width = queries.shape
    wkv = packed[:, : 2 * width]
    wo = packed[:, 2 * width : 3 * width]
    wk = packed[:, 4 * width : 5 * width]
    tokens, flags = [], []
    for piece in pieces:
        held = piece[...].astype(jnp.float32)
        dead = held >= DEAD
        for begin in range(0, held.shape[0], tile):
            part = held[begin : begin + tile]
            gone = dead[begin : begin + tile]
            tokens.append(jnp.where(gone, part[:1], part).astype(jnp.bfloat16))
            flags.append(jnp.where(gone, 0.0, 1.0).astype(jnp.bfloat16))
    tokens = jnp.concatenate(tokens, axis=0)
    flags = jnp.concatenate(flags, axis=0)
    count = tokens.shape[0]
    kvm = dot(tokens, wkv).astype(jnp.bfloat16)
    keys = kvm[:, :width]
    values = kvm[:, width:] * flags
    lane_head = head_of_lane(count, width, heads)
    for head in range(heads):
        at = pl.ds(head * count, count)
        kbd[at, :] = only(keys, head, lane_head)
        vbd[at, :] = flagged(values, flags, head, heads, lane_head)
    middle = heads // 2 * count
    for begin in range(0, rows, block):
        at = pl.ds(begin, block)
        x = queries[at, :].astype(jnp.float32)
        scores = dot_t(qc[at, :], kbd[...])
        weights = []
        for head in range(heads):
            s = scores[:, head * count : (head + 1) * count]
            top = jnp.max(s, axis=-1, keepdims=True)
            weights.append(weigh(s, top, scales[head : head + 1, :1]))
        low = dot(jnp.concatenate(weights[: heads // 2], axis=1), vbd[:middle, :])
        high = dot(jnp.concatenate(weights[heads // 2 :], axis=1), vbd[middle:, :])
        x1 = x + dot(normed(low, high), wo)
        x1_ref[at, :] = x1
        hn1 = rms_round(x1)
        hn_ref[at, :] = hn1
        key = dot(hn1, wk).astype(jnp.bfloat16)
        slot = lax.broadcasted_iota(jnp.int32, (block, width), 0) + begin
        if begin == 0:
            first = key[:1]
        kv_ref[at, :] = jnp.where(slot < counts[:1, :1], key, first)
        value = dot_t(wvt[...], hn1).astype(jnp.bfloat16)
        slot = lax.broadcasted_iota(jnp.int32, (width, block), 1) + begin
        value = jnp.where(slot < counts[:1, :1], value, jnp.bfloat16(DEAD_V))
        for part in range(0, block, width):
            place = begin + part
            size = min(block, width)
            target = pl.ds(rows + place // width * width, width)
            lanes = pl.ds(place % width, size)
            kv_ref[target, lanes] = value[:, part : part + size]


def transposed_values(kv, vt, heads):
    rows, width = vt.shape[1], kv.shape[1]
    hsize, part = width // heads, vt.shape[0] // heads
    for begin in range(0, rows, width):
        lanes = pl.ds(begin, width)
        values = kv[rows + begin : rows + begin + width, :]
        live = values < jnp.bfloat16(DEAD_V)
        flags = jnp.where(live[: part - hsize], jnp.bfloat16(1), jnp.bfloat16(0))
        values = jnp.where(live, values, jnp.bfloat16(0))
        for head in range(heads):
            at = head * part
            vt[at : at + hsize, lanes] = values[head * hsize : (head + 1) * hsize]
            vt[at + hsize : at + part, lanes] = flags


def head_rows(width, heads, lanes):
    row = lax.broadcasted_iota(jnp.int32, (width, lanes), 0) // (width // heads)
    lane = lax.broadcasted_iota(jnp.int32, (width, lanes), 1)
    return jnp.where(row == lane, 1.0, 0.0).astype(jnp.bfloat16)


def key_sizes(keys, heads, lanes):
    wide = keys.astype(jnp.float32)
    norms = dot((wide * wide).astype(jnp.bfloat16), head_rows(keys.shape[1], heads, lanes))
    return jnp.max(norms, axis=0, keepdims=True)


def query_sizes(q, scales, heads):
    hsize = q.shape[0] // heads
    lane = lax.broadcasted_iota(jnp.int32, (1, scales.shape[1]), 1)
    sizes = jnp.zeros((1, scales.shape[1]), jnp.float32)
    for head in range(heads):
        part = q[head * hsize : (head + 1) * hsize].astype(jnp.float32)
        norm = jnp.max(jnp.sum(part * part, axis=0, keepdims=True), axis=1, keepdims=True)
        scale = scales[heads + head : heads + head + 1, :]
        sizes = jnp.where(lane == head, norm * scale * scale, sizes)
    return sizes


def half_attention(scales, qt, kv, vt, heads, s_held, p_held, sizes, use):
    rows, width = vt.shape[1], kv.shape[1]
    part = vt.shape[0] // heads
    depth = qt.shape[0] // heads
    per = heads * depth // width
    block = s_held.shape[2]
    units = [(head, begin) for head in range(heads) for begin in range(0, rows, block)]
    bounds = sizes * key_sizes(kv[:rows, :], heads, sizes.shape[1])
    small = jnp.max(bounds) <= LIMIT * LIMIT

    def score(unit):
        head, begin = units[unit]
        lanes = head // per * depth
        q = qt[head * depth : (head + 1) * depth, begin : begin + block]
        return dot(kv[:rows, lanes : lanes + depth], q)

    def scale_of(unit):
        head = units[unit][0]
        return scales[heads + head : heads + head + 1, :1]

    def mix(unit, top):
        head, begin = units[unit]
        total = dot(vt[head * part : (head + 1) * part, :], p_held[unit % 2])
        use(head, pl.ds(begin, block), top, total)

    @pl.when(small)
    def unshifted():
        zero = jnp.zeros((1, block), jnp.float32)
        for step in range(len(units) + 1):
            if step < len(units):
                p_held[step % 2] = jnp.exp2(score(step) * scale_of(step)).astype(jnp.bfloat16)
            if 0 <= step - 1:
                mix(step - 1, zero)

    @pl.when(jnp.logical_not(small))
    def shifted():
        tops = {}
        for step in range(len(units) + 2):
            if step < len(units):
                s = score(step)
                s_held[step % 2] = s
                tops[step] = jnp.max(s, axis=0, keepdims=True)
            last = step - 1
            if 0 <= last < len(units):
                p_held[last % 2] = weigh(s_held[last % 2], tops[last], scale_of(last))
            if 0 <= step - 2:
                mix(step - 2, tops[step - 2])


def own_kernel(
    heads, scales, hn, kv, wqt, qt, top_ref, sum_ref, size_ref, vt, s_held, p_held
):
    width = hn.shape[1]
    hsize = width // heads
    depth = qt.shape[0] // heads
    part = vt.shape[0] // heads
    q = dot_t(wqt[...], hn[...]).astype(jnp.bfloat16)
    sizes = query_sizes(q, scales, heads)
    size_ref[...] = jnp.broadcast_to(sizes, size_ref.shape)
    qt[...] = jnp.zeros_like(qt)
    for head in range(heads):
        begin = head * hsize
        at = head * depth + begin % depth
        qt[at : at + hsize, :] = q[begin : begin + hsize]
    transposed_values(kv, vt, heads)

    def use(head, at, top, total):
        top_ref[head : head + 1, at] = top
        sum_ref[head * part : (head + 1) * part, at] = total

    half_attention(scales, qt, kv, vt, heads, s_held, p_held, sizes, use)


def rest_kernel(
    heads,
    scales,
    counts,
    x1_ref,
    kv,
    qt,
    top_ref,
    sum_ref,
    size_ref,
    wo,
    up,
    down,
    w1,
    w2,
    w3,
    features,
    boxes,
    vt,
    s_held,
    p_held,
    ctx,
    out,
    upper,
    wo_held,
    up_held,
    down_held,
    w1_held,
    w2_held,
    w3_held,
    sems,
):
    rows, width = x1_ref.shape
    hsize = width // heads
    part = vt.shape[0] // heads
    held = (wo_held, up_held, down_held, w1_held, w2_held, w3_held)
    pairs = zip((wo, up, down, w1, w2, w3), held)
    copies = [pltpu.make_async_copy(a, b, sems.at[i]) for i, (a, b) in enumerate(pairs)]
    for copy in copies:
        copy.start()
    transposed_values(kv, vt, heads)

    def use(head, at, top, total):
        scale = scales[heads + head : heads + head + 1, :1]
        first = top_ref[head : head + 1, at]
        most = jnp.maximum(first, top)
        total = total * jnp.exp2((top - most) * scale)
        total += sum_ref[head * part : (head + 1) * part, at] * jnp.exp2((first - most) * scale)
        mixed = total[:hsize] / total[hsize : hsize + 1]
        ctx[head * hsize : (head + 1) * hsize, at] = mixed.astype(jnp.bfloat16)

    half_attention(scales, qt, kv, vt, heads, s_held, p_held, size_ref[:1, :], use)
    for copy in copies:
        copy.wait()
    block = upper.shape[1]
    starts = list(range(0, rows, block))
    ff = up_held.shape[1]
    chunk = ff // 4
    x2, x3, leaves = {}, {}, []

    def project(i):
        at = pl.ds(starts[i], block)
        mixed = lax.dot_general(
            ctx[:, at], wo_held[...], (((0,), (0,)), ((), ())), preferred_element_type=jnp.float32
        )
        x2[i] = x1_ref[at, :] + mixed

    def widen(i):
        hn2 = rms_round(x2[i])
        for begin in range(0, ff, chunk):
            cut = pl.ds(begin, chunk)
            upper[i % 2, :, cut] = jnp.maximum(dot(hn2, up_held[:, cut]), 0.0).astype(jnp.bfloat16)

    def narrow(i):
        at = pl.ds(starts[i], block)
        x3[i] = x2[i] + dot(upper[i % 2], down_held[...])
        slot = lax.broadcasted_iota(jnp.int32, (block, width), 0) + starts[i]
        out[at, :] = jnp.where(slot < counts[:1, :1], x3[i], 0.0)
        leaves.append(
            pltpu.make_async_copy(out.at[at, :], features.at[at, :], sems.at[len(copies) + i])
        )
        leaves[-1].start()

    def box(i):
        b1 = jnp.maximum(dot(rms_round(x3[i]), w1_held[...]), 0.0).astype(jnp.bfloat16)
        b2 = jnp.maximum(dot(b1, w2_held[...]), 0.0).astype(jnp.bfloat16)
        raw = dot_t(w3_held[...], b2)
        slot = lax.broadcasted_iota(jnp.int32, raw.shape, 1) + starts[i]
        boxes[:, pl.ds(starts[i], block)] = jnp.where(
            slot < counts[:1, :1], 1.0 / (1.0 + jnp.exp(-raw)), 0.0
        )

    for step in range(len(starts) + 3):
        for stage, work in enumerate((project, widen, narrow, box)):
            if 0 <= step - stage < len(starts):
                work(step - stage)
    for leave in leaves:
        leave.wait()


def in_hbm(x):
    return pltpu.with_memory_space_constraint(x, pltpu.HBM)


def swap(x, axis):
    size = lax.axis_size(axis)
    return lax.ppermute(x, axis, [(i, i ^ 1) for i in range(size)])


def local(
    queries,
    counts,
    memory,
    mem_mask,
    cross_wq,
    cross_wkv,
    cross_wo,
    self_wqkv,
    self_wo,
    ffn_up,
    ffn_down,
    box_w1,
    box_w2,
    box_w3,
    cross_temp,
    self_temp,
):
    rows, width = queries.shape
    heads = cross_temp.shape[0]
    tile = memory.shape[0]
    params = pltpu.CompilerParams(vmem_limit_bytes=32 * 2**20)
    marked = pl.pallas_call(
        mark_kernel,
        out_shape=pltpu.VMEM((lax.axis_size("row"), tile, width), memory.dtype),
        in_specs=[HBM, HBM],
        out_specs=VMEM,
        scratch_shapes=[
            pltpu.VMEM(memory.shape, memory.dtype),
            pltpu.SMEM(mem_mask.shape, mem_mask.dtype),
            pltpu.SemaphoreType.DMA((2,)),
        ],
        name="mark",
    )(in_hbm(memory), in_hbm(mem_mask))
    gathered = lax.all_to_all(marked, "row", 0, 0, tiled=True)
    pieces = [gathered.reshape(-1, width)]
    tokens = pltpu.VMEM((rows, width), jnp.bfloat16)
    packed_width = cross_wkv.shape[1] + cross_wo.shape[1] + self_wqkv.shape[1]
    sources = (queries, cross_wq, cross_temp, self_temp, cross_wkv, cross_wo, self_wqkv)
    x, qc, scales, live, packed, wvt, wqt = pl.pallas_call(
        load_kernel,
        out_shape=[
            tokens,
            tokens,
            pltpu.VMEM((2 * heads, 128), jnp.float32),
            pltpu.VMEM((8, 128), jnp.int32),
            pltpu.VMEM((width, packed_width), jnp.bfloat16),
            pltpu.VMEM((width, width), jnp.bfloat16),
            pltpu.VMEM((width, width), jnp.bfloat16),
        ],
        in_specs=[SMEM] + [HBM] * len(sources),
        out_specs=[VMEM] * 7,
        scratch_shapes=[
            pltpu.VMEM(cross_wq.shape, cross_wq.dtype),
            pltpu.SMEM(cross_temp.shape, cross_temp.dtype),
            pltpu.SMEM(self_temp.shape, self_temp.dtype),
            pltpu.SemaphoreType.DMA((len(sources),)),
        ],
        compiler_params=params,
        cost_estimate=pl.CostEstimate(
            flops=2 * rows * width * width, bytes_accessed=4 * 2**20, transcendentals=0
        ),
        name="load",
    )(counts, *map(in_hbm, sources))
    count = sum(piece.shape[0] for piece in pieces)
    block = rows if count <= 128 else min(rows, 128)
    kv_shape = pltpu.VMEM((2 * rows, width), jnp.bfloat16)
    x1, hn, kv = pl.pallas_call(
        functools.partial(cross_kernel, len(pieces), block, tile, heads),
        out_shape=(pltpu.VMEM((rows, width), jnp.float32), tokens, kv_shape),
        in_specs=[VMEM] * (6 + len(pieces)),
        out_specs=(VMEM, VMEM, VMEM),
        scratch_shapes=[
            pltpu.VMEM((heads * count, width), jnp.bfloat16),
            pltpu.VMEM((heads * count, width), jnp.bfloat16),
        ],
        compiler_params=params,
        name="cross",
    )(scales, live, x, qc, *pieces, packed, wvt)
    other = swap(kv, "col")
    part = width // heads + 16
    depth = min(128, width)
    block = min(256, rows)
    held = [
        pltpu.VMEM((heads * part, rows), jnp.bfloat16),
        pltpu.VMEM((2, rows, block), jnp.float32),
        pltpu.VMEM((2, rows, block), jnp.bfloat16),
    ]
    qt, tops, sums, sizes = pl.pallas_call(
        functools.partial(own_kernel, heads),
        out_shape=(
            pltpu.VMEM((heads * depth, rows), jnp.bfloat16),
            pltpu.VMEM((heads, rows), jnp.float32),
            pltpu.VMEM((heads * part, rows), jnp.float32),
            pltpu.VMEM((8, 128), jnp.float32),
        ),
        in_specs=[VMEM] * 4,
        out_specs=(VMEM, VMEM, VMEM, VMEM),
        scratch_shapes=held,
        compiler_params=params,
        cost_estimate=pl.CostEstimate(
            flops=8 * heads * rows * rows * width, bytes_accessed=2**20, transcendentals=0
        ),
        name="own",
    )(scales, hn, kv, wqt)
    late = (self_wo, ffn_up, ffn_down, box_w1, box_w2, jnp.transpose(box_w3))
    return pl.pallas_call(
        functools.partial(rest_kernel, heads),
        out_shape=(
            jax.ShapeDtypeStruct((rows, width), jnp.float32),
            jax.ShapeDtypeStruct((box_w3.shape[1], rows), jnp.float32),
        ),
        in_specs=[VMEM] * 8 + [HBM] * len(late),
        out_specs=(HBM, VMEM),
        scratch_shapes=held
        + [
            pltpu.VMEM((width, rows), jnp.bfloat16),
            pltpu.VMEM((rows, width), jnp.float32),
            pltpu.VMEM((2, block, ffn_up.shape[1]), jnp.bfloat16),
        ]
        + [pltpu.VMEM(w.shape, w.dtype) for w in late]
        + [pltpu.SemaphoreType.DMA((len(late) + rows // block,))],
        compiler_params=params,
        name="rest",
    )(scales, live, x1, other, qt, tops, sums, sizes, *map(in_hbm, late))


def solution(mesh):
    return jax.shard_map(
        local,
        mesh=mesh,
        in_specs=(
            P(("parts", "row", "col"), None),
            P(("parts", "row", "col")),
            P(("parts", "row", "col"), None),
            P(("parts", "row", "col")),
            P(),
            P(),
            P(),
            P(),
            P(),
            P(),
            P(),
            P(),
            P(),
            P(),
            P(),
            P(),
        ),
        out_specs=(P(("parts", "row", "col"), None), P(None, ("parts", "row", "col"))),
        check_vma=False,
    )
```

```python
import functools
import math

import jax
import jax.numpy as jnp
from jax import lax
from jax.experimental import pallas as pl
from jax.experimental.pallas import tpu as pltpu
from jax.sharding import PartitionSpec as P

EPS = 1e-06
DEAD = 64.0
DEAD_V = 4096.0
LOG2E = math.log2(math.e)
LIMIT = 100.0
VMEM = pl.BlockSpec(memory_space=pltpu.VMEM)
SMEM = pl.BlockSpec(memory_space=pltpu.SMEM)
HBM = pl.BlockSpec(memory_space=pltpu.HBM)


def rms_round(x):
    return (x * lax.rsqrt(jnp.mean(x * x, axis=-1, keepdims=True) + EPS)).astype(jnp.bfloat16)


def dot(a, b):
    return jnp.dot(a, b, preferred_element_type=jnp.float32)


def dot_t(a, b):
    return lax.dot_general(a, b, (((1,), (1,)), ((), ())), preferred_element_type=jnp.float32)


def dot_l(a, b):
    return lax.dot_general(a, b, (((0,), (0,)), ((), ())), preferred_element_type=jnp.float32)


def weigh(scores, top, scale):
    return jnp.exp2((scores - top) * scale).astype(jnp.bfloat16)


def mark_kernel(memory, mask, out, held, flags, sems):
    copies = [
        pltpu.make_async_copy(memory, held, sems.at[0]),
        pltpu.make_async_copy(mask, flags, sems.at[1]),
    ]
    for copy in copies:
        copy.start()
    for copy in copies:
        copy.wait()
    row = lax.broadcasted_iota(jnp.int32, held.shape, 0)
    tokens = held[...].astype(jnp.float32)
    for j in range(held.shape[0]):
        tokens = jnp.where((row == j) & (flags[j] <= 0), DEAD, tokens)
    tokens = tokens.astype(jnp.bfloat16)
    for copy in range(out.shape[0]):
        out[copy] = tokens


def spread(qt, q, heads):
    depth = qt.shape[0] // heads
    hsize = q.shape[0] // heads
    qt[...] = jnp.zeros_like(qt)
    for head in range(heads):
        begin = head * hsize
        at = head * depth + begin % depth
        qt[at : at + hsize, :] = q[begin : begin + hsize]


def load_kernel(
    counts,
    queries,
    wq,
    cross_temp,
    self_temp,
    wkv,
    wo,
    wqkv,
    x_ref,
    qt_ref,
    scale_ref,
    count_ref,
    packed,
    turned,
    wq_held,
    cross_held,
    self_held,
    sems,
):
    width = x_ref.shape[1]
    pairs = [(queries, x_ref), (wq, wq_held), (cross_temp, cross_held), (self_temp, self_held)]
    begin = 0
    for source in (wkv, wo, wqkv):
        end = begin + source.shape[1]
        pairs.append((source, packed.at[:, begin:end]))
        begin = end
    copies = [pltpu.make_async_copy(a, b, sems.at[i]) for i, (a, b) in enumerate(pairs)]
    for copy in copies:
        copy.start()
    for copy in copies[:4]:
        copy.wait()
    heads = cross_temp.shape[0]
    factor = LOG2E / math.sqrt(width // heads)
    lanes = scale_ref.shape[1]
    for side, temp in enumerate((cross_held, self_held)):
        for head in range(heads):
            at = pl.ds(side * heads + head, 1)
            scale_ref[at, :] = jnp.full((1, lanes), temp[head] * factor, jnp.float32)
    count_ref[...] = jnp.full(count_ref.shape, counts[0], jnp.int32)
    hn0 = rms_round(x_ref[...].astype(jnp.float32))
    spread(qt_ref, dot_t(jnp.transpose(wq_held[...]), hn0).astype(jnp.bfloat16), heads)
    for copy in copies[4:]:
        copy.wait()
    for place, begin in enumerate((width, 3 * width, 5 * width)):
        turned[place] = jnp.transpose(packed[:, begin : begin + width])


def cross_kernel(tile, heads, scales, counts, queries, qt, tokens, packed, turned, *refs):
    x1_ref, hn_ref, kv_ref, vt, ctx = refs
    rows, width = queries.shape
    hsize = width // heads
    part = vt.shape[0] // heads
    depth = qt.shape[0] // heads
    per = heads * depth // width
    held = tokens[...].astype(jnp.float32)
    dead = held >= DEAD
    alive = jnp.where(dead, 0.0, held).astype(jnp.bfloat16)
    flags = jnp.where(dead, 0.0, 1.0).astype(jnp.bfloat16)
    filled = []
    for begin in range(0, held.shape[0], tile):
        piece = held[begin : begin + tile]
        filled.append(jnp.where(dead[begin : begin + tile], piece[:1], piece))
    filled = jnp.concatenate(filled, axis=0).astype(jnp.bfloat16)
    keys = dot(filled, packed[:, :width]).astype(jnp.bfloat16)
    values = dot_t(turned[0], alive).astype(jnp.bfloat16)
    first = jnp.where(lax.broadcasted_iota(jnp.int32, (part - hsize, width), 1) == 0, 1.0, 0.0)
    flags = dot_t(first.astype(jnp.bfloat16), flags).astype(jnp.bfloat16)
    for head in range(heads):
        at = head * part
        vt[at : at + hsize, :] = values[head * hsize : (head + 1) * hsize]
        vt[at + hsize : at + part, :] = flags
    for head in range(heads):
        lanes = head // per * depth
        s = dot(keys[:, lanes : lanes + depth], qt[head * depth : (head + 1) * depth, :])
        top = jnp.max(s, axis=0, keepdims=True)
        weights = weigh(s, top, scales[head : head + 1, :1])
        total = dot(vt[head * part : (head + 1) * part, :], weights)
        mixed = total[:hsize] * (1.0 / total[hsize : hsize + 1])
        ctx[head * hsize : (head + 1) * hsize, :] = mixed.astype(jnp.bfloat16)
    x1 = queries[...].astype(jnp.float32) + dot_l(ctx[...], packed[:, 2 * width : 3 * width])
    x1_ref[...] = x1
    hn1 = rms_round(x1)
    hn_ref[...] = hn1
    key = dot(hn1, packed[:, 4 * width : 5 * width]).astype(jnp.bfloat16)
    slot = lax.broadcasted_iota(jnp.int32, (rows, width), 0)
    kv_ref[:rows, :] = jnp.where(slot < counts[:1, :1], key, key[:1])
    value = dot_t(turned[2], hn1).astype(jnp.bfloat16)
    slot = lax.broadcasted_iota(jnp.int32, (width, rows), 1)
    value = jnp.where(slot < counts[:1, :1], value, jnp.bfloat16(DEAD_V))
    for begin in range(0, rows, width):
        kv_ref[rows + begin : rows + begin + width, :] = value[:, begin : begin + width]


def transposed_values(kv, vt, heads):
    rows, width = vt.shape[1], kv.shape[1]
    hsize, part = width // heads, vt.shape[0] // heads
    for begin in range(0, rows, width):
        lanes = pl.ds(begin, width)
        values = kv[rows + begin : rows + begin + width, :]
        live = values < jnp.bfloat16(DEAD_V)
        flags = jnp.where(live[: part - hsize], jnp.bfloat16(1), jnp.bfloat16(0))
        values = jnp.where(live, values, jnp.bfloat16(0))
        for head in range(heads):
            at = head * part
            vt[at : at + hsize, lanes] = values[head * hsize : (head + 1) * hsize]
            vt[at + hsize : at + part, lanes] = flags


def largest(q, heads, q_axis):
    width = q.shape[1 - q_axis]
    head = lax.broadcasted_iota(jnp.int32, (16, width), 0)
    lane = lax.broadcasted_iota(jnp.int32, (16, width), 1) // (width // heads)
    mine = jnp.where(head == lane, 1.0, 0.0).astype(jnp.bfloat16)
    wide = q.astype(jnp.float32)
    square = (wide * wide).astype(jnp.bfloat16)
    return jnp.max((dot if q_axis else dot_t)(mine, square), axis=1, keepdims=True)


def half_attention(scales, qt, kv, vt, heads, s_held, p_held, sizes, use):
    rows, width = vt.shape[1], kv.shape[1]
    part = vt.shape[0] // heads
    depth = qt.shape[0] // heads
    per = heads * depth // width
    block = s_held.shape[2]
    units = [(head, begin) for head in range(heads) for begin in range(0, rows, block)]
    small = jnp.max(sizes * largest(kv[:rows, :], heads, 0)[:heads]) <= LIMIT * LIMIT

    def score(unit):
        head, begin = units[unit]
        lanes = head // per * depth
        q = qt[head * depth : (head + 1) * depth, begin : begin + block]
        return dot(kv[:rows, lanes : lanes + depth], q)

    def scale_of(unit):
        head = units[unit][0]
        return scales[heads + head : heads + head + 1, :1]

    def mix(unit, top):
        head, begin = units[unit]
        total = dot(vt[head * part : (head + 1) * part, :], p_held[unit % 2])
        use(head, pl.ds(begin, block), top, total)

    @pl.when(small)
    def unshifted():
        zero = jnp.zeros((1, block), jnp.float32)
        for step in range(len(units) + 1):
            if step < len(units):
                p_held[step % 2] = jnp.exp2(score(step) * scale_of(step)).astype(jnp.bfloat16)
            if 0 <= step - 1:
                mix(step - 1, zero)

    @pl.when(jnp.logical_not(small))
    def shifted():
        tops = {}
        for step in range(len(units) + 2):
            if step < len(units):
                s = score(step)
                s_held[step % 2] = s
                tops[step] = jnp.max(s, axis=0, keepdims=True)
            last = step - 1
            if 0 <= last < len(units):
                p_held[last % 2] = weigh(s_held[last % 2], tops[last], scale_of(last))
            if 0 <= step - 2:
                mix(step - 2, tops[step - 2])


def own_kernel(
    heads, scales, hn, kv, turned, qt, top_ref, sum_ref, size_ref, vt, s_held, p_held
):
    part = vt.shape[0] // heads
    q = dot_t(turned[1], hn[...]).astype(jnp.bfloat16)
    scale = scales[heads : 2 * heads, :]
    sizes = largest(q, heads, 1)[:heads] * (scale * scale)
    size_ref[...] = sizes
    spread(qt, q, heads)
    transposed_values(kv, vt, heads)

    def use(head, at, top, total):
        top_ref[head : head + 1, at] = top
        sum_ref[head * part : (head + 1) * part, at] = total

    half_attention(scales, qt, kv, vt, heads, s_held, p_held, sizes, use)


def rest_kernel(
    heads,
    scales,
    counts,
    x1_ref,
    kv,
    qt,
    top_ref,
    sum_ref,
    size_ref,
    wo,
    up,
    down,
    w1,
    w2,
    w3,
    features,
    boxes,
    vt,
    s_held,
    p_held,
    ctx,
    out,
    upper,
    wo_held,
    up_held,
    down_held,
    w1_held,
    w2_held,
    w3_held,
    sems,
):
    rows, width = x1_ref.shape
    hsize = width // heads
    part = vt.shape[0] // heads
    held = (wo_held, up_held, down_held, w1_held, w2_held, w3_held)
    pairs = zip((wo, up, down, w1, w2, w3), held)
    copies = [pltpu.make_async_copy(a, b, sems.at[i]) for i, (a, b) in enumerate(pairs)]
    for copy in copies:
        copy.start()
    transposed_values(kv, vt, heads)

    def use(head, at, top, total):
        scale = scales[heads + head : heads + head + 1, :1]
        first = top_ref[head : head + 1, at]
        most = jnp.maximum(first, top)
        total = total * jnp.exp2((top - most) * scale)
        total += sum_ref[head * part : (head + 1) * part, at] * jnp.exp2((first - most) * scale)
        mixed = total[:hsize] * (1.0 / total[hsize : hsize + 1])
        ctx[head * hsize : (head + 1) * hsize, at] = mixed.astype(jnp.bfloat16)

    half_attention(scales, qt, kv, vt, heads, s_held, p_held, size_ref[...], use)
    for copy in copies:
        copy.wait()
    block = upper.shape[1]
    starts = list(range(0, rows, block))
    ff = up_held.shape[1]
    chunk = ff // 4
    x2, x3 = {}, {}
    leave = pltpu.make_async_copy(out, features, sems.at[len(copies)])

    def project(i):
        at = pl.ds(starts[i], block)
        x2[i] = x1_ref[at, :] + dot_l(ctx[:, at], wo_held[...])

    def widen(i):
        hn2 = rms_round(x2[i])
        for begin in range(0, ff, chunk):
            cut = pl.ds(begin, chunk)
            upper[i % 2, :, cut] = jnp.maximum(dot(hn2, up_held[:, cut]), 0.0).astype(jnp.bfloat16)

    def narrow(i):
        at = pl.ds(starts[i], block)
        x3[i] = x2[i] + dot(upper[i % 2], down_held[...])
        slot = lax.broadcasted_iota(jnp.int32, (block, width), 0) + starts[i]
        out[at, :] = jnp.where(slot < counts[:1, :1], x3[i], 0.0)
        if i == len(starts) - 1:
            leave.start()

    def box(i):
        b1 = jnp.maximum(dot(rms_round(x3[i]), w1_held[...]), 0.0).astype(jnp.bfloat16)
        b2 = jnp.maximum(dot(b1, w2_held[...]), 0.0).astype(jnp.bfloat16)
        raw = dot_t(w3_held[...], b2)
        slot = lax.broadcasted_iota(jnp.int32, raw.shape, 1) + starts[i]
        boxes[:, pl.ds(starts[i], block)] = jnp.where(
            slot < counts[:1, :1], 1.0 / (1.0 + jnp.exp(-raw)), 0.0
        )

    for step in range(len(starts) + 3):
        for stage, work in enumerate((project, widen, narrow, box)):
            if 0 <= step - stage < len(starts):
                work(step - stage)
    leave.wait()


def in_hbm(x):
    return pltpu.with_memory_space_constraint(x, pltpu.HBM)


def swap(x, axis):
    size = lax.axis_size(axis)
    return lax.ppermute(x, axis, [(i, i ^ 1) for i in range(size)])


def local(
    queries,
    counts,
    memory,
    mem_mask,
    cross_wq,
    cross_wkv,
    cross_wo,
    self_wqkv,
    self_wo,
    ffn_up,
    ffn_down,
    box_w1,
    box_w2,
    box_w3,
    cross_temp,
    self_temp,
):
    rows, width = queries.shape
    heads = cross_temp.shape[0]
    tile = memory.shape[0]
    params = pltpu.CompilerParams(vmem_limit_bytes=32 * 2**20)
    marked = pl.pallas_call(
        mark_kernel,
        out_shape=pltpu.VMEM((lax.axis_size("row"), tile, width), memory.dtype),
        in_specs=[HBM, HBM],
        out_specs=VMEM,
        scratch_shapes=[
            pltpu.VMEM(memory.shape, memory.dtype),
            pltpu.SMEM(mem_mask.shape, mem_mask.dtype),
            pltpu.SemaphoreType.DMA((2,)),
        ],
        name="mark",
    )(in_hbm(memory), in_hbm(mem_mask))
    gathered = lax.all_to_all(marked, "row", 0, 0, tiled=True)
    gathered = gathered.reshape(-1, width)
    tokens = pltpu.VMEM((rows, width), jnp.bfloat16)
    packed_width = cross_wkv.shape[1] + cross_wo.shape[1] + self_wqkv.shape[1]
    sources = (queries, cross_wq, cross_temp, self_temp, cross_wkv, cross_wo, self_wqkv)
    depth = min(128, width)
    qt_shape = pltpu.VMEM((heads * depth, rows), jnp.bfloat16)
    x, qt, scales, live, packed, turned = pl.pallas_call(
        load_kernel,
        out_shape=[
            tokens,
            qt_shape,
            pltpu.VMEM((2 * heads, 128), jnp.float32),
            pltpu.VMEM((8, 128), jnp.int32),
            pltpu.VMEM((width, packed_width), jnp.bfloat16),
            pltpu.VMEM((3, width, width), jnp.bfloat16),
        ],
        in_specs=[SMEM] + [HBM] * len(sources),
        out_specs=[VMEM] * 6,
        scratch_shapes=[
            pltpu.VMEM(cross_wq.shape, cross_wq.dtype),
            pltpu.SMEM(cross_temp.shape, cross_temp.dtype),
            pltpu.SMEM(self_temp.shape, self_temp.dtype),
            pltpu.SemaphoreType.DMA((len(sources),)),
        ],
        compiler_params=params,
        cost_estimate=pl.CostEstimate(
            flops=2 * rows * width * width, bytes_accessed=4 * 2**20, transcendentals=0
        ),
        name="load",
    )(counts, *map(in_hbm, sources))
    part = width // heads + 16
    x1, hn, kv = pl.pallas_call(
        functools.partial(cross_kernel, tile, heads),
        out_shape=(
            pltpu.VMEM((rows, width), jnp.float32),
            tokens,
            pltpu.VMEM((2 * rows, width), jnp.bfloat16),
        ),
        in_specs=[VMEM] * 7,
        out_specs=(VMEM, VMEM, VMEM),
        scratch_shapes=[
            pltpu.VMEM((heads * part, gathered.shape[0]), jnp.bfloat16),
            pltpu.VMEM((width, rows), jnp.bfloat16),
        ],
        compiler_params=params,
        name="cross",
    )(scales, live, x, qt, gathered, packed, turned)
    other = swap(kv, "col")
    block = min(256, rows)
    held = [
        pltpu.VMEM((heads * part, rows), jnp.bfloat16),
        pltpu.VMEM((2, rows, block), jnp.float32),
        pltpu.VMEM((2, rows, block), jnp.bfloat16),
    ]
    qt, tops, sums, sizes = pl.pallas_call(
        functools.partial(own_kernel, heads),
        out_shape=(
            qt_shape,
            pltpu.VMEM((heads, rows), jnp.float32),
            pltpu.VMEM((heads * part, rows), jnp.float32),
            pltpu.VMEM((heads, 128), jnp.float32),
        ),
        in_specs=[VMEM] * 4,
        out_specs=(VMEM, VMEM, VMEM, VMEM),
        scratch_shapes=held,
        compiler_params=params,
        cost_estimate=pl.CostEstimate(
            flops=8 * heads * rows * rows * width, bytes_accessed=2**20, transcendentals=0
        ),
        name="own",
    )(scales, hn, kv, turned)
    late = (self_wo, ffn_up, ffn_down, box_w1, box_w2, jnp.transpose(box_w3))
    return pl.pallas_call(
        functools.partial(rest_kernel, heads),
        out_shape=(
            jax.ShapeDtypeStruct((rows, width), jnp.float32),
            jax.ShapeDtypeStruct((box_w3.shape[1], rows), jnp.float32),
        ),
        in_specs=[VMEM] * 8 + [HBM] * len(late),
        out_specs=(HBM, VMEM),
        scratch_shapes=held
        + [
            pltpu.VMEM((width, rows), jnp.bfloat16),
            pltpu.VMEM((rows, width), jnp.float32),
            pltpu.VMEM((2, block, ffn_up.shape[1]), jnp.bfloat16),
        ]
        + [pltpu.VMEM(w.shape, w.dtype) for w in late]
        + [pltpu.SemaphoreType.DMA((len(late) + 1,))],
        compiler_params=params,
        name="rest",
    )(scales, live, x1, other, qt, tops, sums, sizes, *map(in_hbm, late))


def solution(mesh):
    return jax.shard_map(
        local,
        mesh=mesh,
        in_specs=(
            P(("parts", "row", "col"), None),
            P(("parts", "row", "col")),
            P(("parts", "row", "col"), None),
            P(("parts", "row", "col")),
            P(),
            P(),
            P(),
            P(),
            P(),
            P(),
            P(),
            P(),
            P(),
            P(),
            P(),
            P(),
        ),
        out_specs=(P(("parts", "row", "col"), None), P(None, ("parts", "row", "col"))),
        check_vma=False,
    )
```

```python
import functools
import math

import jax
import jax.numpy as jnp
from jax import lax
from jax.experimental import pallas as pl
from jax.experimental.pallas import tpu as pltpu
from jax.sharding import PartitionSpec as P

EPS = 1e-06
DEAD = 64.0
DEAD_V = 4096.0
LOG2E = math.log2(math.e)
LIMIT = 100.0
VMEM = pl.BlockSpec(memory_space=pltpu.VMEM)
SMEM = pl.BlockSpec(memory_space=pltpu.SMEM)
HBM = pl.BlockSpec(memory_space=pltpu.HBM)


def rms_round(x):
    return (x * lax.rsqrt(jnp.mean(x * x, axis=-1, keepdims=True) + EPS)).astype(jnp.bfloat16)


def dot(a, b):
    return jnp.dot(a, b, preferred_element_type=jnp.float32)


def dot_t(a, b):
    return lax.dot_general(a, b, (((1,), (1,)), ((), ())), preferred_element_type=jnp.float32)


def head_of_lane(rows, width, heads):
    return lax.broadcasted_iota(jnp.int32, (rows, width), 1) // (width // heads)


def only(x, head, lane_head):
    return jnp.where(lane_head == head, x, jnp.zeros_like(x))


def flagged(values, flags, head, heads, lane_head):
    other = (head + heads // 2) % heads
    rest = jnp.where(lane_head == other, flags, jnp.zeros_like(values))
    return jnp.where(lane_head == head, values, rest)


def weigh(scores, top, scale):
    return jnp.exp2((scores - top) * scale).astype(jnp.bfloat16)


def normed(low, high):
    half = low.shape[1] // 2
    return jnp.concatenate(
        [low[:, :half] / low[:, half:], high[:, half:] / high[:, :half]], axis=1
    ).astype(jnp.bfloat16)


def mark_kernel(memory, mask, out, held, flags, sems):
    copies = [
        pltpu.make_async_copy(memory, held, sems.at[0]),
        pltpu.make_async_copy(mask, flags, sems.at[1]),
    ]
    for copy in copies:
        copy.start()
    for copy in copies:
        copy.wait()
    row = lax.broadcasted_iota(jnp.int32, held.shape, 0)
    tokens = held[...].astype(jnp.float32)
    for j in range(held.shape[0]):
        tokens = jnp.where((row == j) & (flags[j] <= 0), DEAD, tokens)
    tokens = tokens.astype(jnp.bfloat16)
    for copy in range(out.shape[0]):
        out[copy] = tokens


def load_kernel(
    counts,
    queries,
    wq,
    cross_temp,
    self_temp,
    wkv,
    wo,
    wqkv,
    x_ref,
    qc_ref,
    scale_ref,
    count_ref,
    packed,
    wq_held,
    cross_held,
    self_held,
    sems,
):
    width = x_ref.shape[1]
    pairs = [(queries, x_ref), (wq, wq_held), (cross_temp, cross_held), (self_temp, self_held)]
    begin = 0
    for source in (wkv, wo, wqkv):
        end = begin + source.shape[1]
        pairs.append((source, packed.at[:, begin:end]))
        begin = end
    copies = [pltpu.make_async_copy(a, b, sems.at[i]) for i, (a, b) in enumerate(pairs)]
    for copy in copies:
        copy.start()
    for copy in copies[:4]:
        copy.wait()
    heads = cross_temp.shape[0]
    factor = LOG2E / math.sqrt(width // heads)
    lanes = scale_ref.shape[1]
    for side, temp in enumerate((cross_held, self_held)):
        for head in range(heads):
            at = pl.ds(side * heads + head, 1)
            scale_ref[at, :] = jnp.full((1, lanes), temp[head] * factor, jnp.float32)
    lane = lax.broadcasted_iota(jnp.int32, (1, lanes), 1)
    squares = jnp.zeros((1, lanes), jnp.float32)
    for head in range(heads):
        scale = self_held[head] * factor
        squares = jnp.where(lane == head, scale * scale, squares)
    scale_ref[2 * heads : 2 * heads + 1, :] = squares
    count_ref[...] = jnp.full(count_ref.shape, counts[0], jnp.int32)
    x = x_ref[...].astype(jnp.float32)
    qc_ref[...] = dot(rms_round(x), wq_held[...]).astype(jnp.bfloat16)
    for copy in copies[4:]:
        copy.wait()


def cross_kernel(n, block, tile, heads, scales, counts, queries, qc, *refs):
    pieces = refs[:n]
    packed, x1_ref, hn_ref, kv_ref, kbd, vbd = refs[n:]
    rows, width = queries.shape
    wkv = packed[:, : 2 * width]
    wo = packed[:, 2 * width : 3 * width]
    wkv_self = packed[:, 4 * width :]
    tokens, flags = [], []
    for piece in pieces:
        held = piece[...].astype(jnp.float32)
        dead = held >= DEAD
        for begin in range(0, held.shape[0], tile):
            part = held[begin : begin + tile]
            gone = dead[begin : begin + tile]
            tokens.append(jnp.where(gone, part[:1], part).astype(jnp.bfloat16))
            flags.append(jnp.where(gone, 0.0, 1.0).astype(jnp.bfloat16))
    tokens = jnp.concatenate(tokens, axis=0)
    flags = jnp.concatenate(flags, axis=0)
    count = tokens.shape[0]
    kvm = dot(tokens, wkv).astype(jnp.bfloat16)
    keys = kvm[:, :width]
    values = kvm[:, width:] * flags
    lane_head = head_of_lane(count, width, heads)
    for head in range(heads):
        at = pl.ds(head * count, count)
        kbd[at, :] = only(keys, head, lane_head)
        vbd[at, :] = flagged(values, flags, head, heads, lane_head)
    middle = heads // 2 * count
    for begin in range(0, rows, block):
        at = pl.ds(begin, block)
        x = queries[at, :].astype(jnp.float32)
        scores = dot_t(qc[at, :], kbd[...])
        weights = []
        for head in range(heads):
            s = scores[:, head * count : (head + 1) * count]
            top = jnp.max(s, axis=-1, keepdims=True)
            weights.append(weigh(s, top, scales[head : head + 1, :1]))
        low = dot(jnp.concatenate(weights[: heads // 2], axis=1), vbd[:middle, :])
        high = dot(jnp.concatenate(weights[heads // 2 :], axis=1), vbd[middle:, :])
        x1 = x + dot(normed(low, high), wo)
        x1_ref[at, :] = x1
        hn1 = rms_round(x1)
        hn_ref[at, :] = hn1
        kv = dot(hn1, wkv_self).astype(jnp.bfloat16)
        slot = lax.broadcasted_iota(jnp.int32, (block, width), 0) + begin
        live = slot < counts[:1, :1]
        key = kv[:, :width]
        if begin == 0:
            first = key[:1]
        kv_ref[at, :width] = jnp.where(live, key, first)
        kv_ref[at, width:] = jnp.where(live, kv[:, width:], jnp.bfloat16(DEAD_V))


def largest(x, heads, lanes):
    width = x.shape[1]
    row = lax.broadcasted_iota(jnp.int32, (width, lanes), 0) // (width // heads)
    lane = lax.broadcasted_iota(jnp.int32, (width, lanes), 1)
    mine = jnp.where(row == lane, 1.0, 0.0).astype(jnp.bfloat16)
    wide = x.astype(jnp.float32)
    return jnp.max(dot((wide * wide).astype(jnp.bfloat16), mine), axis=0, keepdims=True)


def stack_values(kv, vbd, heads):
    rows, width = kv.shape[0], kv.shape[1] // 2
    lane_head = head_of_lane(rows, width, heads)
    values = kv[:, width:]
    live = values < jnp.bfloat16(DEAD_V)
    flags = jnp.where(live, jnp.bfloat16(1), jnp.bfloat16(0))
    values = jnp.where(live, values, jnp.bfloat16(0))
    for head in range(heads):
        vbd[head * rows : (head + 1) * rows, :] = flagged(values, flags, head, heads, lane_head)


def halves(low, high):
    half = low.shape[1] // 2
    mixed = jnp.concatenate([low[:, :half], high[:, half:]], axis=1)
    total = jnp.concatenate([low[:, half:], high[:, :half]], axis=1)
    return mixed, total


def half_attention(scales, qm, kv, vbd, heads, p_held, shift):
    rows, width = kv.shape[0], kv.shape[1] // 2
    depth = qm.shape[1]
    per = heads * depth // width
    group = heads // 2
    lane_head = head_of_lane(rows, width, heads)
    tops = jnp.zeros((rows, width), jnp.float32)
    sums = []
    for head in range(heads):
        lanes = head // per * depth
        s = dot_t(qm[head * rows : (head + 1) * rows, :], kv[:, lanes : lanes + depth])
        scale = scales[heads + head : heads + head + 1, :1]
        at = head % group * rows
        if shift is None:
            weights = jnp.exp2(s * scale).astype(jnp.bfloat16)
        else:
            top = jnp.max(s, axis=1, keepdims=True)
            tops = jnp.where(lane_head == head, top * scale, tops)
            weights = weigh(s, top, scale)
        p_held[head // group, :, at : at + rows] = weights
        if (head + 1) % group == 0:
            mine = vbd[(head + 1 - group) * rows : (head + 1) * rows, :]
            sums.append(dot(p_held[head // group], mine))
    if shift is not None:
        shift[...] = tops
    return halves(*sums)


def own_kernel(
    heads, scales, hn, kv, packed, qm, mixed_ref, total_ref, shift_ref, size_ref, flag_ref, vbd, p_held
):
    rows, width = hn.shape
    depth = qm.shape[1]
    q = dot(hn[...], packed[:, 3 * width : 4 * width]).astype(jnp.bfloat16)
    sizes = largest(q, heads, scales.shape[1]) * scales[2 * heads : 2 * heads + 1, :]
    size_ref[...] = jnp.broadcast_to(sizes, size_ref.shape)
    lane_head = head_of_lane(rows, width, heads)
    for head in range(heads):
        lanes = head // (heads * depth // width) * depth
        mine = only(q, head, lane_head)
        qm[head * rows : (head + 1) * rows, :] = mine[:, lanes : lanes + depth]
    stack_values(kv, vbd, heads)
    small = jnp.max(sizes * largest(kv[:, :width], heads, sizes.shape[1])) <= LIMIT * LIMIT

    @pl.when(small)
    def unshifted():
        mixed_ref[...], total_ref[...] = half_attention(scales, qm, kv, vbd, heads, p_held, None)
        shift_ref[...] = jnp.zeros_like(shift_ref)
        flag_ref[...] = jnp.ones_like(flag_ref)

    @pl.when(jnp.logical_not(small))
    def shifted():
        mixed_ref[...], total_ref[...] = half_attention(
            scales, qm, kv, vbd, heads, p_held, shift_ref
        )
        flag_ref[...] = jnp.zeros_like(flag_ref)


def rest_kernel(
    heads,
    scales,
    counts,
    x1_ref,
    kv,
    qm,
    mixed_ref,
    total_ref,
    shift_ref,
    size_ref,
    flag_ref,
    wo,
    up,
    down,
    w1,
    w2,
    w3,
    features,
    boxes,
    vbd,
    p_held,
    ctx,
    shift,
    out,
    upper,
    wo_held,
    up_held,
    down_held,
    w1_held,
    w2_held,
    w3_held,
    sems,
):
    rows, width = x1_ref.shape
    held = (wo_held, up_held, down_held, w1_held, w2_held, w3_held)
    pairs = zip((wo, up, down, w1, w2, w3), held)
    copies = [pltpu.make_async_copy(a, b, sems.at[i]) for i, (a, b) in enumerate(pairs)]
    for copy in copies:
        copy.start()
    stack_values(kv, vbd, heads)
    bounds = size_ref[:1, :] * largest(kv[:, :width], heads, size_ref.shape[1])
    bounds = jnp.where(flag_ref[:1, :] > 0.0, bounds, 2.0 * LIMIT * LIMIT)
    small = jnp.max(bounds) <= LIMIT * LIMIT

    @pl.when(small)
    def unshifted():
        mixed, total = half_attention(scales, qm, kv, vbd, heads, p_held, None)
        total = total + total_ref[...]
        ctx[...] = ((mixed + mixed_ref[...]) * (1.0 / total)).astype(jnp.bfloat16)

    @pl.when(jnp.logical_not(small))
    def shifted():
        mixed, total = half_attention(scales, qm, kv, vbd, heads, p_held, shift)
        most = jnp.maximum(shift[...], shift_ref[...])
        mine, theirs = jnp.exp2(shift_ref[...] - most), jnp.exp2(shift[...] - most)
        total = total * theirs + total_ref[...] * mine
        ctx[...] = ((mixed * theirs + mixed_ref[...] * mine) / total).astype(jnp.bfloat16)

    for copy in copies:
        copy.wait()
    block = upper.shape[1]
    starts = list(range(0, rows, block))
    ff = up_held.shape[1]
    chunk = ff // 4
    x2, x3 = {}, {}
    leave = pltpu.make_async_copy(out, features, sems.at[len(copies)])

    def project(i):
        at = pl.ds(starts[i], block)
        x2[i] = x1_ref[at, :] + dot(ctx[at, :], wo_held[...])

    def widen(i):
        hn2 = rms_round(x2[i])
        for begin in range(0, ff, chunk):
            cut = pl.ds(begin, chunk)
            upper[i % 2, :, cut] = jnp.maximum(dot(hn2, up_held[:, cut]), 0.0).astype(jnp.bfloat16)

    def narrow(i):
        at = pl.ds(starts[i], block)
        x3[i] = x2[i] + dot(upper[i % 2], down_held[...])
        slot = lax.broadcasted_iota(jnp.int32, (block, width), 0) + starts[i]
        out[at, :] = jnp.where(slot < counts[:1, :1], x3[i], 0.0)
        if i == len(starts) - 1:
            leave.start()

    def box(i):
        b1 = jnp.maximum(dot(rms_round(x3[i]), w1_held[...]), 0.0).astype(jnp.bfloat16)
        b2 = jnp.maximum(dot(b1, w2_held[...]), 0.0).astype(jnp.bfloat16)
        raw = dot_t(w3_held[...], b2)
        slot = lax.broadcasted_iota(jnp.int32, raw.shape, 1) + starts[i]
        boxes[:, pl.ds(starts[i], block)] = jnp.where(
            slot < counts[:1, :1], 1.0 / (1.0 + jnp.exp(-raw)), 0.0
        )

    for step in range(len(starts) + 3):
        for stage, work in enumerate((project, widen, narrow, box)):
            if 0 <= step - stage < len(starts):
                work(step - stage)
    leave.wait()


def in_hbm(x):
    return pltpu.with_memory_space_constraint(x, pltpu.HBM)


def swap(x, axis):
    size = lax.axis_size(axis)
    return lax.ppermute(x, axis, [(i, i ^ 1) for i in range(size)])


def local(
    queries,
    counts,
    memory,
    mem_mask,
    cross_wq,
    cross_wkv,
    cross_wo,
    self_wqkv,
    self_wo,
    ffn_up,
    ffn_down,
    box_w1,
    box_w2,
    box_w3,
    cross_temp,
    self_temp,
):
    rows, width = queries.shape
    heads = cross_temp.shape[0]
    tile = memory.shape[0]
    params = pltpu.CompilerParams(vmem_limit_bytes=32 * 2**20)
    marked = pl.pallas_call(
        mark_kernel,
        out_shape=pltpu.VMEM((lax.axis_size("row"), tile, width), memory.dtype),
        in_specs=[HBM, HBM],
        out_specs=VMEM,
        scratch_shapes=[
            pltpu.VMEM(memory.shape, memory.dtype),
            pltpu.SMEM(mem_mask.shape, mem_mask.dtype),
            pltpu.SemaphoreType.DMA((2,)),
        ],
        name="mark",
    )(in_hbm(memory), in_hbm(mem_mask))
    gathered = lax.all_to_all(marked, "row", 0, 0, tiled=True)
    pieces = [gathered.reshape(-1, width)]
    tokens = pltpu.VMEM((rows, width), jnp.bfloat16)
    packed_width = cross_wkv.shape[1] + cross_wo.shape[1] + self_wqkv.shape[1]
    sources = (queries, cross_wq, cross_temp, self_temp, cross_wkv, cross_wo, self_wqkv)
    x, qc, scales, live, packed = pl.pallas_call(
        load_kernel,
        out_shape=[
            tokens,
            tokens,
            pltpu.VMEM((3 * heads, 128), jnp.float32),
            pltpu.VMEM((8, 128), jnp.int32),
            pltpu.VMEM((width, packed_width), jnp.bfloat16),
        ],
        in_specs=[SMEM] + [HBM] * len(sources),
        out_specs=[VMEM] * 5,
        scratch_shapes=[
            pltpu.VMEM(cross_wq.shape, cross_wq.dtype),
            pltpu.SMEM(cross_temp.shape, cross_temp.dtype),
            pltpu.SMEM(self_temp.shape, self_temp.dtype),
            pltpu.SemaphoreType.DMA((len(sources),)),
        ],
        compiler_params=params,
        cost_estimate=pl.CostEstimate(
            flops=2 * rows * width * width, bytes_accessed=4 * 2**20, transcendentals=0
        ),
        name="load",
    )(counts, *map(in_hbm, sources))
    count = sum(piece.shape[0] for piece in pieces)
    block = rows if count <= 128 else min(rows, 128)
    kv_shape = pltpu.VMEM((rows, 2 * width), jnp.bfloat16)
    x1, hn, kv = pl.pallas_call(
        functools.partial(cross_kernel, len(pieces), block, tile, heads),
        out_shape=(pltpu.VMEM((rows, width), jnp.float32), tokens, kv_shape),
        in_specs=[VMEM] * (5 + len(pieces)),
        out_specs=(VMEM, VMEM, VMEM),
        scratch_shapes=[
            pltpu.VMEM((heads * count, width), jnp.bfloat16),
            pltpu.VMEM((heads * count, width), jnp.bfloat16),
        ],
        compiler_params=params,
        name="cross",
    )(scales, live, x, qc, *pieces, packed)
    other = swap(kv, "col")
    depth = min(128, width)
    block = min(256, rows)
    wide = pltpu.VMEM((rows, width), jnp.float32)
    line = pltpu.VMEM((8, 128), jnp.float32)
    held = [
        pltpu.VMEM((heads * rows, width), jnp.bfloat16),
        pltpu.VMEM((2, rows, heads // 2 * rows), jnp.bfloat16),
    ]
    qm, *state = pl.pallas_call(
        functools.partial(own_kernel, heads),
        out_shape=(pltpu.VMEM((heads * rows, depth), jnp.bfloat16), wide, wide, wide, line, line),
        in_specs=[VMEM] * 4,
        out_specs=(VMEM,) * 6,
        scratch_shapes=held,
        compiler_params=params,
        cost_estimate=pl.CostEstimate(
            flops=8 * heads * rows * rows * width, bytes_accessed=2**20, transcendentals=0
        ),
        name="own",
    )(scales, hn, kv, packed)
    late = (self_wo, ffn_up, ffn_down, box_w1, box_w2, jnp.transpose(box_w3))
    return pl.pallas_call(
        functools.partial(rest_kernel, heads),
        out_shape=(
            jax.ShapeDtypeStruct((rows, width), jnp.float32),
            jax.ShapeDtypeStruct((box_w3.shape[1], rows), jnp.float32),
        ),
        in_specs=[VMEM] * 10 + [HBM] * len(late),
        out_specs=(HBM, VMEM),
        scratch_shapes=held
        + [
            pltpu.VMEM((rows, width), jnp.bfloat16),
            wide,
            wide,
            pltpu.VMEM((2, block, ffn_up.shape[1]), jnp.bfloat16),
        ]
        + [pltpu.VMEM(w.shape, w.dtype) for w in late]
        + [pltpu.SemaphoreType.DMA((len(late) + 1,))],
        compiler_params=params,
        name="rest",
    )(scales, live, x1, other, qm, *state, *map(in_hbm, late))


def solution(mesh):
    return jax.shard_map(
        local,
        mesh=mesh,
        in_specs=(
            P(("parts", "row", "col"), None),
            P(("parts", "row", "col")),
            P(("parts", "row", "col"), None),
            P(("parts", "row", "col")),
            P(),
            P(),
            P(),
            P(),
            P(),
            P(),
            P(),
            P(),
            P(),
            P(),
            P(),
            P(),
        ),
        out_specs=(P(("parts", "row", "col"), None), P(None, ("parts", "row", "col"))),
        check_vma=False,
    )
```

```python
import functools
import math

import jax
import jax.numpy as jnp
from jax import lax
from jax.experimental import pallas as pl
from jax.experimental.pallas import tpu as pltpu
from jax.sharding import PartitionSpec as P

EPS = 1e-06
DEAD = 64.0
DEAD_V = 4096.0
LIMIT = 69.0
VMEM = pl.BlockSpec(memory_space=pltpu.VMEM)
SMEM = pl.BlockSpec(memory_space=pltpu.SMEM)
HBM = pl.BlockSpec(memory_space=pltpu.HBM)


def rms_round(x):
    return (x * lax.rsqrt(jnp.mean(x * x, axis=-1, keepdims=True) + EPS)).astype(jnp.bfloat16)


def dot(a, b):
    return jnp.dot(a, b, preferred_element_type=jnp.float32)


def dot_t(a, b):
    return lax.dot_general(a, b, (((1,), (1,)), ((), ())), preferred_element_type=jnp.float32)


def head_of_lane(rows, width, heads):
    return lax.broadcasted_iota(jnp.int32, (rows, width), 1) // (width // heads)


def only(x, head, lane_head):
    return jnp.where(lane_head == head, x, jnp.zeros_like(x))


def flagged(values, flags, head, heads, lane_head):
    other = (head + heads // 2) % heads
    rest = jnp.where(lane_head == other, flags, jnp.zeros_like(values))
    return jnp.where(lane_head == head, values, rest)


def weigh(scores, top, scale):
    return jnp.exp((scores - top) * scale).astype(jnp.bfloat16)


def normed(low, high):
    half = low.shape[1] // 2
    return jnp.concatenate(
        [low[:, :half] / low[:, half:], high[:, half:] / high[:, :half]], axis=1
    ).astype(jnp.bfloat16)


def mark_kernel(memory, mask, out, held, flags, sems):
    copies = [
        pltpu.make_async_copy(memory, held, sems.at[0]),
        pltpu.make_async_copy(mask, flags, sems.at[1]),
    ]
    for copy in copies:
        copy.start()
    for copy in copies:
        copy.wait()
    row = lax.broadcasted_iota(jnp.int32, held.shape, 0)
    tokens = held[...].astype(jnp.float32)
    for j in range(held.shape[0]):
        tokens = jnp.where((row == j) & (flags[j] <= 0), DEAD, tokens)
    tokens = tokens.astype(jnp.bfloat16)
    for copy in range(out.shape[0]):
        out[copy] = tokens


def load_kernel(
    counts,
    queries,
    wq,
    cross_temp,
    self_temp,
    wkv,
    wo,
    wqkv,
    x_ref,
    qc_ref,
    scale_ref,
    count_ref,
    packed,
    wvt_ref,
    wqt_ref,
    wq_held,
    cross_held,
    self_held,
    sems,
):
    width = x_ref.shape[1]
    pairs = [(queries, x_ref), (wq, wq_held), (cross_temp, cross_held), (self_temp, self_held)]
    begin = 0
    for source in (wkv, wo, wqkv):
        end = begin + source.shape[1]
        pairs.append((source, packed.at[:, begin:end]))
        begin = end
    copies = [pltpu.make_async_copy(a, b, sems.at[i]) for i, (a, b) in enumerate(pairs)]
    for copy in copies:
        copy.start()
    for copy in copies[:4]:
        copy.wait()
    heads = cross_temp.shape[0]
    factor = 1.0 / math.sqrt(width // heads)
    lanes = scale_ref.shape[1]
    for side, temp in enumerate((cross_held, self_held)):
        for head in range(heads):
            at = pl.ds(side * heads + head, 1)
            scale_ref[at, :] = jnp.full((1, lanes), temp[head] * factor, jnp.float32)
    count_ref[...] = jnp.full(count_ref.shape, counts[0], jnp.int32)
    x = x_ref[...].astype(jnp.float32)
    qc_ref[...] = dot(rms_round(x), wq_held[...]).astype(jnp.bfloat16)
    for copy in copies[4:]:
        copy.wait()
    wvt_ref[...] = jnp.transpose(packed[:, -width:])
    wqt_ref[...] = jnp.transpose(packed[:, -3 * width : -2 * width])


def cross_kernel(n, block, tile, heads, scales, counts, queries, qc, *refs):
    pieces = refs[:n]
    packed, wvt, x1_ref, hn_ref, kv_ref, kbd, vbd = refs[n:]
    rows, width = queries.shape
    wkv = packed[:, : 2 * width]
    wo = packed[:, 2 * width : 3 * width]
    wk = packed[:, 4 * width : 5 * width]
    tokens, flags = [], []
    for piece in pieces:
        held = piece[...].astype(jnp.float32)
        dead = held >= DEAD
        for begin in range(0, held.shape[0], tile):
            part = held[begin : begin + tile]
            gone = dead[begin : begin + tile]
            tokens.append(jnp.where(gone, part[:1], part).astype(jnp.bfloat16))
            flags.append(jnp.where(gone, 0.0, 1.0).astype(jnp.bfloat16))
    tokens = jnp.concatenate(tokens, axis=0)
    flags = jnp.concatenate(flags, axis=0)
    count = tokens.shape[0]
    kvm = dot(tokens, wkv).astype(jnp.bfloat16)
    keys = kvm[:, :width]
    values = kvm[:, width:] * flags
    lane_head = head_of_lane(count, width, heads)
    for head in range(heads):
        at = pl.ds(head * count, count)
        kbd[at, :] = only(keys, head, lane_head)
        vbd[at, :] = flagged(values, flags, head, heads, lane_head)
    middle = heads // 2 * count
    for begin in range(0, rows, block):
        at = pl.ds(begin, block)
        x = queries[at, :].astype(jnp.float32)
        scores = dot_t(qc[at, :], kbd[...])
        weights = []
        for head in range(heads):
            s = scores[:, head * count : (head + 1) * count]
            top = jnp.max(s, axis=-1, keepdims=True)
            weights.append(weigh(s, top, scales[head : head + 1, :1]))
        low = dot(jnp.concatenate(weights[: heads // 2], axis=1), vbd[:middle, :])
        high = dot(jnp.concatenate(weights[heads // 2 :], axis=1), vbd[middle:, :])
        x1 = x + dot(normed(low, high), wo)
        x1_ref[at, :] = x1
        hn1 = rms_round(x1)
        hn_ref[at, :] = hn1
        key = dot(hn1, wk).astype(jnp.bfloat16)
        slot = lax.broadcasted_iota(jnp.int32, (block, width), 0) + begin
        if begin == 0:
            first = key[:1]
        kv_ref[at, :] = jnp.where(slot < counts[:1, :1], key, first)
        value = dot_t(wvt[...], hn1).astype(jnp.bfloat16)
        slot = lax.broadcasted_iota(jnp.int32, (width, block), 1) + begin
        value = jnp.where(slot < counts[:1, :1], value, jnp.bfloat16(DEAD_V))
        for part in range(0, block, width):
            place = begin + part
            size = min(block, width)
            target = pl.ds(rows + place // width * width, width)
            lanes = pl.ds(place % width, size)
            kv_ref[target, lanes] = value[:, part : part + size]


def transposed_values(kv, vt, heads):
    rows, width = vt.shape[1], kv.shape[1]
    hsize, part = width // heads, vt.shape[0] // heads
    for begin in range(0, rows, width):
        lanes = pl.ds(begin, width)
        values = kv[rows + begin : rows + begin + width, :]
        live = values < jnp.bfloat16(DEAD_V)
        flags = jnp.where(live[: part - hsize], jnp.bfloat16(1), jnp.bfloat16(0))
        values = jnp.where(live, values, jnp.bfloat16(0))
        for head in range(heads):
            at = head * part
            vt[at : at + hsize, lanes] = values[head * hsize : (head + 1) * hsize]
            vt[at + hsize : at + part, lanes] = flags


def head_rows(width, heads, lanes):
    row = lax.broadcasted_iota(jnp.int32, (width, lanes), 0) // (width // heads)
    lane = lax.broadcasted_iota(jnp.int32, (width, lanes), 1)
    return jnp.where(row == lane, 1.0, 0.0).astype(jnp.bfloat16)


def key_sizes(keys, heads, lanes):
    wide = keys.astype(jnp.float32)
    norms = dot((wide * wide).astype(jnp.bfloat16), head_rows(keys.shape[1], heads, lanes))
    return jnp.max(norms, axis=0, keepdims=True)


def query_sizes(q, scales, heads):
    hsize = q.shape[0] // heads
    lane = lax.broadcasted_iota(jnp.int32, (1, scales.shape[1]), 1)
    sizes = jnp.zeros((1, scales.shape[1]), jnp.float32)
    for head in range(heads):
        part = q[head * hsize : (head + 1) * hsize].astype(jnp.float32)
        norm = jnp.max(jnp.sum(part * part, axis=0, keepdims=True), axis=1, keepdims=True)
        scale = scales[heads + head : heads + head + 1, :]
        sizes = jnp.where(lane == head, norm * scale * scale, sizes)
    return sizes


def half_attention(scales, qt, kv, vt, heads, s_held, p_held, sizes, use):
    rows, width = vt.shape[1], kv.shape[1]
    part = vt.shape[0] // heads
    depth = qt.shape[0] // heads
    per = heads * depth // width
    block = s_held.shape[2]
    units = [(head, begin) for head in range(heads) for begin in range(0, rows, block)]
    bounds = sizes * key_sizes(kv[:rows, :], heads, sizes.shape[1])
    small = jnp.max(bounds) <= LIMIT * LIMIT

    def score(unit):
        head, begin = units[unit]
        lanes = head // per * depth
        q = qt[head * depth : (head + 1) * depth, begin : begin + block]
        return dot(kv[:rows, lanes : lanes + depth], q)

    def scale_of(unit):
        head = units[unit][0]
        return scales[heads + head : heads + head + 1, :1]

    def mix(unit, top):
        head, begin = units[unit]
        total = dot(vt[head * part : (head + 1) * part, :], p_held[unit % 2])
        use(head, pl.ds(begin, block), top, total)

    @pl.when(small)
    def unshifted():
        zero = jnp.zeros((1, block), jnp.float32)
        for step in range(len(units) + 1):
            if step < len(units):
                p_held[step % 2] = jnp.exp(score(step) * scale_of(step)).astype(jnp.bfloat16)
            if 0 <= step - 1:
                mix(step - 1, zero)

    @pl.when(jnp.logical_not(small))
    def shifted():
        tops = {}
        for step in range(len(units) + 2):
            if step < len(units):
                s = score(step)
                s_held[step % 2] = s
                tops[step] = jnp.max(s, axis=0, keepdims=True)
            last = step - 1
            if 0 <= last < len(units):
                p_held[last % 2] = weigh(s_held[last % 2], tops[last], scale_of(last))
            if 0 <= step - 2:
                mix(step - 2, tops[step - 2])


def own_kernel(
    heads, scales, hn, kv, wqt, qt, top_ref, sum_ref, size_ref, vt, s_held, p_held
):
    width = hn.shape[1]
    hsize = width // heads
    depth = qt.shape[0] // heads
    part = vt.shape[0] // heads
    q = dot_t(wqt[...], hn[...]).astype(jnp.bfloat16)
    sizes = query_sizes(q, scales, heads)
    size_ref[...] = jnp.broadcast_to(sizes, size_ref.shape)
    qt[...] = jnp.zeros_like(qt)
    for head in range(heads):
        begin = head * hsize
        at = head * depth + begin % depth
        qt[at : at + hsize, :] = q[begin : begin + hsize]
    transposed_values(kv, vt, heads)

    def use(head, at, top, total):
        top_ref[head : head + 1, at] = top
        sum_ref[head * part : (head + 1) * part, at] = total

    half_attention(scales, qt, kv, vt, heads, s_held, p_held, sizes, use)


def rest_kernel(
    heads,
    scales,
    counts,
    x1_ref,
    kv,
    qt,
    top_ref,
    sum_ref,
    size_ref,
    wo,
    up,
    down,
    w1,
    w2,
    w3,
    features,
    boxes,
    vt,
    s_held,
    p_held,
    ctx,
    out,
    upper,
    wo_held,
    up_held,
    down_held,
    w1_held,
    w2_held,
    w3_held,
    sems,
):
    rows, width = x1_ref.shape
    hsize = width // heads
    part = vt.shape[0] // heads
    held = (wo_held, up_held, down_held, w1_held, w2_held, w3_held)
    pairs = zip((wo, up, down, w1, w2, w3), held)
    copies = [pltpu.make_async_copy(a, b, sems.at[i]) for i, (a, b) in enumerate(pairs)]
    for copy in copies:
        copy.start()
    transposed_values(kv, vt, heads)

    def use(head, at, top, total):
        scale = scales[heads + head : heads + head + 1, :1]
        first = top_ref[head : head + 1, at]
        most = jnp.maximum(first, top)
        total = total * jnp.exp((top - most) * scale)
        total += sum_ref[head * part : (head + 1) * part, at] * jnp.exp((first - most) * scale)
        mixed = total[:hsize] / total[hsize : hsize + 1]
        ctx[head * hsize : (head + 1) * hsize, at] = mixed.astype(jnp.bfloat16)

    half_attention(scales, qt, kv, vt, heads, s_held, p_held, size_ref[:1, :], use)
    for copy in copies:
        copy.wait()
    block = upper.shape[1]
    starts = list(range(0, rows, block))
    ff = up_held.shape[1]
    chunk = ff // 4
    x2, x3, leaves = {}, {}, []

    def project(i):
        at = pl.ds(starts[i], block)
        mixed = lax.dot_general(
            ctx[:, at], wo_held[...], (((0,), (0,)), ((), ())), preferred_element_type=jnp.float32
        )
        x2[i] = x1_ref[at, :] + mixed

    def widen(i):
        hn2 = rms_round(x2[i])
        for begin in range(0, ff, chunk):
            cut = pl.ds(begin, chunk)
            upper[i % 2, :, cut] = jnp.maximum(dot(hn2, up_held[:, cut]), 0.0).astype(jnp.bfloat16)

    def narrow(i):
        at = pl.ds(starts[i], block)
        x3[i] = x2[i] + dot(upper[i % 2], down_held[...])
        slot = lax.broadcasted_iota(jnp.int32, (block, width), 0) + starts[i]
        out[at, :] = jnp.where(slot < counts[:1, :1], x3[i], 0.0)
        leaves.append(
            pltpu.make_async_copy(out.at[at, :], features.at[at, :], sems.at[len(copies) + i])
        )
        leaves[-1].start()

    def box(i):
        b1 = jnp.maximum(dot(rms_round(x3[i]), w1_held[...]), 0.0).astype(jnp.bfloat16)
        b2 = jnp.maximum(dot(b1, w2_held[...]), 0.0).astype(jnp.bfloat16)
        raw = dot_t(w3_held[...], b2)
        slot = lax.broadcasted_iota(jnp.int32, raw.shape, 1) + starts[i]
        boxes[:, pl.ds(starts[i], block)] = jnp.where(
            slot < counts[:1, :1], 1.0 / (1.0 + jnp.exp(-raw)), 0.0
        )

    for step in range(len(starts) + 3):
        for stage, work in enumerate((project, widen, narrow, box)):
            if 0 <= step - stage < len(starts):
                work(step - stage)
    for leave in leaves:
        leave.wait()


def in_hbm(x):
    return pltpu.with_memory_space_constraint(x, pltpu.HBM)


def swap(x, axis):
    size = lax.axis_size(axis)
    return lax.ppermute(x, axis, [(i, i ^ 1) for i in range(size)])


def local(
    queries,
    counts,
    memory,
    mem_mask,
    cross_wq,
    cross_wkv,
    cross_wo,
    self_wqkv,
    self_wo,
    ffn_up,
    ffn_down,
    box_w1,
    box_w2,
    box_w3,
    cross_temp,
    self_temp,
):
    rows, width = queries.shape
    heads = cross_temp.shape[0]
    tile = memory.shape[0]
    params = pltpu.CompilerParams(vmem_limit_bytes=32 * 2**20)
    marked = pl.pallas_call(
        mark_kernel,
        out_shape=pltpu.VMEM((lax.axis_size("row"), tile, width), memory.dtype),
        in_specs=[HBM, HBM],
        out_specs=VMEM,
        scratch_shapes=[
            pltpu.VMEM(memory.shape, memory.dtype),
            pltpu.SMEM(mem_mask.shape, mem_mask.dtype),
            pltpu.SemaphoreType.DMA((2,)),
        ],
        name="mark",
    )(in_hbm(memory), in_hbm(mem_mask))
    gathered = lax.all_to_all(marked, "row", 0, 0, tiled=True)
    pieces = [gathered.reshape(-1, width)]
    tokens = pltpu.VMEM((rows, width), jnp.bfloat16)
    packed_width = cross_wkv.shape[1] + cross_wo.shape[1] + self_wqkv.shape[1]
    sources = (queries, cross_wq, cross_temp, self_temp, cross_wkv, cross_wo, self_wqkv)
    x, qc, scales, live, packed, wvt, wqt = pl.pallas_call(
        load_kernel,
        out_shape=[
            tokens,
            tokens,
            pltpu.VMEM((2 * heads, 128), jnp.float32),
            pltpu.VMEM((8, 128), jnp.int32),
            pltpu.VMEM((width, packed_width), jnp.bfloat16),
            pltpu.VMEM((width, width), jnp.bfloat16),
            pltpu.VMEM((width, width), jnp.bfloat16),
        ],
        in_specs=[SMEM] + [HBM] * len(sources),
        out_specs=[VMEM] * 7,
        scratch_shapes=[
            pltpu.VMEM(cross_wq.shape, cross_wq.dtype),
            pltpu.SMEM(cross_temp.shape, cross_temp.dtype),
            pltpu.SMEM(self_temp.shape, self_temp.dtype),
            pltpu.SemaphoreType.DMA((len(sources),)),
        ],
        compiler_params=params,
        cost_estimate=pl.CostEstimate(
            flops=2 * rows * width * width, bytes_accessed=4 * 2**20, transcendentals=0
        ),
        name="load",
    )(counts, *map(in_hbm, sources))
    count = sum(piece.shape[0] for piece in pieces)
    block = rows if count <= 128 else min(rows, 128)
    kv_shape = pltpu.VMEM((2 * rows, width), jnp.bfloat16)
    x1, hn, kv = pl.pallas_call(
        functools.partial(cross_kernel, len(pieces), block, tile, heads),
        out_shape=(pltpu.VMEM((rows, width), jnp.float32), tokens, kv_shape),
        in_specs=[VMEM] * (6 + len(pieces)),
        out_specs=(VMEM, VMEM, VMEM),
        scratch_shapes=[
            pltpu.VMEM((heads * count, width), jnp.bfloat16),
            pltpu.VMEM((heads * count, width), jnp.bfloat16),
        ],
        compiler_params=params,
        name="cross",
    )(scales, live, x, qc, *pieces, packed, wvt)
    other = swap(kv, "col")
    part = width // heads + 16
    depth = min(128, width)
    block = min(256, rows)
    held = [
        pltpu.VMEM((heads * part, rows), jnp.bfloat16),
        pltpu.VMEM((2, rows, block), jnp.float32),
        pltpu.VMEM((2, rows, block), jnp.bfloat16),
    ]
    qt, tops, sums, sizes = pl.pallas_call(
        functools.partial(own_kernel, heads),
        out_shape=(
            pltpu.VMEM((heads * depth, rows), jnp.bfloat16),
            pltpu.VMEM((heads, rows), jnp.float32),
            pltpu.VMEM((heads * part, rows), jnp.float32),
            pltpu.VMEM((8, 128), jnp.float32),
        ),
        in_specs=[VMEM] * 4,
        out_specs=(VMEM, VMEM, VMEM, VMEM),
        scratch_shapes=held,
        compiler_params=params,
        cost_estimate=pl.CostEstimate(
            flops=8 * heads * rows * rows * width, bytes_accessed=2**20, transcendentals=0
        ),
        name="own",
    )(scales, hn, kv, wqt)
    late = (self_wo, ffn_up, ffn_down, box_w1, box_w2, jnp.transpose(box_w3))
    return pl.pallas_call(
        functools.partial(rest_kernel, heads),
        out_shape=(
            jax.ShapeDtypeStruct((rows, width), jnp.float32),
            jax.ShapeDtypeStruct((box_w3.shape[1], rows), jnp.float32),
        ),
        in_specs=[VMEM] * 8 + [HBM] * len(late),
        out_specs=(HBM, VMEM),
        scratch_shapes=held
        + [
            pltpu.VMEM((width, rows), jnp.bfloat16),
            pltpu.VMEM((rows, width), jnp.float32),
            pltpu.VMEM((2, block, ffn_up.shape[1]), jnp.bfloat16),
        ]
        + [pltpu.VMEM(w.shape, w.dtype) for w in late]
        + [pltpu.SemaphoreType.DMA((len(late) + rows // block,))],
        compiler_params=params,
        name="rest",
    )(scales, live, x1, other, qt, tops, sums, sizes, *map(in_hbm, late))


def solution(mesh):
    return jax.shard_map(
        local,
        mesh=mesh,
        in_specs=(
            P(("parts", "row", "col"), None),
            P(("parts", "row", "col")),
            P(("parts", "row", "col"), None),
            P(("parts", "row", "col")),
            P(),
            P(),
            P(),
            P(),
            P(),
            P(),
            P(),
            P(),
            P(),
            P(),
            P(),
            P(),
        ),
        out_specs=(P(("parts", "row", "col"), None), P(None, ("parts", "row", "col"))),
        check_vma=False,
    )
```

```python
import functools
import math

import jax
import jax.numpy as jnp
from jax import lax
from jax.experimental import pallas as pl
from jax.experimental.pallas import tpu as pltpu
from jax.sharding import PartitionSpec as P

EPS = 1e-06
DEAD = 64.0
DEAD_V = 4096.0
STEP = 128
LIMIT = 69.0
VMEM = pl.BlockSpec(memory_space=pltpu.VMEM)
SMEM = pl.BlockSpec(memory_space=pltpu.SMEM)
HBM = pl.BlockSpec(memory_space=pltpu.HBM)


def rms_round(x):
    return (x * lax.rsqrt(jnp.mean(x * x, axis=-1, keepdims=True) + EPS)).astype(jnp.bfloat16)


def dot(a, b):
    return jnp.dot(a, b, preferred_element_type=jnp.float32)


def dot_t(a, b):
    return lax.dot_general(a, b, (((1,), (1,)), ((), ())), preferred_element_type=jnp.float32)


def head_of_lane(rows, width, heads):
    return lax.broadcasted_iota(jnp.int32, (rows, width), 1) // (width // heads)


def only(x, head, lane_head):
    return jnp.where(lane_head == head, x, jnp.zeros_like(x))


def flagged(values, flags, head, heads, lane_head):
    other = (head + heads // 2) % heads
    rest = jnp.where(lane_head == other, flags, jnp.zeros_like(values))
    return jnp.where(lane_head == head, values, rest)


def weigh(scores, top, scale):
    return jnp.exp((scores - top) * scale).astype(jnp.bfloat16)


def normed(low, high):
    half = low.shape[1] // 2
    return jnp.concatenate(
        [low[:, :half] / low[:, half:], high[:, half:] / high[:, :half]], axis=1
    ).astype(jnp.bfloat16)


def mark_kernel(memory, mask, out, held, flags, sems):
    copies = [
        pltpu.make_async_copy(memory, held, sems.at[0]),
        pltpu.make_async_copy(mask, flags, sems.at[1]),
    ]
    for copy in copies:
        copy.start()
    for copy in copies:
        copy.wait()
    row = lax.broadcasted_iota(jnp.int32, held.shape, 0)
    tokens = held[...].astype(jnp.float32)
    for j in range(held.shape[0]):
        tokens = jnp.where((row == j) & (flags[j] <= 0), DEAD, tokens)
    tokens = tokens.astype(jnp.bfloat16)
    for copy in range(out.shape[0]):
        out[copy] = tokens


def load_kernel(
    counts,
    queries,
    wq,
    cross_temp,
    self_temp,
    wkv,
    wo,
    wqkv,
    x_ref,
    qc_ref,
    scale_ref,
    count_ref,
    packed,
    wvt_ref,
    wqt_ref,
    wq_held,
    cross_held,
    self_held,
    sems,
):
    width = x_ref.shape[1]
    pairs = [(queries, x_ref), (wq, wq_held), (cross_temp, cross_held), (self_temp, self_held)]
    begin = 0
    for source in (wkv, wo, wqkv):
        end = begin + source.shape[1]
        pairs.append((source, packed.at[:, begin:end]))
        begin = end
    copies = [pltpu.make_async_copy(a, b, sems.at[i]) for i, (a, b) in enumerate(pairs)]
    for copy in copies:
        copy.start()
    for copy in copies[:4]:
        copy.wait()
    heads = cross_temp.shape[0]
    factor = 1.0 / math.sqrt(width // heads)
    lanes = scale_ref.shape[1]
    for side, temp in enumerate((cross_held, self_held)):
        for head in range(heads):
            at = pl.ds(side * heads + head, 1)
            scale_ref[at, :] = jnp.full((1, lanes), temp[head] * factor, jnp.float32)
    count_ref[...] = jnp.full(count_ref.shape, counts[0], jnp.int32)
    x = x_ref[...].astype(jnp.float32)
    qc_ref[...] = dot(rms_round(x), wq_held[...]).astype(jnp.bfloat16)
    for copy in copies[4:]:
        copy.wait()
    wvt_ref[...] = jnp.transpose(packed[:, -width:])
    wqt_ref[...] = jnp.transpose(packed[:, -3 * width : -2 * width])


def cross_kernel(n, block, tile, heads, scales, counts, queries, qc, *refs):
    pieces = refs[:n]
    packed, wvt, x1_ref, hn_ref, kv_ref, kbd, vbd = refs[n:]
    rows, width = queries.shape
    wkv = packed[:, : 2 * width]
    wo = packed[:, 2 * width : 3 * width]
    wk = packed[:, 4 * width : 5 * width]
    tokens, flags = [], []
    for piece in pieces:
        held = piece[...].astype(jnp.float32)
        dead = held >= DEAD
        for begin in range(0, held.shape[0], tile):
            part = held[begin : begin + tile]
            gone = dead[begin : begin + tile]
            tokens.append(jnp.where(gone, part[:1], part).astype(jnp.bfloat16))
            flags.append(jnp.where(gone, 0.0, 1.0).astype(jnp.bfloat16))
    tokens = jnp.concatenate(tokens, axis=0)
    flags = jnp.concatenate(flags, axis=0)
    count = tokens.shape[0]
    kvm = dot(tokens, wkv).astype(jnp.bfloat16)
    keys = kvm[:, :width]
    values = kvm[:, width:] * flags
    lane_head = head_of_lane(count, width, heads)
    for head in range(heads):
        at = pl.ds(head * count, count)
        kbd[at, :] = only(keys, head, lane_head)
        vbd[at, :] = flagged(values, flags, head, heads, lane_head)
    middle = heads // 2 * count
    for begin in range(0, rows, block):
        at = pl.ds(begin, block)
        x = queries[at, :].astype(jnp.float32)
        scores = dot_t(qc[at, :], kbd[...])
        weights = []
        for head in range(heads):
            s = scores[:, head * count : (head + 1) * count]
            top = jnp.max(s, axis=-1, keepdims=True)
            weights.append(weigh(s, top, scales[head : head + 1, :1]))
        low = dot(jnp.concatenate(weights[: heads // 2], axis=1), vbd[:middle, :])
        high = dot(jnp.concatenate(weights[heads // 2 :], axis=1), vbd[middle:, :])
        x1 = x + dot(normed(low, high), wo)
        x1_ref[at, :] = x1
        hn1 = rms_round(x1)
        hn_ref[at, :] = hn1
        key = dot(hn1, wk).astype(jnp.bfloat16)
        slot = lax.broadcasted_iota(jnp.int32, (block, width), 0) + begin
        if begin == 0:
            first = key[:1]
        kv_ref[at, :] = jnp.where(slot < counts[:1, :1], key, first)
        value = dot_t(wvt[...], hn1).astype(jnp.bfloat16)
        slot = lax.broadcasted_iota(jnp.int32, (width, block), 1) + begin
        value = jnp.where(slot < counts[:1, :1], value, jnp.bfloat16(DEAD_V))
        for part in range(0, block, width):
            place = begin + part
            size = min(block, width)
            target = pl.ds(rows + place // width * width, width)
            lanes = pl.ds(place % width, size)
            kv_ref[target, lanes] = value[:, part : part + size]


def transposed_values(kv, vt, heads):
    rows, width = vt.shape[1], kv.shape[1]
    hsize, part = width // heads, vt.shape[0] // heads
    for begin in range(0, rows, width):
        lanes = pl.ds(begin, width)
        values = kv[rows + begin : rows + begin + width, :]
        live = values < jnp.bfloat16(DEAD_V)
        flags = jnp.where(live[: part - hsize], jnp.bfloat16(1), jnp.bfloat16(0))
        values = jnp.where(live, values, jnp.bfloat16(0))
        for head in range(heads):
            at = head * part
            vt[at : at + hsize, lanes] = values[head * hsize : (head + 1) * hsize]
            vt[at + hsize : at + part, lanes] = flags


def head_rows(width, heads, lanes):
    row = lax.broadcasted_iota(jnp.int32, (width, lanes), 0) // (width // heads)
    lane = lax.broadcasted_iota(jnp.int32, (width, lanes), 1)
    return jnp.where(row == lane, 1.0, 0.0).astype(jnp.bfloat16)


def key_sizes(keys, heads, lanes):
    wide = keys.astype(jnp.float32)
    norms = dot((wide * wide).astype(jnp.bfloat16), head_rows(keys.shape[1], heads, lanes))
    return jnp.max(norms, axis=0, keepdims=True)


def query_sizes(q, scales, heads):
    hsize = q.shape[0] // heads
    lane = lax.broadcasted_iota(jnp.int32, (1, scales.shape[1]), 1)
    sizes = jnp.zeros((1, scales.shape[1]), jnp.float32)
    for head in range(heads):
        part = q[head * hsize : (head + 1) * hsize].astype(jnp.float32)
        norm = jnp.max(jnp.sum(part * part, axis=0, keepdims=True), axis=1, keepdims=True)
        scale = scales[heads + head : heads + head + 1, :]
        sizes = jnp.where(lane == head, norm * scale * scale, sizes)
    return sizes


def half_attention(scales, qt, kv, vt, heads, s_held, p_held, sizes, live, blocks, use):
    rows, width = vt.shape[1], kv.shape[1]
    part = vt.shape[0] // heads
    depth = qt.shape[0] // heads
    per = heads * depth // width
    block = s_held.shape[2]
    steps = rows // STEP
    bound = jnp.max(sizes * key_sizes(kv[:rows, :], heads, sizes.shape[1]), axis=1, keepdims=True)
    choice = jnp.max(jnp.where(bound <= LIMIT * LIMIT, live, float(steps + 1)))

    def score(head, at, keys):
        lanes = head // per * depth
        q = qt[head * depth : (head + 1) * depth, at]
        return dot(kv[:keys, lanes : lanes + depth], q)

    def scale_of(head):
        return scales[heads + head : heads + head + 1, :1]

    def unshifted(keys):
        zero = jnp.zeros((1, block), jnp.float32)

        def visit(index, carry):
            at = pl.ds(pl.multiple_of(index * block, block), block)
            for step in range(heads + 1):
                if step < heads:
                    weights = jnp.exp(score(step, at, keys) * scale_of(step))
                    p_held[step % 2, :keys, :] = weights.astype(jnp.bfloat16)
                last = step - 1
                if 0 <= last:
                    mine = vt[last * part : (last + 1) * part, :keys]
                    use(last, at, zero, dot(mine, p_held[last % 2, :keys, :]))
            return carry

        lax.fori_loop(0, blocks, visit, 0)

    for step in range(1, steps + 1):
        pl.when(choice == float(step))(functools.partial(unshifted, step * STEP))

    @pl.when(choice > float(steps))
    def shifted():
        begins = range(0, rows, block)
        units = [(head, pl.ds(begin, block)) for head in range(heads) for begin in begins]
        tops = {}
        for step in range(len(units) + 2):
            if step < len(units):
                s = score(*units[step], rows)
                s_held[step % 2] = s
                tops[step] = jnp.max(s, axis=0, keepdims=True)
            last = step - 1
            if 0 <= last < len(units):
                p_held[last % 2] = weigh(s_held[last % 2], tops[last], scale_of(units[last][0]))
            last = step - 2
            if 0 <= last:
                head, at = units[last]
                mine = vt[head * part : (head + 1) * part, :]
                use(head, at, tops[last], dot(mine, p_held[last % 2]))


def own_kernel(
    heads, counts, scales, hn, kv, wqt, qt, top_ref, sum_ref, size_ref, vt, s_held, p_held
):
    width = hn.shape[1]
    hsize = width // heads
    depth = qt.shape[0] // heads
    part = vt.shape[0] // heads
    q = dot_t(wqt[...], hn[...]).astype(jnp.bfloat16)
    sizes = query_sizes(q, scales, heads)
    size_ref[...] = jnp.broadcast_to(sizes, size_ref.shape)
    qt[...] = jnp.zeros_like(qt)
    for head in range(heads):
        begin = head * hsize
        at = head * depth + begin % depth
        qt[at : at + hsize, :] = q[begin : begin + hsize]
    transposed_values(kv, vt, heads)

    def use(head, at, top, total):
        top_ref[head : head + 1, at] = top
        sum_ref[head * part : (head + 1) * part, at] = total

    block = s_held.shape[2]
    blocks = lax.div(counts[0] + block - 1, block)
    steps = lax.div(counts[0] + STEP - 1, STEP).astype(jnp.float32)
    half_attention(scales, qt, kv, vt, heads, s_held, p_held, sizes, steps, blocks, use)


def rest_kernel(
    heads,
    counts,
    scales,
    x1_ref,
    kv,
    qt,
    top_ref,
    sum_ref,
    size_ref,
    wo,
    up,
    down,
    w1,
    w2,
    w3,
    features,
    boxes,
    vt,
    s_held,
    p_held,
    ctx,
    out,
    upper,
    wo_held,
    up_held,
    down_held,
    w1_held,
    w2_held,
    w3_held,
    sems,
):
    rows, width = x1_ref.shape
    hsize = width // heads
    part = vt.shape[0] // heads
    held = (wo_held, up_held, down_held, w1_held, w2_held, w3_held)
    pairs = zip((wo, up, down, w1, w2, w3), held)
    copies = [pltpu.make_async_copy(a, b, sems.at[i]) for i, (a, b) in enumerate(pairs)]
    for copy in copies:
        copy.start()
    transposed_values(kv, vt, heads)

    def use(head, at, top, total):
        scale = scales[heads + head : heads + head + 1, :1]
        first = top_ref[head : head + 1, at]
        most = jnp.maximum(first, top)
        total = total * jnp.exp((top - most) * scale)
        total += sum_ref[head * part : (head + 1) * part, at] * jnp.exp((first - most) * scale)
        mixed = total[:hsize] / total[hsize : hsize + 1]
        ctx[head * hsize : (head + 1) * hsize, at] = mixed.astype(jnp.bfloat16)

    block = upper.shape[1]
    count = counts[0]
    blocks = lax.div(count + block - 1, block)
    steps = jnp.ones((1, 1), jnp.float32)
    for token in range(STEP, rows, STEP):
        row = rows + token // width * width
        mark = kv[row : row + 1, token % width : token % width + 1].astype(jnp.float32)
        steps += jnp.where(mark < DEAD_V, 1.0, 0.0)
    half_attention(
        scales, qt, kv, vt, heads, s_held, p_held, size_ref[:1, :], steps, blocks, use
    )
    for copy in copies:
        copy.wait()
    starts = list(range(0, rows, block))
    ff = up_held.shape[1]
    chunk = ff // 4
    x2, x3 = {}, {}

    def leave(i):
        at = pl.ds(starts[i], block)
        return pltpu.make_async_copy(out.at[at, :], features.at[at, :], sems.at[len(copies) + i])

    def project(i):
        at = pl.ds(starts[i], block)
        mixed = lax.dot_general(
            ctx[:, at], wo_held[...], (((0,), (0,)), ((), ())), preferred_element_type=jnp.float32
        )
        x2[i] = x1_ref[at, :] + mixed

    def widen(i):
        hn2 = rms_round(x2[i])
        for begin in range(0, ff, chunk):
            cut = pl.ds(begin, chunk)
            upper[i % 2, :, cut] = jnp.maximum(dot(hn2, up_held[:, cut]), 0.0).astype(jnp.bfloat16)

    def narrow(i):
        at = pl.ds(starts[i], block)
        x3[i] = x2[i] + dot(upper[i % 2], down_held[...])
        slot = lax.broadcasted_iota(jnp.int32, (block, width), 0) + starts[i]
        out[at, :] = jnp.where(slot < count, x3[i], 0.0)
        leave(i).start()

    def box(i):
        b1 = jnp.maximum(dot(rms_round(x3[i]), w1_held[...]), 0.0).astype(jnp.bfloat16)
        b2 = jnp.maximum(dot(b1, w2_held[...]), 0.0).astype(jnp.bfloat16)
        raw = dot_t(w3_held[...], b2)
        slot = lax.broadcasted_iota(jnp.int32, raw.shape, 1) + starts[i]
        boxes[:, pl.ds(starts[i], block)] = jnp.where(
            slot < count, 1.0 / (1.0 + jnp.exp(-raw)), 0.0
        )

    def finish(live):
        for i in range(live, len(starts)):
            at = pl.ds(starts[i], block)
            out[at, :] = jnp.zeros((block, width), jnp.float32)
            boxes[:, at] = jnp.zeros((boxes.shape[0], block), jnp.float32)
            leave(i).start()
        for step in range(live + 3):
            for stage, work in enumerate((project, widen, narrow, box)):
                if 0 <= step - stage < live:
                    work(step - stage)

    for live in range(1, len(starts) + 1):
        pl.when(blocks == live)(functools.partial(finish, live))
    for i in range(len(starts)):
        leave(i).wait()


def in_hbm(x):
    return pltpu.with_memory_space_constraint(x, pltpu.HBM)


def swap(x, axis):
    size = lax.axis_size(axis)
    return lax.ppermute(x, axis, [(i, i ^ 1) for i in range(size)])


def local(
    queries,
    counts,
    memory,
    mem_mask,
    cross_wq,
    cross_wkv,
    cross_wo,
    self_wqkv,
    self_wo,
    ffn_up,
    ffn_down,
    box_w1,
    box_w2,
    box_w3,
    cross_temp,
    self_temp,
):
    rows, width = queries.shape
    heads = cross_temp.shape[0]
    tile = memory.shape[0]
    params = pltpu.CompilerParams(vmem_limit_bytes=32 * 2**20)
    marked = pl.pallas_call(
        mark_kernel,
        out_shape=pltpu.VMEM((lax.axis_size("row"), tile, width), memory.dtype),
        in_specs=[HBM, HBM],
        out_specs=VMEM,
        scratch_shapes=[
            pltpu.VMEM(memory.shape, memory.dtype),
            pltpu.SMEM(mem_mask.shape, mem_mask.dtype),
            pltpu.SemaphoreType.DMA((2,)),
        ],
        name="mark",
    )(in_hbm(memory), in_hbm(mem_mask))
    gathered = lax.all_to_all(marked, "row", 0, 0, tiled=True)
    pieces = [gathered.reshape(-1, width)]
    tokens = pltpu.VMEM((rows, width), jnp.bfloat16)
    packed_width = cross_wkv.shape[1] + cross_wo.shape[1] + self_wqkv.shape[1]
    sources = (queries, cross_wq, cross_temp, self_temp, cross_wkv, cross_wo, self_wqkv)
    x, qc, scales, live, packed, wvt, wqt = pl.pallas_call(
        load_kernel,
        out_shape=[
            tokens,
            tokens,
            pltpu.VMEM((2 * heads, 128), jnp.float32),
            pltpu.VMEM((8, 128), jnp.int32),
            pltpu.VMEM((width, packed_width), jnp.bfloat16),
            pltpu.VMEM((width, width), jnp.bfloat16),
            pltpu.VMEM((width, width), jnp.bfloat16),
        ],
        in_specs=[SMEM] + [HBM] * len(sources),
        out_specs=[VMEM] * 7,
        scratch_shapes=[
            pltpu.VMEM(cross_wq.shape, cross_wq.dtype),
            pltpu.SMEM(cross_temp.shape, cross_temp.dtype),
            pltpu.SMEM(self_temp.shape, self_temp.dtype),
            pltpu.SemaphoreType.DMA((len(sources),)),
        ],
        compiler_params=params,
        cost_estimate=pl.CostEstimate(
            flops=2 * rows * width * width, bytes_accessed=4 * 2**20, transcendentals=0
        ),
        name="load",
    )(counts, *map(in_hbm, sources))
    count = sum(piece.shape[0] for piece in pieces)
    block = rows if count <= 128 else min(rows, 128)
    kv_shape = pltpu.VMEM((2 * rows, width), jnp.bfloat16)
    x1, hn, kv = pl.pallas_call(
        functools.partial(cross_kernel, len(pieces), block, tile, heads),
        out_shape=(pltpu.VMEM((rows, width), jnp.float32), tokens, kv_shape),
        in_specs=[VMEM] * (6 + len(pieces)),
        out_specs=(VMEM, VMEM, VMEM),
        scratch_shapes=[
            pltpu.VMEM((heads * count, width), jnp.bfloat16),
            pltpu.VMEM((heads * count, width), jnp.bfloat16),
        ],
        compiler_params=params,
        name="cross",
    )(scales, live, x, qc, *pieces, packed, wvt)
    other = swap(kv, "col")
    part = width // heads + 16
    depth = min(128, width)
    block = min(256, rows)
    held = [
        pltpu.VMEM((heads * part, rows), jnp.bfloat16),
        pltpu.VMEM((2, rows, block), jnp.float32),
        pltpu.VMEM((2, rows, block), jnp.bfloat16),
    ]
    qt, tops, sums, sizes = pl.pallas_call(
        functools.partial(own_kernel, heads),
        out_shape=(
            pltpu.VMEM((heads * depth, rows), jnp.bfloat16),
            pltpu.VMEM((heads, rows), jnp.float32),
            pltpu.VMEM((heads * part, rows), jnp.float32),
            pltpu.VMEM((8, 128), jnp.float32),
        ),
        in_specs=[SMEM] + [VMEM] * 4,
        out_specs=(VMEM, VMEM, VMEM, VMEM),
        scratch_shapes=held,
        compiler_params=params,
        cost_estimate=pl.CostEstimate(
            flops=8 * heads * rows * rows * width, bytes_accessed=2**20, transcendentals=0
        ),
        name="own",
    )(counts, scales, hn, kv, wqt)
    late = (self_wo, ffn_up, ffn_down, box_w1, box_w2, jnp.transpose(box_w3))
    return pl.pallas_call(
        functools.partial(rest_kernel, heads),
        out_shape=(
            jax.ShapeDtypeStruct((rows, width), jnp.float32),
            jax.ShapeDtypeStruct((box_w3.shape[1], rows), jnp.float32),
        ),
        in_specs=[SMEM] + [VMEM] * 7 + [HBM] * len(late),
        out_specs=(HBM, VMEM),
        scratch_shapes=held
        + [
            pltpu.VMEM((width, rows), jnp.bfloat16),
            pltpu.VMEM((rows, width), jnp.float32),
            pltpu.VMEM((2, block, ffn_up.shape[1]), jnp.bfloat16),
        ]
        + [pltpu.VMEM(w.shape, w.dtype) for w in late]
        + [pltpu.SemaphoreType.DMA((len(late) + rows // block,))],
        compiler_params=params,
        name="rest",
    )(counts, scales, x1, other, qt, tops, sums, sizes, *map(in_hbm, late))


def solution(mesh):
    return jax.shard_map(
        local,
        mesh=mesh,
        in_specs=(
            P(("parts", "row", "col"), None),
            P(("parts", "row", "col")),
            P(("parts", "row", "col"), None),
            P(("parts", "row", "col")),
            P(),
            P(),
            P(),
            P(),
            P(),
            P(),
            P(),
            P(),
            P(),
            P(),
            P(),
            P(),
        ),
        out_specs=(P(("parts", "row", "col"), None), P(None, ("parts", "row", "col"))),
        check_vma=False,
    )
```

```python
import functools
import math

import jax
import jax.numpy as jnp
from jax import lax
from jax.experimental import pallas as pl
from jax.experimental.pallas import tpu as pltpu
from jax.sharding import PartitionSpec as P

EPS = 1e-06
DEAD = 64.0
DEAD_V = 4096.0
STEP = 128
LIMIT = 69.0
VMEM = pl.BlockSpec(memory_space=pltpu.VMEM)
SMEM = pl.BlockSpec(memory_space=pltpu.SMEM)
HBM = pl.BlockSpec(memory_space=pltpu.HBM)


def rms_round(x):
    return (x * lax.rsqrt(jnp.mean(x * x, axis=-1, keepdims=True) + EPS)).astype(jnp.bfloat16)


def dot(a, b):
    return jnp.dot(a, b, preferred_element_type=jnp.float32)


def dot_t(a, b):
    return lax.dot_general(a, b, (((1,), (1,)), ((), ())), preferred_element_type=jnp.float32)


def head_of_lane(rows, width, heads):
    return lax.broadcasted_iota(jnp.int32, (rows, width), 1) // (width // heads)


def only(x, head, lane_head):
    return jnp.where(lane_head == head, x, jnp.zeros_like(x))


def flagged(values, flags, head, heads, lane_head):
    other = (head + heads // 2) % heads
    rest = jnp.where(lane_head == other, flags, jnp.zeros_like(values))
    return jnp.where(lane_head == head, values, rest)


def weigh(scores, top, scale):
    return jnp.exp((scores - top) * scale).astype(jnp.bfloat16)


def normed(low, high):
    half = low.shape[1] // 2
    return jnp.concatenate(
        [low[:, :half] / low[:, half:], high[:, half:] / high[:, :half]], axis=1
    ).astype(jnp.bfloat16)


def mark_kernel(memory, mask, out, held, flags, sems):
    copies = [
        pltpu.make_async_copy(memory, held, sems.at[0]),
        pltpu.make_async_copy(mask, flags, sems.at[1]),
    ]
    for copy in copies:
        copy.start()
    for copy in copies:
        copy.wait()
    row = lax.broadcasted_iota(jnp.int32, held.shape, 0)
    tokens = held[...].astype(jnp.float32)
    for j in range(held.shape[0]):
        tokens = jnp.where((row == j) & (flags[j] <= 0), DEAD, tokens)
    tokens = tokens.astype(jnp.bfloat16)
    for copy in range(out.shape[0]):
        out[copy] = tokens


def load_kernel(
    counts,
    queries,
    wq,
    cross_temp,
    self_temp,
    wkv,
    wo,
    wqkv,
    wo_self,
    w1,
    w2,
    up,
    down,
    x_ref,
    qc_ref,
    scale_ref,
    count_ref,
    packed,
    wvt_ref,
    wqt_ref,
    down_ref,
    wq_held,
    cross_held,
    self_held,
    sems,
):
    width = x_ref.shape[1]
    pairs = [(queries, x_ref), (wq, wq_held), (cross_temp, cross_held), (self_temp, self_held)]
    begin = 0
    for source in (wkv, wo, wqkv, wo_self, w1, w2, up):
        end = begin + source.shape[1]
        pairs.append((source, packed.at[:, begin:end]))
        begin = end
    pairs.append((down, down_ref))
    copies = [pltpu.make_async_copy(a, b, sems.at[i]) for i, (a, b) in enumerate(pairs)]
    for copy in copies:
        copy.start()
    for copy in copies[:4]:
        copy.wait()
    heads = cross_temp.shape[0]
    factor = 1.0 / math.sqrt(width // heads)
    lanes = scale_ref.shape[1]
    for side, temp in enumerate((cross_held, self_held)):
        for head in range(heads):
            at = pl.ds(side * heads + head, 1)
            scale_ref[at, :] = jnp.full((1, lanes), temp[head] * factor, jnp.float32)
    count_ref[...] = jnp.full(count_ref.shape, counts[0], jnp.int32)
    x = x_ref[...].astype(jnp.float32)
    qc_ref[...] = dot(rms_round(x), wq_held[...]).astype(jnp.bfloat16)
    for copy in copies[4:]:
        copy.wait()
    wvt_ref[...] = jnp.transpose(packed[:, 5 * width : 6 * width])
    wqt_ref[...] = jnp.transpose(packed[:, 3 * width : 4 * width])


def cross_kernel(n, block, tile, heads, scales, counts, queries, qc, *refs):
    pieces = refs[:n]
    packed, wvt, wqt, x1_ref, qt, size_ref, kv_ref, kbd, vbd = refs[n:]
    qt[...] = jnp.zeros_like(qt)
    rows, width = queries.shape
    wkv = packed[:, : 2 * width]
    wo = packed[:, 2 * width : 3 * width]
    wk = packed[:, 4 * width : 5 * width]
    tokens, flags = [], []
    for piece in pieces:
        held = piece[...].astype(jnp.float32)
        dead = held >= DEAD
        for begin in range(0, held.shape[0], tile):
            part = held[begin : begin + tile]
            gone = dead[begin : begin + tile]
            tokens.append(jnp.where(gone, part[:1], part).astype(jnp.bfloat16))
            flags.append(jnp.where(gone, 0.0, 1.0).astype(jnp.bfloat16))
    tokens = jnp.concatenate(tokens, axis=0)
    flags = jnp.concatenate(flags, axis=0)
    count = tokens.shape[0]
    kvm = dot(tokens, wkv).astype(jnp.bfloat16)
    keys = kvm[:, :width]
    values = kvm[:, width:] * flags
    lane_head = head_of_lane(count, width, heads)
    for head in range(heads):
        at = pl.ds(head * count, count)
        kbd[at, :] = only(keys, head, lane_head)
        vbd[at, :] = flagged(values, flags, head, heads, lane_head)
    middle = heads // 2 * count
    hsize = width // heads
    depth = qt.shape[0] // heads
    lanes = size_ref.shape[1]
    sizes = [jnp.zeros((1, lanes), jnp.float32)] * 2
    for begin in range(0, rows, block):
        at = pl.ds(begin, block)
        x = queries[at, :].astype(jnp.float32)
        scores = dot_t(qc[at, :], kbd[...])
        weights = []
        for head in range(heads):
            s = scores[:, head * count : (head + 1) * count]
            top = jnp.max(s, axis=-1, keepdims=True)
            weights.append(weigh(s, top, scales[head : head + 1, :1]))
        low = dot(jnp.concatenate(weights[: heads // 2], axis=1), vbd[:middle, :])
        high = dot(jnp.concatenate(weights[heads // 2 :], axis=1), vbd[middle:, :])
        x1 = x + dot(normed(low, high), wo)
        x1_ref[at, :] = x1
        hn1 = rms_round(x1)
        q = dot_t(wqt[...], hn1).astype(jnp.bfloat16)
        for head in range(heads):
            row = head * hsize
            target = pl.ds(head * depth + row % depth, hsize)
            qt[target, at] = q[row : row + hsize]
        key = dot(hn1, wk).astype(jnp.bfloat16)
        slot = lax.broadcasted_iota(jnp.int32, (block, width), 0) + begin
        if begin == 0:
            first = key[:1]
        key = jnp.where(slot < counts[:1, :1], key, first)
        kv_ref[at, :] = key
        new = (query_sizes(q, scales, heads), key_sizes(key, heads, lanes))
        sizes = [jnp.maximum(a, b) for a, b in zip(sizes, new)]
        value = dot_t(wvt[...], hn1).astype(jnp.bfloat16)
        slot = lax.broadcasted_iota(jnp.int32, (width, block), 1) + begin
        value = jnp.where(slot < counts[:1, :1], value, jnp.bfloat16(DEAD_V))
        for part in range(0, block, width):
            place = begin + part
            size = min(block, width)
            target = pl.ds(rows + place // width * width, width)
            spot = pl.ds(place % width, size)
            kv_ref[target, spot] = value[:, part : part + size]
    size_ref[:heads, :] = jnp.broadcast_to(sizes[0], (heads, lanes))
    size_ref[heads:, :] = jnp.broadcast_to(sizes[1], (heads, lanes))


def transposed_values(kv, vt, heads):
    rows, width = vt.shape[1], kv.shape[1]
    hsize, part = width // heads, vt.shape[0] // heads
    for begin in range(0, rows, width):
        lanes = pl.ds(begin, width)
        values = kv[rows + begin : rows + begin + width, :]
        live = values < jnp.bfloat16(DEAD_V)
        flags = jnp.where(live[: part - hsize], jnp.bfloat16(1), jnp.bfloat16(0))
        values = jnp.where(live, values, jnp.bfloat16(0))
        for head in range(heads):
            at = head * part
            vt[at : at + hsize, lanes] = values[head * hsize : (head + 1) * hsize]
            vt[at + hsize : at + part, lanes] = flags


def head_rows(width, heads, lanes):
    row = lax.broadcasted_iota(jnp.int32, (width, lanes), 0) // (width // heads)
    lane = lax.broadcasted_iota(jnp.int32, (width, lanes), 1)
    return jnp.where(row == lane, 1.0, 0.0).astype(jnp.bfloat16)


def key_sizes(keys, heads, lanes):
    wide = keys.astype(jnp.float32)
    norms = dot((wide * wide).astype(jnp.bfloat16), head_rows(keys.shape[1], heads, lanes))
    return jnp.max(norms, axis=0, keepdims=True)


def query_sizes(q, scales, heads):
    hsize = q.shape[0] // heads
    lane = lax.broadcasted_iota(jnp.int32, (1, scales.shape[1]), 1)
    sizes = jnp.zeros((1, scales.shape[1]), jnp.float32)
    for head in range(heads):
        part = q[head * hsize : (head + 1) * hsize].astype(jnp.float32)
        norm = jnp.max(jnp.sum(part * part, axis=0, keepdims=True), axis=1, keepdims=True)
        scale = scales[heads + head : heads + head + 1, :]
        sizes = jnp.where(lane == head, norm * scale * scale, sizes)
    return sizes


def half_attention(scales, qt, kv, vt, heads, s_held, p_held, sizes, live, blocks, use):
    rows, width = vt.shape[1], kv.shape[1]
    part = vt.shape[0] // heads
    depth = qt.shape[0] // heads
    per = heads * depth // width
    block = s_held.shape[2]
    steps = rows // STEP
    bound = jnp.max(sizes, axis=1, keepdims=True)
    choice = jnp.max(jnp.where(bound <= LIMIT * LIMIT, live, float(steps + 1)))

    def score(head, at, keys):
        lanes = head // per * depth
        q = qt[head * depth : (head + 1) * depth, at]
        return dot(kv[:keys, lanes : lanes + depth], q)

    def scale_of(head):
        return scales[heads + head : heads + head + 1, :1]

    def unshifted(keys):
        zero = jnp.zeros((1, block), jnp.float32)

        def visit(index, carry):
            at = pl.ds(pl.multiple_of(index * block, block), block)
            for step in range(heads + 1):
                if step < heads:
                    weights = jnp.exp(score(step, at, keys) * scale_of(step))
                    p_held[step % 2, :keys, :] = weights.astype(jnp.bfloat16)
                last = step - 1
                if 0 <= last:
                    mine = vt[last * part : (last + 1) * part, :keys]
                    use(last, at, zero, dot(mine, p_held[last % 2, :keys, :]))
            return carry

        lax.fori_loop(0, blocks, visit, 0)

    for step in range(1, steps + 1):
        pl.when(choice == float(step))(functools.partial(unshifted, step * STEP))

    @pl.when(choice > float(steps))
    def shifted():
        begins = range(0, rows, block)
        units = [(head, pl.ds(begin, block)) for head in range(heads) for begin in begins]
        tops = {}
        for step in range(len(units) + 2):
            if step < len(units):
                s = score(*units[step], rows)
                s_held[step % 2] = s
                tops[step] = jnp.max(s, axis=0, keepdims=True)
            last = step - 1
            if 0 <= last < len(units):
                p_held[last % 2] = weigh(s_held[last % 2], tops[last], scale_of(units[last][0]))
            last = step - 2
            if 0 <= last:
                head, at = units[last]
                mine = vt[head * part : (head + 1) * part, :]
                use(head, at, tops[last], dot(mine, p_held[last % 2]))


def own_kernel(heads, counts, scales, kv, qt, size_ref, top_ref, sum_ref, vt, s_held, p_held):
    part = vt.shape[0] // heads
    sizes = size_ref[:1, :] * size_ref[heads : heads + 1, :]
    transposed_values(kv, vt, heads)

    def use(head, at, top, total):
        top_ref[head : head + 1, at] = top
        sum_ref[head * part : (head + 1) * part, at] = total

    block = s_held.shape[2]
    blocks = lax.div(counts[0] + block - 1, block)
    steps = lax.div(counts[0] + STEP - 1, STEP).astype(jnp.float32)
    half_attention(scales, qt, kv, vt, heads, s_held, p_held, sizes, steps, blocks, use)


def rest_kernel(
    heads,
    counts,
    scales,
    x1_ref,
    kv,
    qt,
    top_ref,
    sum_ref,
    size_ref,
    packed,
    down_held,
    w3,
    features,
    boxes,
    vt,
    s_held,
    p_held,
    ctx,
    out,
    upper,
    w3_held,
    sems,
):
    rows, width = x1_ref.shape
    hsize = width // heads
    part = vt.shape[0] // heads
    wo_held = packed[:, 6 * width : 7 * width]
    w1_held = packed[:, 7 * width : 8 * width]
    w2_held = packed[:, 8 * width : 9 * width]
    up_held = packed.at[:, pl.ds(9 * width, down_held.shape[0])]
    copies = [pltpu.make_async_copy(w3, w3_held, sems.at[0])]
    copies[0].start()
    transposed_values(kv, vt, heads)

    def use(head, at, top, total):
        scale = scales[heads + head : heads + head + 1, :1]
        first = top_ref[head : head + 1, at]
        most = jnp.maximum(first, top)
        total = total * jnp.exp((top - most) * scale)
        total += sum_ref[head * part : (head + 1) * part, at] * jnp.exp((first - most) * scale)
        mixed = total[:hsize] / total[hsize : hsize + 1]
        ctx[head * hsize : (head + 1) * hsize, at] = mixed.astype(jnp.bfloat16)

    block = upper.shape[1]
    count = counts[0]
    blocks = lax.div(count + block - 1, block)
    steps = jnp.ones((1, 1), jnp.float32)
    for token in range(STEP, rows, STEP):
        row = rows + token // width * width
        mark = kv[row : row + 1, token % width : token % width + 1].astype(jnp.float32)
        steps += jnp.where(mark < DEAD_V, 1.0, 0.0)
    sizes = size_ref[:1, :] * key_sizes(kv[:rows, :], heads, size_ref.shape[1])
    half_attention(scales, qt, kv, vt, heads, s_held, p_held, sizes, steps, blocks, use)
    for copy in copies:
        copy.wait()
    starts = list(range(0, rows, block))
    ff = down_held.shape[0]
    chunk = ff // 4
    x2, x3 = {}, {}

    def leave(i):
        at = pl.ds(starts[i], block)
        return pltpu.make_async_copy(out.at[at, :], features.at[at, :], sems.at[len(copies) + i])

    def project(i):
        at = pl.ds(starts[i], block)
        mixed = lax.dot_general(
            ctx[:, at], wo_held, (((0,), (0,)), ((), ())), preferred_element_type=jnp.float32
        )
        x2[i] = x1_ref[at, :] + mixed

    def widen(i):
        hn2 = rms_round(x2[i])
        for begin in range(0, ff, chunk):
            cut = pl.ds(begin, chunk)
            upper[i % 2, :, cut] = jnp.maximum(dot(hn2, up_held[:, cut]), 0.0).astype(jnp.bfloat16)

    def narrow(i):
        at = pl.ds(starts[i], block)
        x3[i] = x2[i] + dot(upper[i % 2], down_held[...])
        slot = lax.broadcasted_iota(jnp.int32, (block, width), 0) + starts[i]
        out[at, :] = jnp.where(slot < count, x3[i], 0.0)
        leave(i).start()

    def box(i):
        b1 = jnp.maximum(dot(rms_round(x3[i]), w1_held), 0.0).astype(jnp.bfloat16)
        b2 = jnp.maximum(dot(b1, w2_held), 0.0).astype(jnp.bfloat16)
        raw = dot_t(w3_held[...], b2)
        slot = lax.broadcasted_iota(jnp.int32, raw.shape, 1) + starts[i]
        boxes[:, pl.ds(starts[i], block)] = jnp.where(
            slot < count, 1.0 / (1.0 + jnp.exp(-raw)), 0.0
        )

    def finish(live):
        for i in range(live, len(starts)):
            at = pl.ds(starts[i], block)
            out[at, :] = jnp.zeros((block, width), jnp.float32)
            boxes[:, at] = jnp.zeros((boxes.shape[0], block), jnp.float32)
            leave(i).start()
        for step in range(live + 3):
            for stage, work in enumerate((project, widen, narrow, box)):
                if 0 <= step - stage < live:
                    work(step - stage)

    for live in range(1, len(starts) + 1):
        pl.when(blocks == live)(functools.partial(finish, live))
    for i in range(len(starts)):
        leave(i).wait()


def in_hbm(x):
    return pltpu.with_memory_space_constraint(x, pltpu.HBM)


def swap(x, axis):
    size = lax.axis_size(axis)
    return lax.ppermute(x, axis, [(i, i ^ 1) for i in range(size)])


def local(
    queries,
    counts,
    memory,
    mem_mask,
    cross_wq,
    cross_wkv,
    cross_wo,
    self_wqkv,
    self_wo,
    ffn_up,
    ffn_down,
    box_w1,
    box_w2,
    box_w3,
    cross_temp,
    self_temp,
):
    rows, width = queries.shape
    heads = cross_temp.shape[0]
    tile = memory.shape[0]
    params = pltpu.CompilerParams(vmem_limit_bytes=32 * 2**20)
    marked = pl.pallas_call(
        mark_kernel,
        out_shape=pltpu.VMEM((lax.axis_size("row"), tile, width), memory.dtype),
        in_specs=[HBM, HBM],
        out_specs=VMEM,
        scratch_shapes=[
            pltpu.VMEM(memory.shape, memory.dtype),
            pltpu.SMEM(mem_mask.shape, mem_mask.dtype),
            pltpu.SemaphoreType.DMA((2,)),
        ],
        name="mark",
    )(in_hbm(memory), in_hbm(mem_mask))
    gathered = lax.all_to_all(marked, "row", 0, 0, tiled=True)
    pieces = [gathered.reshape(-1, width)]
    tokens = pltpu.VMEM((rows, width), jnp.bfloat16)
    flat = (cross_wkv, cross_wo, self_wqkv, self_wo, box_w1, box_w2, ffn_up)
    packed_width = sum(w.shape[1] for w in flat)
    sources = (queries, cross_wq, cross_temp, self_temp, *flat, ffn_down)
    depth = min(128, width)
    qt_shape = pltpu.VMEM((heads * depth, rows), jnp.bfloat16)
    x, qc, scales, live, packed, wvt, wqt, down = pl.pallas_call(
        load_kernel,
        out_shape=[
            tokens,
            tokens,
            pltpu.VMEM((2 * heads, 128), jnp.float32),
            pltpu.VMEM((8, 128), jnp.int32),
            pltpu.VMEM((width, packed_width), jnp.bfloat16),
            pltpu.VMEM((width, width), jnp.bfloat16),
            pltpu.VMEM((width, width), jnp.bfloat16),
            pltpu.VMEM(ffn_down.shape, jnp.bfloat16),
        ],
        in_specs=[SMEM] + [HBM] * len(sources),
        out_specs=[VMEM] * 8,
        scratch_shapes=[
            pltpu.VMEM(cross_wq.shape, cross_wq.dtype),
            pltpu.SMEM(cross_temp.shape, cross_temp.dtype),
            pltpu.SMEM(self_temp.shape, self_temp.dtype),
            pltpu.SemaphoreType.DMA((len(sources),)),
        ],
        compiler_params=params,
        cost_estimate=pl.CostEstimate(
            flops=2 * rows * width * width, bytes_accessed=4 * 2**20, transcendentals=0
        ),
        name="load",
    )(counts, *map(in_hbm, sources))
    count = sum(piece.shape[0] for piece in pieces)
    block = rows if count <= 128 else min(rows, 128)
    kv_shape = pltpu.VMEM((2 * rows, width), jnp.bfloat16)
    x1, qt, sizes, kv = pl.pallas_call(
        functools.partial(cross_kernel, len(pieces), block, tile, heads),
        out_shape=(
            pltpu.VMEM((rows, width), jnp.float32),
            qt_shape,
            pltpu.VMEM((2 * heads, 128), jnp.float32),
            kv_shape,
        ),
        in_specs=[VMEM] * (7 + len(pieces)),
        out_specs=(VMEM, VMEM, VMEM, VMEM),
        scratch_shapes=[
            pltpu.VMEM((heads * count, width), jnp.bfloat16),
            pltpu.VMEM((heads * count, width), jnp.bfloat16),
        ],
        compiler_params=params,
        name="cross",
    )(scales, live, x, qc, *pieces, packed, wvt, wqt)
    other = swap(kv, "col")
    part = width // heads + 16
    block = min(256, rows)
    held = [
        pltpu.VMEM((heads * part, rows), jnp.bfloat16),
        pltpu.VMEM((2, rows, block), jnp.float32),
        pltpu.VMEM((2, rows, block), jnp.bfloat16),
    ]
    tops, sums = pl.pallas_call(
        functools.partial(own_kernel, heads),
        out_shape=(
            pltpu.VMEM((heads, rows), jnp.float32),
            pltpu.VMEM((heads * part, rows), jnp.float32),
        ),
        in_specs=[SMEM] + [VMEM] * 4,
        out_specs=(VMEM, VMEM),
        scratch_shapes=held,
        compiler_params=params,
        cost_estimate=pl.CostEstimate(
            flops=8 * heads * rows * rows * width, bytes_accessed=2**20, transcendentals=0
        ),
        name="own",
    )(counts, scales, kv, qt, sizes)
    last = jnp.transpose(box_w3)
    return pl.pallas_call(
        functools.partial(rest_kernel, heads),
        out_shape=(
            jax.ShapeDtypeStruct((rows, width), jnp.float32),
            jax.ShapeDtypeStruct((box_w3.shape[1], rows), jnp.float32),
        ),
        in_specs=[SMEM] + [VMEM] * 9 + [HBM],
        out_specs=(HBM, VMEM),
        scratch_shapes=held
        + [
            pltpu.VMEM((width, rows), jnp.bfloat16),
            pltpu.VMEM((rows, width), jnp.float32),
            pltpu.VMEM((2, block, ffn_up.shape[1]), jnp.bfloat16),
        ]
        + [
            pltpu.VMEM(last.shape, last.dtype),
            pltpu.SemaphoreType.DMA((1 + rows // block,)),
        ],
        compiler_params=params,
        name="rest",
    )(counts, scales, x1, other, qt, tops, sums, sizes, packed, down, in_hbm(last))


def solution(mesh):
    return jax.shard_map(
        local,
        mesh=mesh,
        in_specs=(
            P(("parts", "row", "col"), None),
            P(("parts", "row", "col")),
            P(("parts", "row", "col"), None),
            P(("parts", "row", "col")),
            P(),
            P(),
            P(),
            P(),
            P(),
            P(),
            P(),
            P(),
            P(),
            P(),
            P(),
            P(),
        ),
        out_specs=(P(("parts", "row", "col"), None), P(None, ("parts", "row", "col"))),
        check_vma=False,
    )
```

```python
import functools
import math

import jax
import jax.numpy as jnp
from jax import lax
from jax.experimental import pallas as pl
from jax.experimental.pallas import tpu as pltpu
from jax.sharding import PartitionSpec as P

EPS = 1e-06
DEAD = 64.0
DEAD_V = 4096.0
STEP = 128
LIMIT = 77.0
SHIFT = 7.0
VMEM = pl.BlockSpec(memory_space=pltpu.VMEM)
SMEM = pl.BlockSpec(memory_space=pltpu.SMEM)
HBM = pl.BlockSpec(memory_space=pltpu.HBM)


def rms_round(x):
    return (x * lax.rsqrt(jnp.mean(x * x, axis=-1, keepdims=True) + EPS)).astype(jnp.bfloat16)


def dot(a, b):
    return jnp.dot(a, b, preferred_element_type=jnp.float32)


def dot_t(a, b):
    return lax.dot_general(a, b, (((1,), (1,)), ((), ())), preferred_element_type=jnp.float32)


def head_of_lane(rows, width, heads):
    return lax.broadcasted_iota(jnp.int32, (rows, width), 1) // (width // heads)


def only(x, head, lane_head):
    return jnp.where(lane_head == head, x, jnp.zeros_like(x))


def flagged(values, flags, head, heads, lane_head):
    other = (head + heads // 2) % heads
    rest = jnp.where(lane_head == other, flags, jnp.zeros_like(values))
    return jnp.where(lane_head == head, values, rest)


def weigh(scores, top, scale):
    return jnp.exp((scores - top) * scale).astype(jnp.bfloat16)


def normed(low, high):
    half = low.shape[1] // 2
    return jnp.concatenate(
        [low[:, :half] / low[:, half:], high[:, half:] / high[:, :half]], axis=1
    ).astype(jnp.bfloat16)


def mark_kernel(memory, mask, out, held, flags, sems):
    copies = [
        pltpu.make_async_copy(memory, held, sems.at[0]),
        pltpu.make_async_copy(mask, flags, sems.at[1]),
    ]
    for copy in copies:
        copy.start()
    for copy in copies:
        copy.wait()
    row = lax.broadcasted_iota(jnp.int32, held.shape, 0)
    tokens = held[...].astype(jnp.float32)
    for j in range(held.shape[0]):
        tokens = jnp.where((row == j) & (flags[j] <= 0), DEAD, tokens)
    tokens = tokens.astype(jnp.bfloat16)
    for copy in range(out.shape[0]):
        out[copy] = tokens


def load_kernel(
    counts,
    queries,
    wq,
    cross_temp,
    self_temp,
    wkv,
    wo,
    wqkv,
    x_ref,
    qc_ref,
    scale_ref,
    count_ref,
    packed,
    wvt_ref,
    wqt_ref,
    wq_held,
    cross_held,
    self_held,
    sems,
):
    width = x_ref.shape[1]
    pairs = [(queries, x_ref), (wq, wq_held), (cross_temp, cross_held), (self_temp, self_held)]
    begin = 0
    for source in (wkv, wo, wqkv):
        end = begin + source.shape[1]
        pairs.append((source, packed.at[:, begin:end]))
        begin = end
    copies = [pltpu.make_async_copy(a, b, sems.at[i]) for i, (a, b) in enumerate(pairs)]
    for copy in copies:
        copy.start()
    for copy in copies[:4]:
        copy.wait()
    heads = cross_temp.shape[0]
    factor = 1.0 / math.sqrt(width // heads)
    lanes = scale_ref.shape[1]
    for side, temp in enumerate((cross_held, self_held)):
        for head in range(heads):
            at = pl.ds(side * heads + head, 1)
            scale_ref[at, :] = jnp.full((1, lanes), temp[head] * factor, jnp.float32)
    count_ref[...] = jnp.full(count_ref.shape, counts[0], jnp.int32)
    x = x_ref[...].astype(jnp.float32)
    qc_ref[...] = dot(rms_round(x), wq_held[...]).astype(jnp.bfloat16)
    for copy in copies[4:]:
        copy.wait()
    wvt_ref[...] = jnp.transpose(packed[:, -width:])
    wqt_ref[...] = jnp.transpose(packed[:, -3 * width : -2 * width])


def cross_kernel(n, block, tile, heads, scales, counts, queries, qc, *refs):
    pieces = refs[:n]
    packed, wvt, x1_ref, hn_ref, kv_ref, kbd, vbd = refs[n:]
    rows, width = queries.shape
    wkv = packed[:, : 2 * width]
    wo = packed[:, 2 * width : 3 * width]
    wk = packed[:, 4 * width : 5 * width]
    tokens, flags = [], []
    for piece in pieces:
        held = piece[...].astype(jnp.float32)
        dead = held >= DEAD
        for begin in range(0, held.shape[0], tile):
            part = held[begin : begin + tile]
            gone = dead[begin : begin + tile]
            tokens.append(jnp.where(gone, part[:1], part).astype(jnp.bfloat16))
            flags.append(jnp.where(gone, 0.0, 1.0).astype(jnp.bfloat16))
    tokens = jnp.concatenate(tokens, axis=0)
    flags = jnp.concatenate(flags, axis=0)
    count = tokens.shape[0]
    kvm = dot(tokens, wkv).astype(jnp.bfloat16)
    keys = kvm[:, :width]
    values = kvm[:, width:] * flags
    lane_head = head_of_lane(count, width, heads)
    for head in range(heads):
        at = pl.ds(head * count, count)
        kbd[at, :] = only(keys, head, lane_head)
        vbd[at, :] = flagged(values, flags, head, heads, lane_head)
    middle = heads // 2 * count
    for begin in range(0, rows, block):
        at = pl.ds(begin, block)
        x = queries[at, :].astype(jnp.float32)
        scores = dot_t(qc[at, :], kbd[...])
        weights = []
        for head in range(heads):
            s = scores[:, head * count : (head + 1) * count]
            top = jnp.max(s, axis=-1, keepdims=True)
            weights.append(weigh(s, top, scales[head : head + 1, :1]))
        low = dot(jnp.concatenate(weights[: heads // 2], axis=1), vbd[:middle, :])
        high = dot(jnp.concatenate(weights[heads // 2 :], axis=1), vbd[middle:, :])
        x1 = x + dot(normed(low, high), wo)
        x1_ref[at, :] = x1
        hn1 = rms_round(x1)
        hn_ref[at, :] = hn1
        key = dot(hn1, wk).astype(jnp.bfloat16)
        slot = lax.broadcasted_iota(jnp.int32, (block, width), 0) + begin
        if begin == 0:
            first = key[:1]
        kv_ref[at, :] = jnp.where(slot < counts[:1, :1], key, first)
        value = dot_t(wvt[...], hn1).astype(jnp.bfloat16)
        slot = lax.broadcasted_iota(jnp.int32, (width, block), 1) + begin
        value = jnp.where(slot < counts[:1, :1], value, jnp.bfloat16(DEAD_V))
        for part in range(0, block, width):
            place = begin + part
            size = min(block, width)
            target = pl.ds(rows + place // width * width, width)
            lanes = pl.ds(place % width, size)
            kv_ref[target, lanes] = value[:, part : part + size]


def transposed_values(kv, vt, heads):
    rows, width = vt.shape[1], kv.shape[1]
    hsize, part = width // heads, vt.shape[0] // heads
    for begin in range(0, rows, width):
        lanes = pl.ds(begin, width)
        values = kv[rows + begin : rows + begin + width, :]
        live = values < jnp.bfloat16(DEAD_V)
        flags = jnp.where(live[: part - hsize], jnp.bfloat16(1), jnp.bfloat16(0))
        values = jnp.where(live, values, jnp.bfloat16(0))
        for head in range(heads):
            at = head * part
            vt[at : at + hsize, lanes] = values[head * hsize : (head + 1) * hsize]
            vt[at + hsize : at + part, lanes] = flags


def head_rows(width, heads, lanes):
    row = lax.broadcasted_iota(jnp.int32, (width, lanes), 0) // (width // heads)
    lane = lax.broadcasted_iota(jnp.int32, (width, lanes), 1)
    return jnp.where(row == lane, 1.0, 0.0).astype(jnp.bfloat16)


def key_sizes(keys, heads, lanes):
    wide = keys.astype(jnp.float32)
    norms = dot((wide * wide).astype(jnp.bfloat16), head_rows(keys.shape[1], heads, lanes))
    return jnp.max(norms, axis=0, keepdims=True)


def query_sizes(q, scales, heads):
    hsize = q.shape[0] // heads
    lane = lax.broadcasted_iota(jnp.int32, (1, scales.shape[1]), 1)
    sizes = jnp.zeros((1, scales.shape[1]), jnp.float32)
    for head in range(heads):
        part = q[head * hsize : (head + 1) * hsize].astype(jnp.float32)
        norm = jnp.max(jnp.sum(part * part, axis=0, keepdims=True), axis=1, keepdims=True)
        scale = scales[heads + head : heads + head + 1, :]
        sizes = jnp.where(lane == head, norm * scale * scale, sizes)
    return sizes


def half_attention(scales, qt, kv, vt, heads, s_held, p_held, sizes, live, blocks, own, use):
    rows, width = vt.shape[1], kv.shape[1]
    part = vt.shape[0] // heads
    depth = qt.shape[0] // heads
    per = heads * depth // width
    block = s_held.shape[2]
    steps = rows // STEP
    bound = jnp.max(sizes * key_sizes(kv[:rows, :], heads, sizes.shape[1]), axis=1, keepdims=True)
    choice = jnp.max(jnp.where(bound <= LIMIT * LIMIT, live, float(steps + 1)))

    def score(head, at, keys):
        lanes = head // per * depth
        q = qt[head * depth : (head + 1) * depth, at]
        return dot(kv[:keys, lanes : lanes + depth], q)

    def scale_of(head):
        return scales[heads + head : heads + head + 1, :1]

    def unshifted(keys, live_blocks):
        begins = range(0, live_blocks * block, block)
        units = [(head, pl.ds(begin, block)) for head in range(heads) for begin in begins]
        for step in range(len(units) + 1):
            if step < len(units):
                head, at = units[step]
                weights = jnp.exp(score(head, at, keys) * scale_of(head) - SHIFT)
                p_held[step % 2, :keys, :] = weights.astype(jnp.bfloat16)
            last = step - 1
            if 0 <= last:
                head, at = units[last]
                mine = vt[head * part : (head + 1) * part, :keys]
                top = jnp.broadcast_to(SHIFT / scale_of(head), (1, block))
                use(head, at, top, dot(mine, p_held[last % 2, :keys, :]))

    for step in range(1, steps + 1):
        for live_blocks in range(1, rows // block + 1):
            if own and not 0 < step * STEP - (live_blocks - 1) * block <= block:
                continue
            here = (choice == float(step)) & (blocks == live_blocks)
            pl.when(here)(functools.partial(unshifted, step * STEP, live_blocks))

    @pl.when(choice > float(steps))
    def shifted():
        begins = range(0, rows, block)
        units = [(head, pl.ds(begin, block)) for head in range(heads) for begin in begins]
        tops = {}
        for step in range(len(units) + 2):
            if step < len(units):
                s = score(*units[step], rows)
                s_held[step % 2] = s
                tops[step] = jnp.max(s, axis=0, keepdims=True)
            last = step - 1
            if 0 <= last < len(units):
                p_held[last % 2] = weigh(s_held[last % 2], tops[last], scale_of(units[last][0]))
            last = step - 2
            if 0 <= last:
                head, at = units[last]
                mine = vt[head * part : (head + 1) * part, :]
                use(head, at, tops[last], dot(mine, p_held[last % 2]))


def own_kernel(
    heads, counts, scales, hn, kv, wqt, qt, top_ref, sum_ref, size_ref, vt, s_held, p_held
):
    width = hn.shape[1]
    hsize = width // heads
    depth = qt.shape[0] // heads
    part = vt.shape[0] // heads
    q = dot_t(wqt[...], hn[...]).astype(jnp.bfloat16)
    sizes = query_sizes(q, scales, heads)
    size_ref[...] = jnp.broadcast_to(sizes, size_ref.shape)
    qt[...] = jnp.zeros_like(qt)
    for head in range(heads):
        begin = head * hsize
        at = head * depth + begin % depth
        qt[at : at + hsize, :] = q[begin : begin + hsize]
    transposed_values(kv, vt, heads)

    def use(head, at, top, total):
        top_ref[head : head + 1, at] = top
        sum_ref[head * part : (head + 1) * part, at] = total

    block = s_held.shape[2]
    blocks = lax.div(counts[0] + block - 1, block)
    steps = lax.div(counts[0] + STEP - 1, STEP).astype(jnp.float32)
    half_attention(scales, qt, kv, vt, heads, s_held, p_held, sizes, steps, blocks, True, use)


def rest_kernel(
    heads,
    counts,
    scales,
    x1_ref,
    kv,
    qt,
    top_ref,
    sum_ref,
    size_ref,
    wo,
    up,
    down,
    w1,
    w2,
    w3,
    features,
    boxes,
    vt,
    s_held,
    p_held,
    ctx,
    out,
    upper,
    wo_held,
    up_held,
    down_held,
    w1_held,
    w2_held,
    w3_held,
    sems,
):
    rows, width = x1_ref.shape
    hsize = width // heads
    part = vt.shape[0] // heads
    held = (wo_held, up_held, down_held, w1_held, w2_held, w3_held)
    pairs = zip((wo, up, down, w1, w2, w3), held)
    copies = [pltpu.make_async_copy(a, b, sems.at[i]) for i, (a, b) in enumerate(pairs)]
    for copy in copies:
        copy.start()
    transposed_values(kv, vt, heads)

    def use(head, at, top, total):
        scale = scales[heads + head : heads + head + 1, :1]
        first = top_ref[head : head + 1, at]
        most = jnp.maximum(first, top)
        total = total * jnp.exp((top - most) * scale)
        total += sum_ref[head * part : (head + 1) * part, at] * jnp.exp((first - most) * scale)
        mixed = total[:hsize] / total[hsize : hsize + 1]
        ctx[head * hsize : (head + 1) * hsize, at] = mixed.astype(jnp.bfloat16)

    block = upper.shape[1]
    count = counts[0]
    blocks = lax.div(count + block - 1, block)
    steps = jnp.ones((1, 1), jnp.float32)
    for token in range(STEP, rows, STEP):
        row = rows + token // width * width
        mark = kv[row : row + 1, token % width : token % width + 1].astype(jnp.float32)
        steps += jnp.where(mark < DEAD_V, 1.0, 0.0)
    half_attention(
        scales, qt, kv, vt, heads, s_held, p_held, size_ref[:1, :], steps, blocks, False, use
    )
    for copy in copies:
        copy.wait()
    starts = list(range(0, rows, block))
    ff = up_held.shape[1]
    chunk = ff // 4
    x2, x3 = {}, {}

    def leave(i):
        at = pl.ds(starts[i], block)
        return pltpu.make_async_copy(out.at[at, :], features.at[at, :], sems.at[len(copies) + i])

    def project(i):
        at = pl.ds(starts[i], block)
        mixed = lax.dot_general(
            ctx[:, at], wo_held[...], (((0,), (0,)), ((), ())), preferred_element_type=jnp.float32
        )
        x2[i] = x1_ref[at, :] + mixed

    def widen(i):
        hn2 = rms_round(x2[i])
        for begin in range(0, ff, chunk):
            cut = pl.ds(begin, chunk)
            upper[i % 2, :, cut] = jnp.maximum(dot(hn2, up_held[:, cut]), 0.0).astype(jnp.bfloat16)

    def narrow(i):
        at = pl.ds(starts[i], block)
        x3[i] = x2[i] + dot(upper[i % 2], down_held[...])
        slot = lax.broadcasted_iota(jnp.int32, (block, width), 0) + starts[i]
        out[at, :] = jnp.where(slot < count, x3[i], 0.0)
        leave(i).start()

    def box(i):
        b1 = jnp.maximum(dot(rms_round(x3[i]), w1_held[...]), 0.0).astype(jnp.bfloat16)
        b2 = jnp.maximum(dot(b1, w2_held[...]), 0.0).astype(jnp.bfloat16)
        raw = dot_t(w3_held[...], b2)
        slot = lax.broadcasted_iota(jnp.int32, raw.shape, 1) + starts[i]
        boxes[:, pl.ds(starts[i], block)] = jnp.where(
            slot < count, 1.0 / (1.0 + jnp.exp(-raw)), 0.0
        )

    def finish(live):
        for i in range(live, len(starts)):
            at = pl.ds(starts[i], block)
            out[at, :] = jnp.zeros((block, width), jnp.float32)
            boxes[:, at] = jnp.zeros((boxes.shape[0], block), jnp.float32)
            leave(i).start()
        for step in range(live + 3):
            for stage, work in enumerate((project, widen, narrow, box)):
                if 0 <= step - stage < live:
                    work(step - stage)

    for live in range(1, len(starts) + 1):
        pl.when(blocks == live)(functools.partial(finish, live))
    for i in range(len(starts)):
        leave(i).wait()


def in_hbm(x):
    return pltpu.with_memory_space_constraint(x, pltpu.HBM)


def swap(x, axis):
    size = lax.axis_size(axis)
    return lax.ppermute(x, axis, [(i, i ^ 1) for i in range(size)])


def local(
    queries,
    counts,
    memory,
    mem_mask,
    cross_wq,
    cross_wkv,
    cross_wo,
    self_wqkv,
    self_wo,
    ffn_up,
    ffn_down,
    box_w1,
    box_w2,
    box_w3,
    cross_temp,
    self_temp,
):
    rows, width = queries.shape
    heads = cross_temp.shape[0]
    tile = memory.shape[0]
    params = pltpu.CompilerParams(vmem_limit_bytes=32 * 2**20)
    marked = pl.pallas_call(
        mark_kernel,
        out_shape=pltpu.VMEM((lax.axis_size("row"), tile, width), memory.dtype),
        in_specs=[HBM, HBM],
        out_specs=VMEM,
        scratch_shapes=[
            pltpu.VMEM(memory.shape, memory.dtype),
            pltpu.SMEM(mem_mask.shape, mem_mask.dtype),
            pltpu.SemaphoreType.DMA((2,)),
        ],
        name="mark",
    )(in_hbm(memory), in_hbm(mem_mask))
    gathered = lax.all_to_all(marked, "row", 0, 0, tiled=True)
    pieces = [gathered.reshape(-1, width)]
    tokens = pltpu.VMEM((rows, width), jnp.bfloat16)
    packed_width = cross_wkv.shape[1] + cross_wo.shape[1] + self_wqkv.shape[1]
    sources = (queries, cross_wq, cross_temp, self_temp, cross_wkv, cross_wo, self_wqkv)
    x, qc, scales, live, packed, wvt, wqt = pl.pallas_call(
        load_kernel,
        out_shape=[
            tokens,
            tokens,
            pltpu.VMEM((2 * heads, 128), jnp.float32),
            pltpu.VMEM((8, 128), jnp.int32),
            pltpu.VMEM((width, packed_width), jnp.bfloat16),
            pltpu.VMEM((width, width), jnp.bfloat16),
            pltpu.VMEM((width, width), jnp.bfloat16),
        ],
        in_specs=[SMEM] + [HBM] * len(sources),
        out_specs=[VMEM] * 7,
        scratch_shapes=[
            pltpu.VMEM(cross_wq.shape, cross_wq.dtype),
            pltpu.SMEM(cross_temp.shape, cross_temp.dtype),
            pltpu.SMEM(self_temp.shape, self_temp.dtype),
            pltpu.SemaphoreType.DMA((len(sources),)),
        ],
        compiler_params=params,
        cost_estimate=pl.CostEstimate(
            flops=2 * rows * width * width, bytes_accessed=4 * 2**20, transcendentals=0
        ),
        name="load",
    )(counts, *map(in_hbm, sources))
    count = sum(piece.shape[0] for piece in pieces)
    block = rows if count <= 128 else min(rows, 128)
    kv_shape = pltpu.VMEM((2 * rows, width), jnp.bfloat16)
    x1, hn, kv = pl.pallas_call(
        functools.partial(cross_kernel, len(pieces), block, tile, heads),
        out_shape=(pltpu.VMEM((rows, width), jnp.float32), tokens, kv_shape),
        in_specs=[VMEM] * (6 + len(pieces)),
        out_specs=(VMEM, VMEM, VMEM),
        scratch_shapes=[
            pltpu.VMEM((heads * count, width), jnp.bfloat16),
            pltpu.VMEM((heads * count, width), jnp.bfloat16),
        ],
        compiler_params=params,
        name="cross",
    )(scales, live, x, qc, *pieces, packed, wvt)
    other = swap(kv, "col")
    part = width // heads + 16
    depth = min(128, width)
    block = min(256, rows)
    held = [
        pltpu.VMEM((heads * part, rows), jnp.bfloat16),
        pltpu.VMEM((2, rows, block), jnp.float32),
        pltpu.VMEM((2, rows, block), jnp.bfloat16),
    ]
    qt, tops, sums, sizes = pl.pallas_call(
        functools.partial(own_kernel, heads),
        out_shape=(
            pltpu.VMEM((heads * depth, rows), jnp.bfloat16),
            pltpu.VMEM((heads, rows), jnp.float32),
            pltpu.VMEM((heads * part, rows), jnp.float32),
            pltpu.VMEM((8, 128), jnp.float32),
        ),
        in_specs=[SMEM] + [VMEM] * 4,
        out_specs=(VMEM, VMEM, VMEM, VMEM),
        scratch_shapes=held,
        compiler_params=params,
        cost_estimate=pl.CostEstimate(
            flops=8 * heads * rows * rows * width, bytes_accessed=2**20, transcendentals=0
        ),
        name="own",
    )(counts, scales, hn, kv, wqt)
    late = (self_wo, ffn_up, ffn_down, box_w1, box_w2, jnp.transpose(box_w3))
    return pl.pallas_call(
        functools.partial(rest_kernel, heads),
        out_shape=(
            jax.ShapeDtypeStruct((rows, width), jnp.float32),
            jax.ShapeDtypeStruct((box_w3.shape[1], rows), jnp.float32),
        ),
        in_specs=[SMEM] + [VMEM] * 7 + [HBM] * len(late),
        out_specs=(HBM, VMEM),
        scratch_shapes=held
        + [
            pltpu.VMEM((width, rows), jnp.bfloat16),
            pltpu.VMEM((rows, width), jnp.float32),
            pltpu.VMEM((2, block, ffn_up.shape[1]), jnp.bfloat16),
        ]
        + [pltpu.VMEM(w.shape, w.dtype) for w in late]
        + [pltpu.SemaphoreType.DMA((len(late) + rows // block,))],
        compiler_params=params,
        name="rest",
    )(counts, scales, x1, other, qt, tops, sums, sizes, *map(in_hbm, late))


def solution(mesh):
    return jax.shard_map(
        local,
        mesh=mesh,
        in_specs=(
            P(("parts", "row", "col"), None),
            P(("parts", "row", "col")),
            P(("parts", "row", "col"), None),
            P(("parts", "row", "col")),
            P(),
            P(),
            P(),
            P(),
            P(),
            P(),
            P(),
            P(),
            P(),
            P(),
            P(),
            P(),
        ),
        out_specs=(P(("parts", "row", "col"), None), P(None, ("parts", "row", "col"))),
        check_vma=False,
    )
```

```python
import functools
import math

import jax
import jax.numpy as jnp
from jax import lax
from jax.experimental import pallas as pl
from jax.experimental.pallas import tpu as pltpu
from jax.sharding import PartitionSpec as P

EPS = 1e-06
DEAD = 64.0
DEAD_V = 4096.0
STEP = 128
LIMIT = 77.0
SHIFT = 7.0
VMEM = pl.BlockSpec(memory_space=pltpu.VMEM)
SMEM = pl.BlockSpec(memory_space=pltpu.SMEM)
HBM = pl.BlockSpec(memory_space=pltpu.HBM)


def rms_round(x):
    return (x * lax.rsqrt(jnp.mean(x * x, axis=-1, keepdims=True) + EPS)).astype(jnp.bfloat16)


def dot(a, b):
    return jnp.dot(a, b, preferred_element_type=jnp.float32)


def dot_t(a, b):
    return lax.dot_general(a, b, (((1,), (1,)), ((), ())), preferred_element_type=jnp.float32)


def head_of_lane(rows, width, heads):
    return lax.broadcasted_iota(jnp.int32, (rows, width), 1) // (width // heads)


def only(x, head, lane_head):
    return jnp.where(lane_head == head, x, jnp.zeros_like(x))


def flagged(values, flags, head, heads, lane_head):
    other = (head + heads // 2) % heads
    rest = jnp.where(lane_head == other, flags, jnp.zeros_like(values))
    return jnp.where(lane_head == head, values, rest)


def weigh(scores, top, scale):
    return jnp.exp((scores - top) * scale).astype(jnp.bfloat16)


def normed(low, high):
    half = low.shape[1] // 2
    return jnp.concatenate(
        [low[:, :half] / low[:, half:], high[:, half:] / high[:, :half]], axis=1
    ).astype(jnp.bfloat16)


def mark_kernel(memory, mask, out, held, flags, sems):
    copies = [
        pltpu.make_async_copy(memory, held, sems.at[0]),
        pltpu.make_async_copy(mask, flags, sems.at[1]),
    ]
    for copy in copies:
        copy.start()
    for copy in copies:
        copy.wait()
    row = lax.broadcasted_iota(jnp.int32, held.shape, 0)
    tokens = held[...].astype(jnp.float32)
    for j in range(held.shape[0]):
        tokens = jnp.where((row == j) & (flags[j] <= 0), DEAD, tokens)
    tokens = tokens.astype(jnp.bfloat16)
    for copy in range(out.shape[0]):
        out[copy] = tokens


def load_kernel(
    counts,
    queries,
    wq,
    cross_temp,
    self_temp,
    wkv,
    wo,
    wqkv,
    x_ref,
    qc_ref,
    scale_ref,
    count_ref,
    packed,
    wvt_ref,
    wqt_ref,
    wq_held,
    cross_held,
    self_held,
    sems,
):
    width = x_ref.shape[1]
    pairs = [(queries, x_ref), (wq, wq_held), (cross_temp, cross_held), (self_temp, self_held)]
    begin = 0
    for source in (wkv, wo, wqkv):
        end = begin + source.shape[1]
        pairs.append((source, packed.at[:, begin:end]))
        begin = end
    copies = [pltpu.make_async_copy(a, b, sems.at[i]) for i, (a, b) in enumerate(pairs)]
    for copy in copies:
        copy.start()
    for copy in copies[:4]:
        copy.wait()
    heads = cross_temp.shape[0]
    factor = 1.0 / math.sqrt(width // heads)
    lanes = scale_ref.shape[1]
    for side, temp in enumerate((cross_held, self_held)):
        for head in range(heads):
            at = pl.ds(side * heads + head, 1)
            scale_ref[at, :] = jnp.full((1, lanes), temp[head] * factor, jnp.float32)
    count_ref[...] = jnp.full(count_ref.shape, counts[0], jnp.int32)
    x = x_ref[...].astype(jnp.float32)
    qc_ref[...] = dot(rms_round(x), wq_held[...]).astype(jnp.bfloat16)
    for copy in copies[4:]:
        copy.wait()
    wvt_ref[...] = jnp.transpose(packed[:, -width:])
    wqt_ref[...] = jnp.transpose(packed[:, -3 * width : -2 * width])


def cross_kernel(n, block, tile, heads, scales, counts, queries, qc, *refs):
    pieces = refs[:n]
    packed, wvt, x1_ref, hn_ref, kv_ref, kbd, vbd = refs[n:]
    rows, width = queries.shape
    wkv = packed[:, : 2 * width]
    wo = packed[:, 2 * width : 3 * width]
    wk = packed[:, 4 * width : 5 * width]
    tokens, flags = [], []
    for piece in pieces:
        held = piece[...].astype(jnp.float32)
        dead = held >= DEAD
        for begin in range(0, held.shape[0], tile):
            part = held[begin : begin + tile]
            gone = dead[begin : begin + tile]
            tokens.append(jnp.where(gone, part[:1], part).astype(jnp.bfloat16))
            flags.append(jnp.where(gone, 0.0, 1.0).astype(jnp.bfloat16))
    tokens = jnp.concatenate(tokens, axis=0)
    flags = jnp.concatenate(flags, axis=0)
    count = tokens.shape[0]
    kvm = dot(tokens, wkv).astype(jnp.bfloat16)
    keys = kvm[:, :width]
    values = kvm[:, width:] * flags
    lane_head = head_of_lane(count, width, heads)
    for head in range(heads):
        at = pl.ds(head * count, count)
        kbd[at, :] = only(keys, head, lane_head)
        vbd[at, :] = flagged(values, flags, head, heads, lane_head)
    middle = heads // 2 * count
    for begin in range(0, rows, block):
        at = pl.ds(begin, block)
        x = queries[at, :].astype(jnp.float32)
        scores = dot_t(qc[at, :], kbd[...])
        weights = []
        for head in range(heads):
            s = scores[:, head * count : (head + 1) * count]
            top = jnp.max(s, axis=-1, keepdims=True)
            weights.append(weigh(s, top, scales[head : head + 1, :1]))
        low = dot(jnp.concatenate(weights[: heads // 2], axis=1), vbd[:middle, :])
        high = dot(jnp.concatenate(weights[heads // 2 :], axis=1), vbd[middle:, :])
        x1 = x + dot(normed(low, high), wo)
        x1_ref[at, :] = x1
        hn1 = rms_round(x1)
        hn_ref[at, :] = hn1
        key = dot(hn1, wk).astype(jnp.bfloat16)
        slot = lax.broadcasted_iota(jnp.int32, (block, width), 0) + begin
        if begin == 0:
            first = key[:1]
        kv_ref[at, :] = jnp.where(slot < counts[:1, :1], key, first)
        value = dot_t(wvt[...], hn1).astype(jnp.bfloat16)
        slot = lax.broadcasted_iota(jnp.int32, (width, block), 1) + begin
        value = jnp.where(slot < counts[:1, :1], value, jnp.bfloat16(DEAD_V))
        for part in range(0, block, width):
            place = begin + part
            size = min(block, width)
            target = pl.ds(rows + place // width * width, width)
            lanes = pl.ds(place % width, size)
            kv_ref[target, lanes] = value[:, part : part + size]


def transposed_values(kv, vt, heads):
    rows, width = vt.shape[1], kv.shape[1]
    hsize, part = width // heads, vt.shape[0] // heads
    for begin in range(0, rows, width):
        lanes = pl.ds(begin, width)
        values = kv[rows + begin : rows + begin + width, :]
        live = values < jnp.bfloat16(DEAD_V)
        flags = jnp.where(live[: part - hsize], jnp.bfloat16(1), jnp.bfloat16(0))
        values = jnp.where(live, values, jnp.bfloat16(0))
        for head in range(heads):
            at = head * part
            vt[at : at + hsize, lanes] = values[head * hsize : (head + 1) * hsize]
            vt[at + hsize : at + part, lanes] = flags


def head_rows(width, heads, lanes):
    row = lax.broadcasted_iota(jnp.int32, (width, lanes), 0) // (width // heads)
    lane = lax.broadcasted_iota(jnp.int32, (width, lanes), 1)
    return jnp.where(row == lane, 1.0, 0.0).astype(jnp.bfloat16)


def key_sizes(keys, heads, lanes):
    wide = keys.astype(jnp.float32)
    norms = dot((wide * wide).astype(jnp.bfloat16), head_rows(keys.shape[1], heads, lanes))
    return jnp.max(norms, axis=0, keepdims=True)


def query_sizes(q, scales, heads):
    hsize = q.shape[0] // heads
    lane = lax.broadcasted_iota(jnp.int32, (1, scales.shape[1]), 1)
    sizes = jnp.zeros((1, scales.shape[1]), jnp.float32)
    for head in range(heads):
        part = q[head * hsize : (head + 1) * hsize].astype(jnp.float32)
        norm = jnp.max(jnp.sum(part * part, axis=0, keepdims=True), axis=1, keepdims=True)
        scale = scales[heads + head : heads + head + 1, :]
        sizes = jnp.where(lane == head, norm * scale * scale, sizes)
    return sizes


def half_attention(scales, qt, kv, vt, heads, s_held, p_held, sizes, live, blocks, own, use):
    rows, width = vt.shape[1], kv.shape[1]
    part = vt.shape[0] // heads
    depth = qt.shape[0] // heads
    per = heads * depth // width
    block = s_held.shape[2]
    steps = rows // STEP
    bound = jnp.max(sizes * key_sizes(kv[:rows, :], heads, sizes.shape[1]), axis=1, keepdims=True)
    choice = jnp.max(jnp.where(bound <= LIMIT * LIMIT, live, float(steps + 1)))

    def score(head, at, keys):
        lanes = head // per * depth
        q = qt[head * depth : (head + 1) * depth, at]
        return dot(kv[:keys, lanes : lanes + depth], q)

    def scale_of(head):
        return scales[heads + head : heads + head + 1, :1]

    def unshifted(keys, live_blocks):
        begins = range(0, live_blocks * block, block)
        units = [(head, pl.ds(begin, block)) for head in range(heads) for begin in begins]
        for step in range(len(units) + 1):
            if step < len(units):
                head, at = units[step]
                weights = jnp.exp(score(head, at, keys) * scale_of(head) - SHIFT)
                p_held[step % 2, :keys, :] = weights.astype(jnp.bfloat16)
            last = step - 1
            if 0 <= last:
                head, at = units[last]
                mine = vt[head * part : (head + 1) * part, :keys]
                top = jnp.broadcast_to(SHIFT / scale_of(head), (1, block))
                use(head, at, top, dot(mine, p_held[last % 2, :keys, :]))

    for step in range(1, steps + 1):
        for live_blocks in range(1, rows // block + 1):
            if own and not 0 < step * STEP - (live_blocks - 1) * block <= block:
                continue
            here = (choice == float(step)) & (blocks == live_blocks)
            pl.when(here)(functools.partial(unshifted, step * STEP, live_blocks))

    @pl.when(choice > float(steps))
    def shifted():
        begins = range(0, rows, block)
        units = [(head, pl.ds(begin, block)) for head in range(heads) for begin in begins]
        tops = {}
        for step in range(len(units) + 2):
            if step < len(units):
                s = score(*units[step], rows)
                s_held[step % 2] = s
                tops[step] = jnp.max(s, axis=0, keepdims=True)
            last = step - 1
            if 0 <= last < len(units):
                p_held[last % 2] = weigh(s_held[last % 2], tops[last], scale_of(units[last][0]))
            last = step - 2
            if 0 <= last:
                head, at = units[last]
                mine = vt[head * part : (head + 1) * part, :]
                use(head, at, tops[last], dot(mine, p_held[last % 2]))


def own_kernel(
    heads, counts, scales, hn, kv, wqt, qt, top_ref, sum_ref, size_ref, vt, s_held, p_held
):
    width = hn.shape[1]
    hsize = width // heads
    depth = qt.shape[0] // heads
    part = vt.shape[0] // heads
    q = dot_t(wqt[...], hn[...]).astype(jnp.bfloat16)
    sizes = query_sizes(q, scales, heads)
    size_ref[...] = jnp.broadcast_to(sizes, size_ref.shape)
    qt[...] = jnp.zeros_like(qt)
    for head in range(heads):
        begin = head * hsize
        at = head * depth + begin % depth
        qt[at : at + hsize, :] = q[begin : begin + hsize]
    transposed_values(kv, vt, heads)

    def use(head, at, top, total):
        top_ref[head : head + 1, at] = top
        sum_ref[head * part : (head + 1) * part, at] = total

    block = s_held.shape[2]
    blocks = lax.div(counts[0] + block - 1, block)
    steps = lax.div(counts[0] + STEP - 1, STEP).astype(jnp.float32)
    half_attention(scales, qt, kv, vt, heads, s_held, p_held, sizes, steps, blocks, True, use)


def rest_kernel(
    heads,
    counts,
    scales,
    x1_ref,
    kv,
    qt,
    top_ref,
    sum_ref,
    size_ref,
    wo,
    up,
    down,
    w1,
    w2,
    w3,
    features,
    boxes,
    vt,
    s_held,
    p_held,
    ctx,
    out,
    upper,
    wo_held,
    up_held,
    down_held,
    w1_held,
    w2_held,
    w3_held,
    sems,
):
    rows, width = x1_ref.shape
    hsize = width // heads
    part = vt.shape[0] // heads
    held = (wo_held, up_held, down_held, w1_held, w2_held, w3_held)
    pairs = zip((wo, up, down, w1, w2, w3), held)
    copies = [pltpu.make_async_copy(a, b, sems.at[i]) for i, (a, b) in enumerate(pairs)]
    for copy in copies:
        copy.start()
    transposed_values(kv, vt, heads)

    def use(head, at, top, total):
        scale = scales[heads + head : heads + head + 1, :1]
        first = top_ref[head : head + 1, at]
        most = jnp.maximum(first, top)
        total = total * jnp.exp((top - most) * scale)
        total += sum_ref[head * part : (head + 1) * part, at] * jnp.exp((first - most) * scale)
        mixed = total[:hsize] / total[hsize : hsize + 1]
        ctx[head * hsize : (head + 1) * hsize, at] = mixed.astype(jnp.bfloat16)

    block = upper.shape[1]
    count = counts[0]
    blocks = lax.div(count + block - 1, block)
    steps = jnp.ones((1, 1), jnp.float32)
    for token in range(STEP, rows, STEP):
        row = rows + token // width * width
        mark = kv[row : row + 1, token % width : token % width + 1].astype(jnp.float32)
        steps += jnp.where(mark < DEAD_V, 1.0, 0.0)
    half_attention(
        scales, qt, kv, vt, heads, s_held, p_held, size_ref[:1, :], steps, blocks, False, use
    )
    for copy in copies:
        copy.wait()
    starts = list(range(0, rows, block))
    ff = up_held.shape[1]
    chunk = ff // 4
    x2, x3 = {}, {}

    def leave(i):
        at = pl.ds(starts[i], block)
        return pltpu.make_async_copy(out.at[at, :], features.at[at, :], sems.at[len(copies) + i])

    def project(i):
        at = pl.ds(starts[i], block)
        mixed = lax.dot_general(
            ctx[:, at], wo_held[...], (((0,), (0,)), ((), ())), preferred_element_type=jnp.float32
        )
        x2[i] = x1_ref[at, :] + mixed

    def widen(i):
        hn2 = rms_round(x2[i])
        for begin in range(0, ff, chunk):
            cut = pl.ds(begin, chunk)
            upper[i % 2, :, cut] = jnp.maximum(dot(hn2, up_held[:, cut]), 0.0).astype(jnp.bfloat16)

    def narrow(i):
        at = pl.ds(starts[i], block)
        x3[i] = x2[i] + dot(upper[i % 2], down_held[...])
        slot = lax.broadcasted_iota(jnp.int32, (block, width), 0) + starts[i]
        out[at, :] = jnp.where(slot < count, x3[i], 0.0)
        leave(i).start()

    def box(i):
        b1 = jnp.maximum(dot(rms_round(x3[i]), w1_held[...]), 0.0).astype(jnp.bfloat16)
        b2 = jnp.maximum(dot(b1, w2_held[...]), 0.0).astype(jnp.bfloat16)
        raw = dot_t(w3_held[...], b2)
        slot = lax.broadcasted_iota(jnp.int32, raw.shape, 1) + starts[i]
        boxes[:, pl.ds(starts[i], block)] = jnp.where(
            slot < count, 1.0 / (1.0 + jnp.exp(-raw)), 0.0
        )

    def finish(live):
        for i in range(live, len(starts)):
            at = pl.ds(starts[i], block)
            out[at, :] = jnp.zeros((block, width), jnp.float32)
            boxes[:, at] = jnp.zeros((boxes.shape[0], block), jnp.float32)
            leave(i).start()
        for step in range(live + 3):
            for stage, work in enumerate((project, widen, narrow, box)):
                if 0 <= step - stage < live:
                    work(step - stage)

    for live in range(1, len(starts) + 1):
        pl.when(blocks == live)(functools.partial(finish, live))
    for i in range(len(starts)):
        leave(i).wait()


def in_hbm(x):
    return pltpu.with_memory_space_constraint(x, pltpu.HBM)


def swap(x, axis):
    size = lax.axis_size(axis)
    return lax.ppermute(x, axis, [(i, i ^ 1) for i in range(size)])


def local(
    queries,
    counts,
    memory,
    mem_mask,
    cross_wq,
    cross_wkv,
    cross_wo,
    self_wqkv,
    self_wo,
    ffn_up,
    ffn_down,
    box_w1,
    box_w2,
    box_w3,
    cross_temp,
    self_temp,
):
    rows, width = queries.shape
    heads = cross_temp.shape[0]
    tile = memory.shape[0]
    params = pltpu.CompilerParams(vmem_limit_bytes=32 * 2**20)
    marked = pl.pallas_call(
        mark_kernel,
        out_shape=pltpu.VMEM((lax.axis_size("row"), tile, width), memory.dtype),
        in_specs=[HBM, HBM],
        out_specs=VMEM,
        scratch_shapes=[
            pltpu.VMEM(memory.shape, memory.dtype),
            pltpu.SMEM(mem_mask.shape, mem_mask.dtype),
            pltpu.SemaphoreType.DMA((2,)),
        ],
        name="mark",
    )(in_hbm(memory), in_hbm(mem_mask))
    gathered = lax.all_to_all(marked, "row", 0, 0, tiled=True)
    pieces = [gathered.reshape(-1, width)]
    tokens = pltpu.VMEM((rows, width), jnp.bfloat16)
    packed_width = cross_wkv.shape[1] + cross_wo.shape[1] + self_wqkv.shape[1]
    sources = (queries, cross_wq, cross_temp, self_temp, cross_wkv, cross_wo, self_wqkv)
    x, qc, scales, live, packed, wvt, wqt = pl.pallas_call(
        load_kernel,
        out_shape=[
            tokens,
            tokens,
            pltpu.VMEM((2 * heads, 128), jnp.float32),
            pltpu.VMEM((8, 128), jnp.int32),
            pltpu.VMEM((width, packed_width), jnp.bfloat16),
            pltpu.VMEM((width, width), jnp.bfloat16),
            pltpu.VMEM((width, width), jnp.bfloat16),
        ],
        in_specs=[SMEM] + [HBM] * len(sources),
        out_specs=[VMEM] * 7,
        scratch_shapes=[
            pltpu.VMEM(cross_wq.shape, cross_wq.dtype),
            pltpu.SMEM(cross_temp.shape, cross_temp.dtype),
            pltpu.SMEM(self_temp.shape, self_temp.dtype),
            pltpu.SemaphoreType.DMA((len(sources),)),
        ],
        compiler_params=params,
        cost_estimate=pl.CostEstimate(
            flops=2 * rows * width * width, bytes_accessed=4 * 2**20, transcendentals=0
        ),
        name="load",
    )(counts, *map(in_hbm, sources))
    count = sum(piece.shape[0] for piece in pieces)
    block = min(rows, 256 if count <= 128 else 128)
    kv_shape = pltpu.VMEM((2 * rows, width), jnp.bfloat16)
    x1, hn, kv = pl.pallas_call(
        functools.partial(cross_kernel, len(pieces), block, tile, heads),
        out_shape=(pltpu.VMEM((rows, width), jnp.float32), tokens, kv_shape),
        in_specs=[VMEM] * (6 + len(pieces)),
        out_specs=(VMEM, VMEM, VMEM),
        scratch_shapes=[
            pltpu.VMEM((heads * count, width), jnp.bfloat16),
            pltpu.VMEM((heads * count, width), jnp.bfloat16),
        ],
        compiler_params=params,
        name="cross",
    )(scales, live, x, qc, *pieces, packed, wvt)
    other = swap(kv, "col")
    part = width // heads + 16
    depth = min(128, width)
    block = min(256, rows)
    held = [
        pltpu.VMEM((heads * part, rows), jnp.bfloat16),
        pltpu.VMEM((2, rows, block), jnp.float32),
        pltpu.VMEM((2, rows, block), jnp.bfloat16),
    ]
    qt, tops, sums, sizes = pl.pallas_call(
        functools.partial(own_kernel, heads),
        out_shape=(
            pltpu.VMEM((heads * depth, rows), jnp.bfloat16),
            pltpu.VMEM((heads, rows), jnp.float32),
            pltpu.VMEM((heads * part, rows), jnp.float32),
            pltpu.VMEM((8, 128), jnp.float32),
        ),
        in_specs=[SMEM] + [VMEM] * 4,
        out_specs=(VMEM, VMEM, VMEM, VMEM),
        scratch_shapes=held,
        compiler_params=params,
        cost_estimate=pl.CostEstimate(
            flops=8 * heads * rows * rows * width, bytes_accessed=2**20, transcendentals=0
        ),
        name="own",
    )(counts, scales, hn, kv, wqt)
    late = (self_wo, ffn_up, ffn_down, box_w1, box_w2, jnp.transpose(box_w3))
    return pl.pallas_call(
        functools.partial(rest_kernel, heads),
        out_shape=(
            jax.ShapeDtypeStruct((rows, width), jnp.float32),
            jax.ShapeDtypeStruct((box_w3.shape[1], rows), jnp.float32),
        ),
        in_specs=[SMEM] + [VMEM] * 7 + [HBM] * len(late),
        out_specs=(HBM, VMEM),
        scratch_shapes=held
        + [
            pltpu.VMEM((width, rows), jnp.bfloat16),
            pltpu.VMEM((rows, width), jnp.float32),
            pltpu.VMEM((2, block, ffn_up.shape[1]), jnp.bfloat16),
        ]
        + [pltpu.VMEM(w.shape, w.dtype) for w in late]
        + [pltpu.SemaphoreType.DMA((len(late) + rows // block,))],
        compiler_params=params,
        name="rest",
    )(counts, scales, x1, other, qt, tops, sums, sizes, *map(in_hbm, late))


def solution(mesh):
    return jax.shard_map(
        local,
        mesh=mesh,
        in_specs=(
            P(("parts", "row", "col"), None),
            P(("parts", "row", "col")),
            P(("parts", "row", "col"), None),
            P(("parts", "row", "col")),
            P(),
            P(),
            P(),
            P(),
            P(),
            P(),
            P(),
            P(),
            P(),
            P(),
            P(),
            P(),
        ),
        out_specs=(P(("parts", "row", "col"), None), P(None, ("parts", "row", "col"))),
        check_vma=False,
    )
```
